32 devices in a mesh: wide: 16 (over z, y, x), narrow: 2 (over core).
Axes of the slice: x: 2, y: 2, z: 4, core: 2. Of those that a mesh axis runs over, the one named last changes fastest.
Arguments:
- tokens: bfloat16 [32768, 1024], P(('wide', 'narrow')), may hold values from -6 to 6
- class_table: bfloat16 [1024, 1024], P(('wide', 'narrow')), may hold values from -6 to 6
- ada_weight: bfloat16 [1024, 6144], P(('wide', 'narrow')), may hold values from -0.1875 to 0.1875
- qkv_weight: bfloat16 [1024, 3072], P(('wide', 'narrow')), may hold values from -0.1875 to 0.1875
- proj_weight: bfloat16 [1024, 1024], P(('wide', 'narrow')), may hold values from -1 to 1
- head_scale: float32 [16], replicated, may hold values from 8 to 24
- fc1_weight: bfloat16 [1024, 4096], P(('wide', 'narrow')), may hold values from -0.1875 to 0.1875
- fc2_weight: bfloat16 [4096, 1024], P(('wide', 'narrow')), may hold values from -0.125 to 0.125
- levels: int32 [32, 6], P(('wide', 'narrow')), may hold values from 0 to 10, as said below
- labels: int32 [32, 6], P(('wide', 'narrow')), may hold values from 0 to 1023, as said below
- cotangent: bfloat16 [32768, 1024], P(('wide', 'narrow')), may hold values from -6 to 6
Outputs:
- output: bfloat16 [32768, 1024], P(('wide', 'narrow'))
- tokens_grad: bfloat16 [32768, 1024], P(('wide', 'narrow'))
- table_grad: float32 [1024, 1024], P(('wide', 'narrow'))
- ada_grad: float32 [1024, 6144], P(('wide', 'narrow'))
- qkv_grad: float32 [1024, 3072], P(('wide', 'narrow'))
- proj_grad: float32 [1024, 1024], P(('wide', 'narrow'))
- scale_grad: float32 [16], replicated
- fc1_grad: float32 [1024, 4096], P(('wide', 'narrow'))
- fc2_grad: float32 [4096, 1024], P(('wide', 'narrow'))
The draws below stay inside these ranges and needn't reach their ends.
Inputs may be any that keep to these rules, and one draw needn't show every extreme that they name: In each row the nonzero levels come first and lie in 7 to 10; their items' tokens fit in 1024; a 0 marks an empty slot. Slot 0 of the 32 rows names a class of every aligned block of 32 classes exactly once; labels of empty slots are unused.
All inputs are finite; a program needn't handle non-finite values.
Results may differ from the reference program's by a relative error of at most 0.018.
Values may be sent and summed in bfloat16 or wider, within the bound.
No kernel may reach another device: no remote copies, remote signals or barrier semaphores. Data moves between devices by JAX's collectives and lax.ppermute only.
A program may use at most 448 MiB of HBM per device.

```python
import math
import jax
import jax.numpy as jnp
import numpy as np
from jax import lax

D = 1024
HEADS = 16
HEAD = 64
FF = 4096
CLASSES = 1024
ROW = 1024
ITEMS = 6
LEVEL_LO = 7
LEVEL_HI = 10
ROWS = 32
TOKENS = 32768


LENGTH_TABLE = np.array([0, 1, 5, 14, 30, 55, 91, 155, 255, 424, 680], np.int32)


def draw_levels(key, part):
    key = jax.random.fold_in(key, 11)
    drawn = jax.random.randint(key, (ROWS, ITEMS), LEVEL_LO, LEVEL_HI + 1).astype(jnp.int32)
    drawn = drawn.at[0, 0].set(LEVEL_HI)
    lengths = jnp.asarray(LENGTH_TABLE)[drawn]
    running = jnp.cumsum(lengths, axis=1)
    return jnp.where(running <= ROW, drawn, 0).astype(jnp.int32)


def draw_labels(key, part):
    key = jax.random.fold_in(key, 23)
    first_key, order_key, offset_key = jax.random.split(key, 3)
    drawn = jax.random.randint(first_key, (ROWS, ITEMS), 0, CLASSES).astype(jnp.int32)
    block_size = CLASSES // ROWS
    order = jax.random.permutation(order_key, ROWS).astype(jnp.int32)
    offset = jax.random.randint(offset_key, (ROWS,), 0, block_size).astype(jnp.int32)
    offset = jnp.where(order == 0, 0, jnp.where(order == ROWS - 1, block_size - 1, offset))
    return drawn.at[:, 0].set(order * block_size + offset).astype(jnp.int32)


def level_of(stream_key, dims, cuts, least, high):
    factor_of, own = 1.0, jax.random.fold_in(stream_key, 6)
    for axis_at, parts in cuts:
        heights = jnp.exp(jax.random.uniform(jax.random.fold_in(own, axis_at), (parts,), jnp.float32, least / len(cuts), high / len(cuts)))
        factor_of = factor_of * jnp.repeat(heights, dims[axis_at] // parts).reshape([-1 if axis == axis_at else 1 for axis in range(len(dims))])
    return factor_of


def noise(stream_key, dims, scale, bound, cuts=(), kind=jnp.bfloat16):
    loudness = level_of(stream_key, dims, cuts, -0.22, 0.18) if cuts else 1.0
    entries = jax.random.normal(stream_key, dims, jnp.float32) * scale * loudness
    return jnp.minimum(jnp.maximum(entries, -bound), bound).astype(kind)


def setup_inputs(seed: int = 0) -> dict:
    key_list = jax.random.split(jax.random.key(seed), 12)
    return {
        "tokens": noise(key_list[0], (TOKENS, D), 1.0, 6.0, ((0, 32),)),
        "class_table": noise(key_list[1], (CLASSES, D), 1.0, 6.0, ((0, 32),)),
        "ada_weight": noise(key_list[2], (D, 6 * D), D ** -0.5, 0.1875, ((0, 32),)),
        "qkv_weight": noise(key_list[3], (D, 3 * D), D ** -0.5, 0.1875, ((0, 32),)),
        "proj_weight": noise(key_list[4], (D, D), (D // 32) ** -0.5, 1.0, ((0, 32),)),
        "head_scale": jnp.clip(jnp.exp(jax.random.uniform(key_list[5], (HEADS,), jnp.float32, math.log(8.0), math.log(24.0))), 8.0, 24.0),
        "fc1_weight": noise(key_list[6], (D, FF), D ** -0.5, 0.1875, ((0, 32),)),
        "fc2_weight": noise(key_list[7], (FF, D), (FF // 2) ** -0.5, 0.125, ((0, 32),)),
        "levels": draw_levels(jax.random.fold_in(key_list[11], 71), 0),
        "labels": draw_labels(jax.random.fold_in(key_list[11], 71), 0),
        "cotangent": noise(key_list[10], (TOKENS, D), 1.0, 6.0, ((0, 32),)),
    }


FULL_PRECISION = lax.Precision.HIGHEST
NORM_EPS = 1e-06
NEG_LARGE = -1e+30
LENGTH_TABLE = np.array([0, 1, 5, 14, 30, 55, 91, 155, 255, 424, 680], np.int32)
SCALE_BOUNDS = np.array([1, 5, 14, 30, 55, 91, 155, 255, 424], np.int32)

@jax.custom_vjp
def low(v):
    return lax.optimization_barrier(v.astype(jnp.bfloat16)).astype(jnp.float32)

@jax.custom_vjp
def low_back(v):
    return v

def low_keep(v):
    return (low(v), None)

def low_pass(kept, grad):
    return (grad,)

def back_keep(v):
    return (v, None)

def back_low(kept, grad):
    return (low(grad),)
low.defvjp(low_keep, low_pass)
low_back.defvjp(back_keep, back_low)

def layout(level_row, row_count):
    level_hits = level_row[:, None] == jnp.arange(11, dtype=jnp.int32)[None, :]
    lengths = lax.optimization_barrier(jnp.sum(jnp.where(level_hits, jnp.asarray(LENGTH_TABLE)[None, :], 0), axis=1)).astype(jnp.int32)
    starts = (jnp.cumsum(lengths).astype(jnp.int32) - lengths).astype(jnp.int32)
    position = jnp.arange(row_count, dtype=jnp.int32)[:, None]
    inside = (position >= starts[None, :]) & (position < (starts + lengths)[None, :])
    offset = position - starts[None, :]
    reached = lax.optimization_barrier(jnp.sum((offset[:, :, None] >= jnp.asarray(SCALE_BOUNDS)[None, None, :]).astype(jnp.int32), axis=2)).astype(jnp.int32)
    inside_int = inside.astype(jnp.int32)
    slots = jnp.arange(level_row.shape[0], dtype=jnp.int32)[None, :]
    covered = lax.optimization_barrier(jnp.sum(inside_int, axis=1)).astype(jnp.int32)
    item_of = jnp.where(covered > 0, lax.optimization_barrier(jnp.sum(inside_int * slots, axis=1)).astype(jnp.int32), -1).astype(jnp.int32)
    scale_of = lax.optimization_barrier(jnp.sum(inside_int * reached, axis=1)).astype(jnp.int32)
    return (inside.astype(jnp.float32), item_of, scale_of)

def block_mask(item_of, scale_of, first_row, count):
    query_item = lax.dynamic_slice_in_dim(item_of, first_row, count)
    query_scale = lax.dynamic_slice_in_dim(scale_of, first_row, count)
    query_pos = first_row + jnp.arange(count, dtype=jnp.int32)
    key_pos = jnp.arange(item_of.shape[0], dtype=jnp.int32)
    same_item = (query_item[:, None] == item_of[None, :]) & (query_item[:, None] >= 0)
    earlier = scale_of[None, :] <= query_scale[:, None]
    return same_item & earlier | (query_pos[:, None] == key_pos[None, :])

def normalize(values):
    centered = values - lax.optimization_barrier(jnp.mean(values, axis=-1, keepdims=True))
    return centered * lax.rsqrt(lax.optimization_barrier(jnp.mean(centered * centered, axis=-1, keepdims=True)) + NORM_EPS)

def modulate(base, scale_part, shift_part):
    return normalize(base) * (1.0 + scale_part) + shift_part

def unit_rows(values):
    return values * lax.rsqrt(lax.optimization_barrier(jnp.sum(values * values, axis=-1, keepdims=True)) + NORM_EPS)

def row_forward(row_tokens, row_mod, level_row, qkv_weight, proj_weight, head_scale, fc1_weight, fc2_weight):
    member, item_of, scale_of = layout(level_row, ROW)
    per_token = jnp.dot(member, row_mod, precision=FULL_PRECISION)
    gamma1, gamma2, scale1, scale2, shift1, shift2 = jnp.split(per_token, 6, axis=1)
    hidden_one = low(modulate(row_tokens, scale1, shift1))
    projected = low_back(jnp.dot(hidden_one, qkv_weight, precision=FULL_PRECISION)).reshape(ROW, 3, HEADS, HEAD)
    queries = low(unit_rows(projected[:, 0]) * head_scale[None, :, None])
    keys_unit = low(unit_rows(projected[:, 1]))
    values_low = low(projected[:, 2])
    scores = low_back(jnp.einsum('qhd,khd->hqk', queries, keys_unit, precision=FULL_PRECISION))
    allowed = block_mask(item_of, scale_of, 0, ROW)
    attn_prob = jax.nn.softmax(jnp.where(allowed[None], scores, NEG_LARGE), axis=-1)
    mixed = jnp.einsum('hqk,khd->qhd', low(attn_prob), values_low, precision=FULL_PRECISION).reshape(ROW, D)
    mixed = low_back(low(mixed))
    branch = low_back(jnp.dot(mixed, proj_weight, precision=FULL_PRECISION))
    after_attn = row_tokens + gamma1 * branch
    hidden_two = low(modulate(after_attn, scale2, shift2))
    expanded = low_back(jnp.dot(hidden_two, fc1_weight, precision=FULL_PRECISION))
    activated = low(jax.nn.gelu(expanded, approximate=True))
    mlp_out = low_back(jnp.dot(activated, fc2_weight, precision=FULL_PRECISION))
    return after_attn + gamma2 * mlp_out

def forward(tokens, class_table, ada_weight, qkv_weight, proj_weight, head_scale, fc1_weight, fc2_weight, levels, labels):
    class_vec = class_table[labels]
    lifted = low(jax.nn.silu(class_vec))
    modulation = low_back(jnp.einsum('rid,dc->ric', lifted, ada_weight, precision=FULL_PRECISION))

    def one_row(packed):
        row_tokens, row_mod, level_row = packed
        return row_forward(row_tokens, row_mod, level_row, qkv_weight, proj_weight, head_scale, fc1_weight, fc2_weight)
    outputs = lax.map(jax.checkpoint(one_row), (tokens.reshape(ROWS, ROW, D), modulation, levels))
    return outputs.reshape(ROWS * ROW, D)

def reference(tokens, class_table, ada_weight, qkv_weight, proj_weight, head_scale, fc1_weight, fc2_weight, levels, labels, cotangent):
    floats = (tokens.astype(jnp.float32), class_table.astype(jnp.float32), ada_weight.astype(jnp.float32), qkv_weight.astype(jnp.float32), proj_weight.astype(jnp.float32), head_scale.astype(jnp.float32), fc1_weight.astype(jnp.float32), fc2_weight.astype(jnp.float32))

    def run(tok_in, table_in, ada_in, qkv_in, proj_in, scale_in, up_in, down_in):
        return forward(tok_in, table_in, ada_in, qkv_in, proj_in, scale_in, up_in, down_in, levels, labels)
    result, pullback = jax.vjp(run, *floats)
    grads = pullback(cotangent.astype(jnp.float32))
    return (result.astype(jnp.bfloat16), grads[0].astype(jnp.bfloat16), grads[1], grads[2], grads[3], grads[4], grads[5], grads[6], grads[7])
```

```python
import jax
import jax.numpy as jnp
import numpy as np
from jax import lax
from jax.sharding import PartitionSpec as P

FULL_PRECISION = lax.Precision.HIGHEST
NORM_EPS = 1e-06
NEG_LARGE = -1e30
LENGTH_TABLE = np.array([0, 1, 5, 14, 30, 55, 91, 155, 255, 424, 680], np.int32)
SCALE_BOUNDS = np.array([1, 5, 14, 30, 55, 91, 155, 255, 424], np.int32)


BOTH = ("wide", "narrow")


def bit_count(size):
    return size.bit_length() - 1


def flip(values, axis, size, bit):
    return lax.ppermute(values, axis, [(i, i ^ (1 << bit)) for i in range(size)])


def halving_order(wide, narrow, turn):
    inner = list(range(bit_count(narrow)))
    outer = list(range(bit_count(wide)))
    turning, last = outer[:-1], outer[-1:]
    turn = turn % max(1, len(turning))
    return [("narrow", b) for b in inner] + [
        ("wide", b) for b in turning[turn:] + turning[:turn] + last
    ]


def scatter_sum(partial, wide, narrow, turn):
    sizes = {"wide": wide, "narrow": narrow}
    dims = [("wide", b) for b in reversed(range(bit_count(wide)))] + [
        ("narrow", b) for b in reversed(range(bit_count(narrow)))
    ]
    rows, columns = partial.shape
    block = partial.reshape((2,) * len(dims) + (rows // (wide * narrow), columns))
    order = halving_order(wide, narrow, turn)
    for step, (axis, bit) in enumerate(order):
        at = dims.index((axis, bit))
        dims.pop(at)
        mine = (lax.axis_index(axis) >> bit) & 1
        sent = lax.dynamic_index_in_dim(block, 1 - mine, at, keepdims=False)
        kept = lax.dynamic_index_in_dim(block, mine, at, keepdims=False)
        got = flip(sent, axis, sizes[axis], bit)
        block = kept.astype(jnp.float32) + got.astype(jnp.float32)
        if step < len(order) - 1:
            block = block.astype(jnp.bfloat16)
    return block


def layout(level_row, row_count):
    level_hits = level_row[:, None] == jnp.arange(11, dtype=jnp.int32)[None, :]
    lengths = jnp.sum(jnp.where(level_hits, jnp.asarray(LENGTH_TABLE)[None, :], 0), axis=1).astype(
        jnp.int32
    )
    starts = jnp.cumsum(lengths) - lengths
    position = jnp.arange(row_count, dtype=jnp.int32)[:, None]
    inside = (position >= starts[None, :]) & (position < (starts + lengths)[None, :])
    offset = position - starts[None, :]
    reached = jnp.sum(
        (offset[:, :, None] >= jnp.asarray(SCALE_BOUNDS)[None, None, :]).astype(jnp.int32), axis=2
    )
    inside_int = inside.astype(jnp.int32)
    slots = jnp.arange(level_row.shape[0], dtype=jnp.int32)[None, :]
    covered = jnp.sum(inside_int, axis=1)
    item_of = jnp.where(covered > 0, jnp.sum(inside_int * slots, axis=1), -1)
    scale_of = jnp.sum(inside_int * reached, axis=1)
    return (inside.astype(jnp.float32), item_of, scale_of)


def block_mask(item_of, scale_of, first_row, count):
    query_item = lax.dynamic_slice_in_dim(item_of, first_row, count)
    query_scale = lax.dynamic_slice_in_dim(scale_of, first_row, count)
    query_pos = first_row + jnp.arange(count, dtype=jnp.int32)
    key_pos = jnp.arange(item_of.shape[0], dtype=jnp.int32)
    same_item = (query_item[:, None] == item_of[None, :]) & (query_item[:, None] >= 0)
    earlier = scale_of[None, :] <= query_scale[:, None]
    return same_item & earlier | (query_pos[:, None] == key_pos[None, :])


def normalize(values):
    centered = values - jnp.mean(values, axis=-1, keepdims=True)
    return centered * lax.rsqrt(jnp.mean(centered * centered, axis=-1, keepdims=True) + NORM_EPS)


def modulate(base, scale_part, shift_part):
    return normalize(base) * (1.0 + scale_part) + shift_part


def unit_rows(values):
    return values * lax.rsqrt(jnp.sum(values * values, axis=-1, keepdims=True) + NORM_EPS)


def scale_query(values, head_scale):
    return unit_rows(values) * head_scale[None, :, None]


def gelu_tanh(values):
    return jax.nn.gelu(values, approximate=True)


def per_device(
    tokens,
    class_table,
    ada_weight,
    qkv_weight,
    proj_weight,
    head_scale,
    fc1_weight,
    fc2_weight,
    levels,
    labels,
    cotangent,
):
    row_count, model_width = tokens.shape
    head_count = head_scale.shape[0]
    head_size = model_width // head_count
    wide, narrow = lax.axis_size("wide"), lax.axis_size("narrow")
    devices = wide * narrow
    me = lax.axis_index("wide") * narrow + lax.axis_index("narrow")
    slots = labels.shape[1]
    own_classes = class_table.shape[0]
    label_rows = jnp.zeros((16, model_width), jnp.bfloat16)
    label_rows = label_rows.at[0, :slots].set((labels[0] // 256).astype(jnp.bfloat16))
    label_rows = label_rows.at[1, :slots].set((labels[0] % 256).astype(jnp.bfloat16))
    packed = lax.all_gather(
        jnp.concatenate([class_table, label_rows], axis=0), BOTH, axis=0, tiled=False
    )
    table_full = packed[:, :own_classes].reshape(-1, model_width)
    qkv_full, proj_full = (
        lax.all_gather(qkv_weight, BOTH, axis=0, tiled=True),
        lax.all_gather(proj_weight, BOTH, axis=0, tiled=True),
    )
    label_parts = packed[:, own_classes : own_classes + 2, :slots].astype(jnp.int32)
    labels_all = (label_parts[:, 0] * 256 + label_parts[:, 1]).reshape(-1)
    label_pick = (
        labels_all[:, None] == jnp.arange(table_full.shape[0], dtype=jnp.int32)[None, :]
    ).astype(jnp.bfloat16)
    class_vec = jnp.dot(label_pick, table_full, preferred_element_type=jnp.float32)
    lifted = jax.nn.silu(class_vec).astype(jnp.bfloat16)
    ada_columns = lax.all_to_all(ada_weight, BOTH, 1, 0, tiled=True)
    modulation_columns = jnp.dot(lifted, ada_columns, preferred_element_type=jnp.float32)
    modulation = lax.all_to_all(modulation_columns, BOTH, 0, 1, tiled=True)
    member, item_of, scale_of = layout(levels[0], row_count)
    per_token = jnp.dot(member, modulation, precision=FULL_PRECISION)
    gamma1, gamma2, scale1, scale2, shift1, shift2 = jnp.split(per_token, 6, axis=1)
    inputs_full = tokens.astype(jnp.float32)
    hidden_one = modulate(inputs_full, scale1, shift1).astype(jnp.bfloat16)
    projected = jnp.dot(hidden_one, qkv_full, preferred_element_type=jnp.float32).reshape(
        row_count, 3, head_count, head_size
    )
    raw_query = projected[:, 0]
    raw_key = projected[:, 1]
    queries = scale_query(raw_query, head_scale).astype(jnp.bfloat16)
    keys_unit = unit_rows(raw_key).astype(jnp.bfloat16)
    values_low = projected[:, 2].astype(jnp.bfloat16)
    block_rows = min(512, row_count)
    block_count = row_count // block_rows

    def attend(block_index):
        first_row = block_index * block_rows
        query_block = lax.dynamic_slice_in_dim(queries, first_row, block_rows, 0)
        allowed = block_mask(item_of, scale_of, first_row, block_rows)
        scores = jnp.einsum(
            "qhd,khd->hqk", query_block, keys_unit, preferred_element_type=jnp.float32
        )
        scores = jnp.where(allowed[None], scores, NEG_LARGE)
        row_max = jnp.max(scores, axis=-1, keepdims=True)
        expo = jnp.exp(scores - row_max)
        row_total = jnp.sum(expo, axis=-1, keepdims=True)
        prob_low = (expo / row_total).astype(jnp.bfloat16)
        mixed_block = jnp.einsum(
            "hqk,khd->qhd", prob_low, values_low, preferred_element_type=jnp.float32
        )
        return (mixed_block, (row_max + jnp.log(row_total))[..., 0])

    mixed_blocks, log_total = lax.map(attend, jnp.arange(block_count, dtype=jnp.int32))
    mixed = mixed_blocks.reshape(row_count, model_width).astype(jnp.bfloat16)
    branch = jnp.dot(mixed, proj_full, preferred_element_type=jnp.float32)
    after_attn = inputs_full + gamma1 * branch
    hidden_two = modulate(after_attn, scale2, shift2).astype(jnp.bfloat16)
    fc1_full, fc2_full = (
        lax.all_gather(fc1_weight, ("wide", "narrow"), axis=0, tiled=True),
        lax.all_gather(fc2_weight, ("wide", "narrow"), axis=0, tiled=True),
    )
    expanded = jnp.dot(hidden_two, fc1_full, preferred_element_type=jnp.float32)
    activated = gelu_tanh(expanded).astype(jnp.bfloat16)
    mlp_out = jnp.dot(activated, fc2_full, preferred_element_type=jnp.float32)
    output = (after_attn + gamma2 * mlp_out).astype(jnp.bfloat16)
    grad_out = cotangent.astype(jnp.float32)
    fc1_back, fc2_back, qkv_back, proj_back = fc1_full, fc2_full, qkv_full, proj_full
    mlp_down = (grad_out * gamma2).astype(jnp.bfloat16)
    d_gamma2 = grad_out * mlp_out
    fc2_sum = jnp.einsum("tf,td->fd", activated, mlp_down, preferred_element_type=jnp.float32)
    fc2_grad = scatter_sum(fc2_sum.astype(jnp.bfloat16), wide, narrow, 0)
    activated_grad = jnp.einsum("td,fd->tf", mlp_down, fc2_back, preferred_element_type=jnp.float32)
    _, gelu_pull = jax.vjp(gelu_tanh, expanded)
    expanded_grad = gelu_pull(activated_grad)[0].astype(jnp.bfloat16)
    fc1_sum = jnp.einsum("td,tf->df", hidden_two, expanded_grad, preferred_element_type=jnp.float32)
    hidden_two_grad = jnp.einsum(
        "tf,df->td", expanded_grad, fc1_back, preferred_element_type=jnp.float32
    )
    fc1_grad = scatter_sum(fc1_sum.astype(jnp.bfloat16), wide, narrow, 1)
    _, second_pull = jax.vjp(modulate, after_attn, scale2, shift2)
    after_part, d_scale2, d_shift2 = second_pull(hidden_two_grad)
    attn_grad_in = grad_out + after_part
    branch_grad = (attn_grad_in * gamma1).astype(jnp.bfloat16)
    d_gamma1 = attn_grad_in * branch
    proj_sum = jnp.einsum("td,te->de", mixed, branch_grad, preferred_element_type=jnp.float32)
    proj_grad = scatter_sum(proj_sum.astype(jnp.bfloat16), wide, narrow, 2)
    mixed_grad = jnp.einsum("te,de->td", branch_grad, proj_back, preferred_element_type=jnp.float32)
    mixed_grad = mixed_grad.astype(jnp.bfloat16).reshape(row_count, head_count, head_size)

    def back_block(partials, packed):
        key_acc, value_acc = partials
        block_index, block_total = packed
        first_row = block_index * block_rows
        query_block = lax.dynamic_slice_in_dim(queries, first_row, block_rows, 0)
        grad_block = lax.dynamic_slice_in_dim(mixed_grad, first_row, block_rows, 0)
        allowed = block_mask(item_of, scale_of, first_row, block_rows)
        scores = jnp.einsum(
            "qhd,khd->hqk", query_block, keys_unit, preferred_element_type=jnp.float32
        )
        scores = jnp.where(allowed[None], scores, NEG_LARGE)
        attn_prob = jnp.exp(scores - block_total[..., None])
        prob_grad = jnp.einsum(
            "qhd,khd->hqk", grad_block, values_low, preferred_element_type=jnp.float32
        )
        inner = jnp.sum(attn_prob * prob_grad, axis=-1, keepdims=True)
        score_grad = (attn_prob * (prob_grad - inner)).astype(jnp.bfloat16)
        query_part = jnp.einsum(
            "hqk,khd->qhd", score_grad, keys_unit, preferred_element_type=jnp.float32
        )
        key_acc = key_acc + jnp.einsum(
            "hqk,qhd->khd", score_grad, query_block, preferred_element_type=jnp.float32
        )
        value_acc = value_acc + jnp.einsum(
            "hqk,qhd->khd",
            attn_prob.astype(jnp.bfloat16),
            grad_block,
            preferred_element_type=jnp.float32,
        )
        return ((key_acc, value_acc), query_part)

    zero_heads = jnp.zeros((row_count, head_count, head_size), jnp.float32)
    (key_grad, value_grad), query_parts = lax.scan(
        back_block, (zero_heads, zero_heads), (jnp.arange(block_count, dtype=jnp.int32), log_total)
    )
    query_grad = query_parts.reshape(row_count, head_count, head_size)
    _, query_pull = jax.vjp(scale_query, raw_query, head_scale)
    raw_query_grad, scale_part = query_pull(query_grad)
    _, key_pull = jax.vjp(unit_rows, raw_key)
    raw_key_grad = key_pull(key_grad)[0]
    projected_grad = (
        jnp.stack([raw_query_grad, raw_key_grad, value_grad], axis=1)
        .reshape(row_count, 3 * model_width)
        .astype(jnp.bfloat16)
    )
    qkv_sum = jnp.einsum(
        "td,tc->dc", hidden_one, projected_grad, preferred_element_type=jnp.float32
    )
    hidden_one_grad = jnp.einsum(
        "tc,dc->td", projected_grad, qkv_back, preferred_element_type=jnp.float32
    )
    _, first_pull = jax.vjp(modulate, inputs_full, scale1, shift1)
    input_part, d_scale1, d_shift1 = first_pull(hidden_one_grad)
    tokens_grad = (attn_grad_in + input_part).astype(jnp.bfloat16)
    token_mod_grad = jnp.concatenate(
        [d_gamma1, d_gamma2, d_scale1, d_scale2, d_shift1, d_shift2], axis=1
    )
    modulation_grad = jnp.einsum(
        "ti,tc->ic", member, token_mod_grad, precision=FULL_PRECISION
    ).astype(jnp.bfloat16)
    gathered = lax.all_gather(modulation_grad, BOTH, axis=0, tiled=True)
    own_width = model_width // devices
    own_lifted = lax.dynamic_slice_in_dim(lifted, me * own_width, own_width, 1)
    own_vec = lax.dynamic_slice_in_dim(class_vec, me * own_width, own_width, 1)
    ada_grad = jnp.einsum("id,ic->dc", own_lifted, gathered, preferred_element_type=jnp.float32)
    lifted_grad = jnp.einsum("ic,dc->id", gathered, ada_weight, preferred_element_type=jnp.float32)
    _, silu_pull = jax.vjp(jax.nn.silu, own_vec)
    class_grad = silu_pull(lifted_grad)[0]
    table_columns = jnp.einsum(
        "ic,id->cd", label_pick.astype(jnp.float32), class_grad, precision=FULL_PRECISION
    )
    head_rows = -(-head_count // own_width)
    head_rows += -head_rows % 8
    scale_rows = jnp.pad(scale_part, (0, head_rows * own_width - head_count)).reshape(
        1, head_rows, own_width
    )
    outgoing = jnp.concatenate(
        [
            table_columns.reshape(devices, own_classes, own_width),
            jnp.broadcast_to(scale_rows, (devices, head_rows, own_width)),
        ],
        axis=1,
    ).reshape(devices * (own_classes + head_rows), own_width)
    incoming = lax.all_to_all(outgoing, BOTH, 0, 1, tiled=True)
    table_grad = incoming[:own_classes]
    scale_grad = jnp.sum(
        incoming[own_classes:].reshape(head_rows, devices, own_width), axis=1
    ).reshape(-1)[:head_count]
    qkv_grad = scatter_sum(qkv_sum.astype(jnp.bfloat16), wide, narrow, 0)
    return (
        output,
        tokens_grad,
        table_grad,
        ada_grad,
        qkv_grad,
        proj_grad,
        scale_grad,
        fc1_grad,
        fc2_grad,
    )


def solution(mesh):
    in_specs = (
        P(("wide", "narrow"), None),
        P(("wide", "narrow"), None),
        P(("wide", "narrow"), None),
        P(("wide", "narrow"), None),
        P(("wide", "narrow"), None),
        P(),
        P(("wide", "narrow"), None),
        P(("wide", "narrow"), None),
        P(("wide", "narrow"), None),
        P(("wide", "narrow"), None),
        P(("wide", "narrow"), None),
    )
    out_specs = (
        P(("wide", "narrow"), None),
        P(("wide", "narrow"), None),
        P(("wide", "narrow"), None),
        P(("wide", "narrow"), None),
        P(("wide", "narrow"), None),
        P(("wide", "narrow"), None),
        P(),
        P(("wide", "narrow"), None),
        P(("wide", "narrow"), None),
    )
    return jax.shard_map(
        per_device, mesh=mesh, in_specs=in_specs, out_specs=out_specs, check_vma=False
    )
```

```python
import functools
import jax
import jax.numpy as jnp
import numpy as np
from jax import lax
from jax.experimental import pallas as pl
from jax.experimental.pallas import tpu as pltpu
from jax.sharding import PartitionSpec as P

NORM_EPS = 1e-06
BF, F32 = jnp.bfloat16, jnp.float32
VMEM_BYTES = 56 * 2**20
HEAD = 64
PAIR = 2 * HEAD
GROUP = 4
GELU_A, GELU_B = 0.7978845608028654, 0.044715


def nn(a, b):
    return lax.dot_general(a, b, (((1,), (0,)), ((), ())), preferred_element_type=F32)


def nt(a, b):
    return lax.dot_general(a, b, (((1,), (1,)), ((), ())), preferred_element_type=F32)


def tn(a, b):
    return lax.dot_general(a, b, (((0,), (0,)), ((), ())), preferred_element_type=F32)


def halves(x):
    high = x.astype(BF)
    return high, (x - high.astype(F32)).astype(BF)


def params(steps=1):
    return pltpu.CompilerParams(
        vmem_limit_bytes=VMEM_BYTES, dimension_semantics=("arbitrary",) * steps
    )


def cost(flops, size, exps=0):
    return pl.CostEstimate(flops=int(flops), bytes_accessed=int(size), transcendentals=int(exps))


def head_ones(dtype=BF):
    row = lax.broadcasted_iota(jnp.int32, (PAIR, PAIR), 0) // HEAD
    column = lax.broadcasted_iota(jnp.int32, (PAIR, PAIR), 1) // HEAD
    return (row == column).astype(F32).astype(dtype)


def head_sums(x):
    ones = head_ones()
    parts = []
    for at in range(0, x.shape[1], PAIR):
        high, low = halves(x[:, at : at + PAIR])
        parts.append(nn(high, ones) + nn(low, ones))
    return parts[0] if len(parts) == 1 else jnp.concatenate(parts, axis=1)


def centre(x):
    mean = jnp.mean(x, axis=-1, keepdims=True)
    centred = x - mean
    rstd = lax.rsqrt(jnp.mean(centred * centred, axis=-1, keepdims=True) + NORM_EPS)
    return centred * rstd, rstd


def qkv_kernel(places, tokens, member, modulation, *refs, pieces):
    weights, (scale, hidden, q, k, v, rq, rk, ordered) = refs[: 3 * pieces], refs[3 * pieces :]
    step = pl.program_id(0)
    width = tokens.shape[1]
    block = ordered.shape[1]
    per = width // block
    rows = 256

    @pl.when(step == 0)
    def _():
        for at in range(0, tokens.shape[0], rows):
            here = pl.ds(at, rows)
            unit, _ = centre(tokens[here, :].astype(F32))
            sc = nn(member[here, :], modulation[:, 2 * width : 3 * width])
            sh = nn(member[here, :], modulation[:, 4 * width : 5 * width])
            hidden[here, :] = (unit * (1.0 + sc) + sh).astype(BF)

    for which in range(3):

        @pl.when((step >= which * per) & (step < (which + 1) * per))
        def _():
            if pieces == 1:
                ordered[...] = weights[which][...]
            else:
                own, other = weights[2 * which : 2 * which + 2]
                owners = places.shape[1]
                size = width // owners
                for owner in range(owners):
                    place = places[which, owner]
                    at = pl.multiple_of((place // 2) * size, size)
                    put = slice(owner * size, (owner + 1) * size)

                    @pl.when(place % 2 == 0)
                    def _():
                        ordered[put, :] = own[pl.ds(at, size), :]

                    @pl.when(place % 2 == 1)
                    def _():
                        ordered[put, :] = other[pl.ds(at, size), :]

            for at in range(0, tokens.shape[0], rows):
                here = pl.ds(at, rows)
                out = nn(hidden[here, :], ordered[...])
                if which == 0:
                    r = lax.rsqrt(head_sums(out * out) + NORM_EPS)
                    rq[here, :] = r.astype(BF)
                    q[here, :] = (out * r * scale[0:1, :]).astype(BF)
                if which == 1:
                    r = lax.rsqrt(head_sums(out * out) + NORM_EPS)
                    rk[here, :] = r.astype(BF)
                    k[here, :] = (out * r).astype(BF)
                if which == 2:
                    v[here, :] = out.astype(BF)


def qkv_call(places, tokens, member, modulation, weights, scale_lanes, block=512):
    count, width = tokens.shape
    per = width // block
    pieces = len(weights[0])
    part = lambda rows, which: pl.BlockSpec(
        (rows, block), lambda s, p: (0, jnp.clip(s - which * per, 0, per - 1))
    )
    whole = lambda x: pl.BlockSpec(x.shape, lambda s, p: (0, 0))
    columns = [part(count, i) for i in range(3)]
    return pl.pallas_call(
        functools.partial(qkv_kernel, pieces=pieces),
        grid_spec=pltpu.PrefetchScalarGridSpec(
            num_scalar_prefetch=1,
            grid=(3 * per,),
            in_specs=[whole(tokens), whole(member), whole(modulation)]
            + [part(w.shape[0], i) for i in range(3) for w in weights[i]]
            + [part(8, 0)],
            out_specs=[pl.BlockSpec((count, width), lambda s, p: (0, 0))]
            + columns
            + columns[:2]
            + [pl.BlockSpec((width, block), lambda s, p: (0, s))],
        ),
        out_shape=[jax.ShapeDtypeStruct((count, width), BF)] * 6
        + [jax.ShapeDtypeStruct((width, 3 * width), BF)],
        compiler_params=params(),
        cost_estimate=cost(6 * count * width * width, 2 * (13 * count * width)),
        name="qkv_forward",
    )(places, tokens, member, modulation, *[w for ws in weights for w in ws], scale_lanes)


def lane_masked(x, which):
    lane = lax.broadcasted_iota(jnp.int32, x.shape, 1) // HEAD
    return jnp.where(lane == which, x, jnp.zeros_like(x))


def attn_fwd_kernel(span, q, k, v, start, end, mixed, rest, inverse, v_ext, qm, *, qb, kb):
    count = q.shape[0]
    pairs = q.shape[1] // PAIR
    for pair in range(pairs):
        lanes = slice(pair * PAIR, (pair + 1) * PAIR)
        for h in range(2):
            vv = v[:, lanes]
            lane = lax.broadcasted_iota(jnp.int32, vv.shape, 1) // HEAD
            v_ext[2 * pair + h] = jnp.where(lane == h, vv, jnp.ones_like(vv))
            qm[2 * pair + h] = lane_masked(q[:, lanes], h)

    def one_block(i, _):
        first = pl.multiple_of(i * qb, qb)
        here = pl.ds(first, qb)
        low, high = start[here, :], end[here, :]

        def step(j, totals):
            at = pl.multiple_of(j * kb, kb)
            there = pl.ds(at, kb)
            place = at + lax.broadcasted_iota(jnp.int32, (qb, kb), 1)
            seen = (place >= low) & (place < high)
            out = []
            for h in range(2 * pairs):
                pair = h // 2
                s = nt(qm[h, here, :], k[there, pair * PAIR : (pair + 1) * PAIR])
                p = jnp.where(seen, jnp.exp(s), 0.0).astype(BF)
                out.append(totals[h] + nn(p, v_ext[h, there, :]))
            return tuple(out)

        totals = lax.fori_loop(
            span[0, i], span[1, i], step, tuple(jnp.zeros((qb, PAIR), F32) for _ in range(2 * pairs))
        )
        for pair in range(pairs):
            t0, t1 = totals[2 * pair], totals[2 * pair + 1]
            lane = lax.broadcasted_iota(jnp.int32, t0.shape, 1) // HEAD
            top = jnp.where(lane == 0, t0, t1)
            sums = pltpu.roll(jnp.where(lane == 0, t1, t0), HEAD, 1)
            inv = 1.0 / sums
            high_part, low_part = halves(top * inv)
            mixed[here, pair * PAIR : (pair + 1) * PAIR] = high_part
            rest[here, pair * PAIR : (pair + 1) * PAIR] = low_part
            turned = jnp.transpose(inv)
            inverse[0, 2 * pair : 2 * pair + 1, here] = turned[0:1, :]
            inverse[0, 2 * pair + 1 : 2 * pair + 2, here] = turned[HEAD : HEAD + 1, :]
        return 0

    lax.fori_loop(0, count // qb, one_block, 0)


def attn_fwd_call(span, q, k, v, start, end, qb=256, kb=256):
    count, width = q.shape
    lanes = GROUP * HEAD
    column = pl.BlockSpec((count, lanes), lambda g, s: (0, g))
    edge = pl.BlockSpec((count, 1), lambda g, s: (0, 0))
    heads = width // HEAD
    return pl.pallas_call(
        functools.partial(attn_fwd_kernel, qb=qb, kb=kb),
        grid_spec=pltpu.PrefetchScalarGridSpec(
            num_scalar_prefetch=1,
            grid=(heads // GROUP,),
            in_specs=[column, column, column, edge, edge],
            out_specs=[column, column, pl.BlockSpec((1, 8, count), lambda g, s: (g, 0, 0))],
            scratch_shapes=[
                pltpu.VMEM((GROUP, count, PAIR), BF),
                pltpu.VMEM((GROUP, count, PAIR), BF),
            ],
        ),
        out_shape=[
            jax.ShapeDtypeStruct((count, width), BF),
            jax.ShapeDtypeStruct((count, width), BF),
            jax.ShapeDtypeStruct((heads // GROUP, 8, count), F32),
        ],
        compiler_params=params(),
        cost_estimate=cost(16 * count * count * heads * HEAD, 8 * count * width, heads * count * count),
        name="attention_forward",
    )(span, q, k, v, start, end)


def attn_bwd_kernel(
    span, q, k, v, do, start, end, inverse, delta, rq, rk, scale,
    dq, dk, dv, scale_grad, qm, km, dom, dq_acc, dk_acc, dv_acc, *, qb, kb,
):
    count = q.shape[0]
    pairs = q.shape[1] // PAIR
    for pair in range(pairs):
        lanes = slice(pair * PAIR, (pair + 1) * PAIR)
        for h in range(2):
            qm[2 * pair + h] = lane_masked(q[:, lanes], h)
            km[2 * pair + h] = lane_masked(k[:, lanes], h)
            dom[2 * pair + h] = lane_masked(do[:, lanes], h)
    dk_acc[...] = jnp.zeros_like(dk_acc)
    dv_acc[...] = jnp.zeros_like(dv_acc)

    def one_block(i, _):
        first = pl.multiple_of(i * qb, qb)
        here = pl.ds(first, qb)
        low, high = start[0:1, here], end[0:1, here]
        dq_acc[...] = jnp.zeros_like(dq_acc)

        def step(j, _):
            at = pl.multiple_of(j * kb, kb)
            there = pl.ds(at, kb)
            place = at + lax.broadcasted_iota(jnp.int32, (kb, qb), 0)
            seen = (place >= low) & (place < high)
            for pair in range(pairs):
                lanes = slice(pair * PAIR, (pair + 1) * PAIR)
                ps, dss = [], []
                for h in (2 * pair, 2 * pair + 1):
                    s = nt(k[there, lanes], qm[h, here, :])
                    p = jnp.where(seen, jnp.exp(s) * inverse[0, h : h + 1, here], 0.0)
                    dp = nt(v[there, lanes], dom[h, here, :])
                    ps.append(p.astype(BF))
                    dss.append((p * (dp - delta[0, h : h + 1, here])).astype(BF))
                dv_acc[there, lanes] += nn(ps[0], dom[2 * pair, here, :]) + nn(ps[1], dom[2 * pair + 1, here, :])
                dk_acc[there, lanes] += nn(dss[0], qm[2 * pair, here, :]) + nn(dss[1], qm[2 * pair + 1, here, :])
                dq_acc[:, lanes] += tn(dss[0], km[2 * pair, there, :]) + tn(dss[1], km[2 * pair + 1, there, :])
            return 0

        lax.fori_loop(span[0, i], span[1, i], step, 0)
        g = dq_acc[...]
        sc = scale[0:1, :]
        unit = q[here, :].astype(F32) / sc
        inner = head_sums(unit * g)
        dq[here, :] = (sc * rq[here, :].astype(F32) * (g - unit * inner)).astype(BF)
        return jnp.sum(inner, axis=0, keepdims=True)

    def looped(i, total):
        return total + one_block(i, 0)

    total = lax.fori_loop(0, count // qb, looped, jnp.zeros((1, q.shape[1]), F32))
    scale_grad[...] = jnp.broadcast_to(total, scale_grad.shape)
    for at in range(0, count, qb):
        here = pl.ds(at, qb)
        g = dk_acc[here, :]
        unit = k[here, :].astype(F32)
        dk[here, :] = (rk[here, :].astype(F32) * (g - unit * head_sums(unit * g))).astype(BF)
    dv[...] = dv_acc[...].astype(BF)


def attn_bwd_call(span, q, k, v, do, start, end, inverse, delta, rq, rk, scale_lanes, qb=256, kb=256):
    count, width = q.shape
    lanes = GROUP * HEAD
    column = pl.BlockSpec((count, lanes), lambda g, s: (0, g))
    edge = pl.BlockSpec((8, count), lambda g, s: (0, 0))
    row = pl.BlockSpec((1, 8, count), lambda g, s: (g, 0, 0))
    small = pl.BlockSpec((8, lanes), lambda g, s: (0, g))
    heads = width // HEAD
    return pl.pallas_call(
        functools.partial(attn_bwd_kernel, qb=qb, kb=kb),
        grid_spec=pltpu.PrefetchScalarGridSpec(
            num_scalar_prefetch=1,
            grid=(heads // GROUP,),
            in_specs=[column] * 4 + [edge] * 2 + [row] * 2 + [column] * 2 + [small],
            out_specs=[column] * 3 + [small],
            scratch_shapes=[pltpu.VMEM((GROUP, count, PAIR), BF)] * 3
            + [pltpu.VMEM((qb, lanes), F32)]
            + [pltpu.VMEM((count, lanes), F32)] * 2,
        ),
        out_shape=[jax.ShapeDtypeStruct((count, width), BF)] * 3
        + [jax.ShapeDtypeStruct((8, width), F32)],
        compiler_params=params(),
        cost_estimate=cost(40 * count * count * heads * HEAD, 18 * count * width, heads * count * count),
        name="attention_backward",
    )(span, q, k, v, do, start, end, inverse, delta, rq, rk, scale_lanes)


def proj_kernel(tokens, mixed, cotangent, member, modulation, weight, after, branch, hidden, down):
    width = tokens.shape[1]
    part = lambda i: nn(member[...], modulation[:, i * width : (i + 1) * width])
    out = nn(mixed[...], weight[...])
    total = tokens[...].astype(F32) + part(0) * out
    after[...] = total
    branch[...] = out.astype(BF)
    unit, _ = centre(total)
    hidden[...] = (unit * (1.0 + part(3)) + part(5)).astype(BF)
    down[...] = (cotangent[...].astype(F32) * part(1)).astype(BF)


def proj_call(tokens, mixed, cotangent, member, modulation, weight, rows=256):
    count, width = tokens.shape
    some = pl.BlockSpec((rows, width), lambda s: (s, 0))
    whole = lambda x: pl.BlockSpec(x.shape, lambda s: (0, 0))
    return pl.pallas_call(
        proj_kernel,
        grid=(count // rows,),
        in_specs=[
            some,
            some,
            some,
            pl.BlockSpec((rows, member.shape[1]), lambda s: (s, 0)),
            whole(modulation),
            pl.BlockSpec((width, width), lambda s: (0, 0)),
        ],
        out_specs=[some] * 4,
        out_shape=[
            jax.ShapeDtypeStruct((count, width), d) for d in (F32, BF, BF, BF)
        ],
        compiler_params=params(),
        cost_estimate=cost(2 * count * width * width, 16 * count * width),
        name="projection",
    )(tokens, mixed, cotangent, member, modulation, weight)


def split_blocks(odd, result, rows, kept, sent):
    result = result.astype(BF)
    for at in range(0, result.shape[0], 2 * rows):
        even_part = result[at : at + rows]
        odd_part = result[at + rows : at + 2 * rows]
        put = slice(at // 2, at // 2 + rows)
        kept[put, :] = jnp.where(odd, odd_part, even_part)
        sent[put, :] = jnp.where(odd, even_part, odd_part)


def mlp_kernel(core, hidden, down, up_w, down_w, *refs, rows, own):
    split = len(refs) == 9
    mlp, back = refs[:2]
    grads = refs[2:-3]
    active, grad, turned = refs[-3:]
    step = pl.program_id(0)
    odd = core[0] == 1

    @pl.when(step == 0)
    def _():
        mlp[...] = jnp.zeros_like(mlp)
        back[...] = jnp.zeros_like(back)
        turned[...] = jnp.transpose(hidden[...])

    for at in range(0, hidden.shape[0], rows):
        here = pl.ds(at, rows)
        e = nn(hidden[here, :], up_w[...])
        da = nt(down[here, :], down_w[...])
        square = e * e
        t = jnp.tanh(e * (GELU_A + GELU_A * GELU_B * square))
        half = 0.5 + 0.5 * t
        act = (e * half).astype(BF)
        slope = half + e * (0.5 - 0.5 * t * t) * (GELU_A + 3.0 * GELU_A * GELU_B * square)
        de = (da * slope).astype(BF)
        active[here, :] = act
        grad[here, :] = de
        mlp[here, :] += nn(act, down_w[...])
        back[here, :] += nt(de, up_w[...])
    if split:
        split_blocks(odd, tn(active[...], down[...]), own, grads[2], grads[3])
        split_blocks(odd, nn(turned[...], grad[...]), own, grads[0], grads[1])
    else:
        grads[1][...] = tn(active[...], down[...]).astype(BF)
        grads[0][...] = nn(turned[...], grad[...]).astype(BF)


def mlp_call(core, hidden, down, packed, own, split, block=512, rows=256):
    count, width = hidden.shape
    units = (packed.shape[1] - width) // 2
    per = width // block
    whole = pl.BlockSpec((count, width), lambda s, c: (0, 0))
    first_up, first_down = width // block, (width + units) // width
    wide = lambda n, first: pl.BlockSpec((n, block), lambda s, c: (0, first + s))
    tall = lambda n, first: pl.BlockSpec((n, width), lambda s, c: (s % per, first + s // per))
    kept = 2 if split else 1
    copies = 2 if split else 1
    return pl.pallas_call(
        functools.partial(mlp_kernel, rows=rows, own=own),
        grid_spec=pltpu.PrefetchScalarGridSpec(
            num_scalar_prefetch=1,
            grid=(units // block,),
            in_specs=[whole, whole, wide(width, first_up), tall(block, first_down)],
            out_specs=[whole, whole]
            + [wide(width // kept, 0)] * copies
            + [tall(block // kept, 0)] * copies,
            scratch_shapes=[
                pltpu.VMEM((count, block), BF),
                pltpu.VMEM((count, block), BF),
                pltpu.VMEM((width, count), BF),
            ],
        ),
        out_shape=[jax.ShapeDtypeStruct((count, width), F32)] * 2
        + [jax.ShapeDtypeStruct((width // kept, units), BF)] * (2 * copies),
        compiler_params=params(),
        cost_estimate=cost(12 * count * width * units, 8 * width * units + 12 * count * width),
        name="feed_forward",
    )(core, hidden, down, packed, packed)


def item_sums(turned, x):
    high, low = halves(x)
    return nn(turned, high) + nn(turned, low)


def norm_back(unit, rstd, w):
    inner = jnp.mean(w * unit, axis=-1, keepdims=True)
    return (w - jnp.mean(w, axis=-1, keepdims=True) - unit * inner) * rstd


def middle_kernel(
    mlp, back, after, cotangent, branch, mixed, rest, member, turned, modulation, weight,
    output, grad_in, branch_grad, mixed_grad, delta, sums,
):
    width = after.shape[1]
    part = lambda i: nn(member[...], modulation[:, i * width : (i + 1) * width])
    upstream = cotangent[...].astype(F32)
    v = after[...]
    output[...] = (v + part(1) * mlp[...]).astype(BF)
    g = back[...]
    unit, rstd = centre(v)
    total = upstream + norm_back(unit, rstd, g * (1.0 + part(3)))
    grad_in[...] = total
    down = (total * part(0)).astype(BF)
    branch_grad[...] = down
    mg = nt(down, weight[...]).astype(BF)
    mixed_grad[...] = mg
    product = mg.astype(F32) * (mixed[...].astype(F32) + rest[...].astype(F32))
    head = lax.broadcasted_iota(jnp.int32, (32, width), 0)
    lane = lax.broadcasted_iota(jnp.int32, (32, width), 1) // HEAD
    wanted = GROUP * (head // 8) + head % 8
    pick = jnp.where((wanted == lane) & (head % 8 < GROUP), 1.0, 0.0).astype(BF)
    high, low = halves(product)
    delta[...] = nt(pick, high) + nt(pick, low)

    @pl.when(pl.program_id(0) == 0)
    def _():
        sums[...] = jnp.zeros_like(sums)

    for i, x in enumerate((total * branch[...].astype(F32), upstream * mlp[...], g * unit, g)):
        sums[:, i * width : (i + 1) * width] += item_sums(turned[...], x)


def middle_call(mlp, back, after, cotangent, branch, mixed, rest, member, turned, modulation, weight, rows=256):
    count, width = after.shape
    some = pl.BlockSpec((rows, width), lambda s: (s, 0))
    whole = lambda x: pl.BlockSpec(x.shape, lambda s: (0, 0))
    items = turned.shape[0]
    heads = 8 * (width // HEAD // GROUP)
    return pl.pallas_call(
        middle_kernel,
        grid=(count // rows,),
        in_specs=[some] * 7
        + [
            pl.BlockSpec((rows, member.shape[1]), lambda s: (s, 0)),
            pl.BlockSpec((items, rows), lambda s: (0, s)),
            whole(modulation),
            pl.BlockSpec((width, width), lambda s: (0, 0)),
        ],
        out_specs=[some] * 4
        + [
            pl.BlockSpec((heads, rows), lambda s: (0, s)),
            pl.BlockSpec((items, 4 * width), lambda s: (0, 0)),
        ],
        out_shape=[jax.ShapeDtypeStruct((count, width), d) for d in (BF, F32, BF, BF)]
        + [
            jax.ShapeDtypeStruct((heads, count), F32),
            jax.ShapeDtypeStruct((items, 4 * width), F32),
        ],
        compiler_params=params(),
        cost_estimate=cost(4 * count * width * width, 30 * count * width),
        name="middle",
    )(mlp, back, after, cotangent, branch, mixed, rest, member, turned, modulation, weight)


def first_kernel(dq, dk, dv, weight, tokens, grad_in, member, turned, modulation, tokens_grad, sums):
    width = tokens.shape[1]
    g = (
        nt(dq[...], weight[:, :width])
        + nt(dk[...], weight[:, width : 2 * width])
        + nt(dv[...], weight[:, 2 * width :])
    )
    unit, rstd = centre(tokens[...].astype(F32))
    sc = nn(member[...], modulation[:, 2 * width : 3 * width])
    tokens_grad[...] = (grad_in[...] + norm_back(unit, rstd, g * (1.0 + sc))).astype(BF)

    @pl.when(pl.program_id(0) == 0)
    def _():
        sums[...] = jnp.zeros_like(sums)

    for i, x in enumerate((g * unit, g)):
        sums[:, i * width : (i + 1) * width] += item_sums(turned[...], x)


def first_call(dq, dk, dv, weight, tokens, grad_in, member, turned, modulation, rows=256):
    count, width = tokens.shape
    some = pl.BlockSpec((rows, width), lambda s: (s, 0))
    whole = lambda x: pl.BlockSpec(x.shape, lambda s: (0, 0))
    items = turned.shape[0]
    return pl.pallas_call(
        first_kernel,
        grid=(count // rows,),
        in_specs=[some] * 3
        + [
            whole(weight),
            some,
            some,
            pl.BlockSpec((rows, member.shape[1]), lambda s: (s, 0)),
            pl.BlockSpec((items, rows), lambda s: (0, s)),
            whole(modulation),
        ],
        out_specs=[some, pl.BlockSpec((items, 2 * width), lambda s: (0, 0))],
        out_shape=[
            jax.ShapeDtypeStruct((count, width), BF),
            jax.ShapeDtypeStruct((items, 2 * width), F32),
        ],
        compiler_params=params(),
        cost_estimate=cost(6 * count * width * width, 18 * count * width),
        name="first_norm_backward",
    )(dq, dk, dv, weight, tokens, grad_in, member, turned, modulation)


def weight_grad_kernel(core, *refs, rows, count):
    split = (len(refs) - 2 - count) == 2
    x = refs[0]
    ys = refs[1 : 1 + count]
    outs = refs[1 + count : -1]
    turned = refs[-1]
    step = pl.program_id(0)
    per = pl.num_programs(0) // count

    @pl.when(step == 0)
    def _():
        turned[...] = jnp.transpose(x[...])

    for which in range(count):

        @pl.when((step >= which * per) & (step < (which + 1) * per))
        def _():
            result = nn(turned[...], ys[which][...])
            if split:
                split_blocks(core[0] == 1, result, rows, outs[0], outs[1])
            else:
                outs[0][...] = result.astype(BF)


def weight_grad_call(core, x, ys, rows, split, block=512):
    count, width = x.shape
    columns = ys[0].shape[1]
    per = columns // block
    steps = per * len(ys)
    wide = lambda n: pl.BlockSpec((n, block), lambda s, c: (0, s))
    shapes = [(width // 2, columns * len(ys))] * 2 if split else [(width, columns * len(ys))]
    part = lambda which: pl.BlockSpec(
        (count, block), lambda s, c: (0, jnp.clip(s - which * per, 0, per - 1))
    )
    return pl.pallas_call(
        functools.partial(weight_grad_kernel, rows=rows, count=len(ys)),
        grid_spec=pltpu.PrefetchScalarGridSpec(
            num_scalar_prefetch=1,
            grid=(steps,),
            in_specs=[pl.BlockSpec((count, width), lambda s, c: (0, 0))]
            + [part(i) for i in range(len(ys))],
            out_specs=[wide(shape[0]) for shape in shapes],
            scratch_shapes=[pltpu.VMEM((width, count), BF)],
        ),
        out_shape=[jax.ShapeDtypeStruct(s, BF) for s in shapes],
        compiler_params=params(),
        cost_estimate=cost(2 * count * width * columns * len(ys), 4 * count * columns * len(ys)),
        name="weight_grad",
    )(core, x, *ys)


BOTH = ("wide", "narrow")
LENGTH_TABLE = np.array([0, 1, 5, 14, 30, 55, 91, 155, 255, 424, 680], np.int32)
SCALE_BOUNDS = np.array([1, 5, 14, 30, 55, 91, 155, 255, 424], np.int32)


def bit_count(size):
    return size.bit_length() - 1


def flip(values, axis, size, bit):
    return lax.ppermute(values, axis, [(i, i ^ (1 << bit)) for i in range(size)])


def chip_order(wide, turn):
    outer = list(range(bit_count(wide)))
    turning, last = outer[:-1], outer[-1:]
    turn = turn % max(1, len(turning))
    return turning[turn:] + turning[:turn] + last


def sum_to_owners(block, dims, order, sizes):
    dims = list(dims)
    for step, (axis, bit) in enumerate(order):
        at = dims.index((axis, bit))
        dims.pop(at)
        mine = (lax.axis_index(axis) >> bit) & 1
        sent = lax.dynamic_index_in_dim(block, 1 - mine, at, keepdims=False)
        kept = lax.dynamic_index_in_dim(block, mine, at, keepdims=False)
        got = flip(sent, axis, sizes[axis], bit)
        block = kept.astype(F32) + got.astype(F32)
        if step < len(order) - 1:
            block = block.astype(BF)
    return block


def scatter_sum(parts, sizes, turn):
    wide, narrow = sizes["wide"], sizes["narrow"]
    dims = [("wide", b) for b in reversed(range(bit_count(wide)))]
    dims += [("narrow", b) for b in reversed(range(bit_count(narrow)))]
    order = [("narrow", b) for b in range(bit_count(narrow))]
    order += [("wide", b) for b in chip_order(wide, turn)]
    if len(parts) == 2:
        kept, sent = parts
        got = flip(sent, "narrow", narrow, 0)
        block = (kept.astype(F32) + got.astype(F32)).astype(BF)
        dims.remove(("narrow", 0))
        order = order[1:]
    else:
        (block,) = parts
    own = block.shape[0] // 2 ** len(dims)
    return sum_to_owners(block.reshape((2,) * len(dims) + (own, block.shape[1])), dims, order, sizes)


def gather_halves(shard, sizes, order):
    block = shard[None]
    for bit in order:
        got = flip(block, "wide", sizes["wide"], bit)
        block = jnp.concatenate([block, got], axis=0)
    block = block.reshape(-1, shard.shape[1])
    return block, flip(block, "narrow", sizes["narrow"], 0)


def relative_place(owner, me, order):
    apart = owner ^ me
    place = jnp.zeros_like(apart)
    for at, bit in enumerate(order):
        place = place | (((apart >> (bit + 1)) & 1) << at)
    return 2 * place + (apart & 1)


def layout(level_row, count):
    lengths = jnp.sum(
        jnp.where(
            level_row[:, None] == jnp.arange(11, dtype=jnp.int32)[None, :],
            jnp.asarray(LENGTH_TABLE)[None, :],
            0,
        ),
        axis=1,
    ).astype(jnp.int32)
    starts = jnp.cumsum(lengths) - lengths
    position = jnp.arange(count, dtype=jnp.int32)[None, :]
    inside = (position >= starts[:, None]) & (position < (starts + lengths)[:, None])
    inside_int = inside.astype(jnp.int32)
    covered = jnp.sum(inside_int, axis=0, keepdims=True) > 0
    first = jnp.where(covered, jnp.sum(inside_int * starts[:, None], axis=0, keepdims=True), position)
    offset = position - first
    length = jnp.full_like(position, int(LENGTH_TABLE[1]))
    for low, high in zip(LENGTH_TABLE[1:-1], LENGTH_TABLE[2:]):
        length = jnp.where(offset >= int(low), int(high), length)
    return inside, first, first + jnp.where(covered, length, 1)


def per_device(
    tokens,
    class_table,
    ada_weight,
    qkv_weight,
    proj_weight,
    head_scale,
    fc1_weight,
    fc2_weight,
    levels,
    labels,
    cotangent,
):
    count, width = tokens.shape
    head_count = head_scale.shape[0]
    sizes = {"wide": lax.axis_size("wide"), "narrow": lax.axis_size("narrow")}
    devices = sizes["wide"] * sizes["narrow"]
    me = lax.axis_index("wide") * sizes["narrow"] + lax.axis_index("narrow")
    core = (lax.axis_index("narrow") & 1).reshape(1).astype(jnp.int32)
    owners = jnp.arange(devices, dtype=jnp.int32)
    slots = labels.shape[1]
    own = proj_weight.shape[0]
    blocks = fc2_weight.shape[0] // own
    paired = own % 16 == 0 and sizes["narrow"] == 2

    label_block = jnp.zeros((own, PAIR), BF)
    label_block = label_block.at[0, :slots].set((labels[0] // 256).astype(BF))
    label_block = label_block.at[1, :slots].set((labels[0] % 256).astype(BF))
    table_shard = jnp.concatenate([class_table, label_block], axis=1)
    if paired:
        orders = [chip_order(sizes["wide"], turn)[::-1] for turn in range(3)]
        table_halves = gather_halves(table_shard, sizes, orders[0])
        table_all = jnp.stack([h.reshape(-1, own, width + PAIR) for h in table_halves], axis=1)
        table_all = table_all.reshape(devices, own, width + PAIR)
        weights = [
            gather_halves(qkv_weight[:, i * width : (i + 1) * width], sizes, orders[i])
            for i in range(3)
        ]
        table_places = relative_place(owners, me, orders[0])
        places = jnp.stack([relative_place(owners, me, o) for o in orders]).astype(jnp.int32)
    else:
        table_all = lax.all_gather(table_shard, BOTH, axis=0, tiled=False)
        qkv_all = lax.all_gather(qkv_weight, BOTH, axis=0, tiled=True)
        weights = [(qkv_all[:, i * width : (i + 1) * width],) for i in range(3)]
        table_places = owners
        places = jnp.stack([owners] * 3)
    up_shard = fc1_weight.reshape(own, devices, blocks, own).transpose(0, 2, 1, 3)
    packed = lax.all_gather(
        jnp.concatenate(
            [proj_weight, up_shard.reshape(own, -1)]
            + [fc2_weight[i * own : (i + 1) * own] for i in range(blocks)],
            axis=1,
        ),
        BOTH,
        axis=0,
        tiled=True,
    )

    picked = (table_places[:, None] == owners[None, :]).astype(F32)
    label_parts = jnp.dot(
        picked, table_all[:, :2, width : width + 2 * slots].reshape(devices, -1).astype(F32)
    ).reshape(devices, 2, 2 * slots)
    labels_all = (256.0 * label_parts[:, 0, :slots] + label_parts[:, 1, :slots]).astype(jnp.int32)
    labels_all = labels_all.reshape(-1)
    label_owner = labels_all // own
    if paired:
        label_place = relative_place(label_owner, me, orders[0]) * own + labels_all % own
    else:
        label_place = labels_all
    label_pick = (
        label_place[:, None] == jnp.arange(devices * own, dtype=jnp.int32)[None, :]
    ).astype(BF)
    class_vec = jnp.dot(
        label_pick, table_all[:, :, :width].reshape(-1, width), preferred_element_type=F32
    )
    lifted = jax.nn.silu(class_vec).astype(BF)
    ada_columns = lax.all_to_all(ada_weight, BOTH, 1, 0, tiled=True)
    modulation = lax.all_to_all(
        jnp.dot(lifted, ada_columns, preferred_element_type=F32), BOTH, 0, 1, tiled=True
    )
    high = lax.reduce_precision(modulation, 8, 7)
    middle = lax.reduce_precision(modulation - high, 8, 7)
    low = modulation - high - middle
    terms = jnp.pad(jnp.concatenate([high, middle, low]), ((0, 32 - 3 * slots), (0, 0))).astype(BF)

    inside, first, last = layout(levels[0], count)
    turned = jnp.pad(inside.astype(BF), ((0, 16 - slots), (0, 0)))
    member = jnp.pad(jnp.concatenate([inside] * 3).astype(BF), ((0, 32 - 3 * slots), (0, 0))).T
    starts = jnp.broadcast_to(first, (8, count))
    ends = jnp.broadcast_to(last, (8, count))
    tile = 256
    span = jnp.concatenate(
        [first[:, ::tile] // tile, (last[:, tile - 1 :: tile] + tile - 1) // tile]
    ).astype(jnp.int32)
    scale_lanes = jnp.broadcast_to(jnp.repeat(head_scale, width // head_count)[None], (8, width))

    hidden_one, q, k, v, rq, rk, qkv_full = qkv_call(
        places, tokens, member, terms, weights, scale_lanes
    )
    mixed, rest, inverse = attn_fwd_call(
        span, q, k, v, first.reshape(count, 1), last.reshape(count, 1), tile, tile
    )
    after, branch, hidden_two, down = proj_call(tokens, mixed, cotangent, member, terms, packed)
    mlp, back, *grads = mlp_call(core, hidden_two, down, packed, own, paired)
    split = 2 if paired else 1
    fc1_grad = scatter_sum(grads[:split], sizes, 0)
    fc2_grad = scatter_sum(grads[split:], sizes, 1)
    fc1_grad = fc1_grad.reshape(own, blocks, devices, own).transpose(0, 2, 1, 3).reshape(own, -1)
    fc2_grad = fc2_grad.reshape(own, blocks, width).transpose(1, 0, 2).reshape(-1, width)
    output, grad_in, branch_grad, mixed_grad, delta, sums = middle_call(
        mlp, back, after, cotangent, branch, mixed, rest, member, turned, terms, packed
    )
    proj_grad = scatter_sum(
        weight_grad_call(core, mixed, [branch_grad], own, paired), sizes, 2
    )
    dq, dk, dv, scale_part = attn_bwd_call(
        span, q, k, v, mixed_grad, starts, ends, inverse,
        delta.reshape(-1, 8, count), rq, rk, scale_lanes, tile, tile,
    )
    qkv_grad = scatter_sum(weight_grad_call(core, hidden_one, [dq, dk, dv], own, paired), sizes, 0)
    tokens_grad, first_sums = first_call(
        dq, dk, dv, qkv_full, tokens, grad_in, member, turned, terms
    )

    early, late = sums[:slots].astype(BF), first_sums[:slots].astype(BF)
    early_all = lax.all_gather(early, BOTH, axis=0, tiled=True)
    late_all = lax.all_gather(late, BOTH, axis=0, tiled=True)
    cut = lambda x, i: x[:, i * width : (i + 1) * width]
    pieces = [cut(early_all, 0), cut(early_all, 1), cut(late_all, 0), cut(early_all, 2), cut(late_all, 1), cut(early_all, 3)]
    modulation_grad = jnp.concatenate(pieces, axis=1)
    own_width = width // devices
    own_lifted = lax.dynamic_slice_in_dim(lifted, me * own_width, own_width, 1)
    own_vec = lax.dynamic_slice_in_dim(class_vec, me * own_width, own_width, 1)
    ada_grad = tn(own_lifted, modulation_grad)
    lifted_grad = nt(modulation_grad, ada_weight)
    _, silu_pull = jax.vjp(jax.nn.silu, own_vec)
    class_grad = silu_pull(lifted_grad)[0]
    label_true = (labels_all[:, None] == jnp.arange(devices * own, dtype=jnp.int32)[None, :]).astype(F32)
    table_columns = jnp.einsum("ic,id->cd", label_true, class_grad, precision=lax.Precision.HIGHEST)
    scale_sums = scale_part[0].reshape(head_count, HEAD)[:, 0]
    head_rows = -(-head_count // own_width)
    head_rows += -head_rows % 8
    scale_rows = jnp.pad(scale_sums, (0, head_rows * own_width - head_count)).reshape(
        1, head_rows, own_width
    )
    outgoing = jnp.concatenate(
        [
            table_columns.reshape(devices, own, own_width),
            jnp.broadcast_to(scale_rows, (devices, head_rows, own_width)),
        ],
        axis=1,
    ).reshape(-1, own_width)
    incoming = lax.all_to_all(outgoing, BOTH, 0, 1, tiled=True)
    table_grad = incoming[:own]
    scale_grad = jnp.sum(incoming[own:].reshape(head_rows, devices, own_width), axis=1).reshape(-1)[
        :head_count
    ]
    return (
        output,
        tokens_grad,
        table_grad,
        ada_grad,
        qkv_grad,
        proj_grad,
        scale_grad,
        fc1_grad,
        fc2_grad,
    )


def solution(mesh):
    rows = P(BOTH, None)
    in_specs = (rows,) * 5 + (P(),) + (rows,) * 5
    out_specs = (rows,) * 6 + (P(),) + (rows,) * 2
    return jax.shard_map(
        per_device, mesh=mesh, in_specs=in_specs, out_specs=out_specs, check_vma=False
    )
```

```python
import functools
import jax
import jax.numpy as jnp
import numpy as np
from jax import lax
from jax.experimental import pallas as pl
from jax.experimental.pallas import tpu as pltpu
from jax.sharding import PartitionSpec as P

NORM_EPS = 1e-06
BF, F32 = jnp.bfloat16, jnp.float32
VMEM_BYTES = 56 * 2**20
HEAD = 64
PAIR = 2 * HEAD
GROUP = 4
GELU_A, GELU_B = 0.7978845608028654, 0.044715


def nn(a, b):
    return lax.dot_general(a, b, (((1,), (0,)), ((), ())), preferred_element_type=F32)


def nt(a, b):
    return lax.dot_general(a, b, (((1,), (1,)), ((), ())), preferred_element_type=F32)


def tn(a, b):
    return lax.dot_general(a, b, (((0,), (0,)), ((), ())), preferred_element_type=F32)


def halves(x):
    high = x.astype(BF)
    return high, (x - high.astype(F32)).astype(BF)


def params(steps=1):
    return pltpu.CompilerParams(
        vmem_limit_bytes=VMEM_BYTES, dimension_semantics=("arbitrary",) * steps
    )


def cost(flops, size, exps=0):
    return pl.CostEstimate(flops=int(flops), bytes_accessed=int(size), transcendentals=int(exps))


awaited, done = [], []


def await_all(*values):
    awaited.extend(values)


def launch(kernel, grid_spec=None, grid=None, in_specs=None, out_specs=None, out_shape=None, **others):
    spec = grid_spec or dict(num_scalar_prefetch=0, grid=grid, in_specs=in_specs, out_specs=out_specs)
    waits = tuple(awaited)
    awaited.clear()
    given = spec["num_scalar_prefetch"] + len(spec["in_specs"])
    single = not isinstance(out_shape, (list, tuple))
    outs = [spec["out_specs"]] if single else list(spec["out_specs"])
    shapes = [out_shape] if single else list(out_shape)

    def body(*refs):
        mark = refs[given + len(waits)]
        mark[...] = jnp.zeros_like(mark)
        kernel(*refs[:given], *refs[given + len(waits) + 1 :])

    zeros = lambda *_: (0, 0)
    spec = dict(
        spec,
        in_specs=list(spec["in_specs"]) + [pl.BlockSpec(memory_space=pl.ANY)] * len(waits),
        out_specs=[pl.BlockSpec((8, PAIR), zeros)] + outs,
    )
    shapes = [jax.ShapeDtypeStruct((8, PAIR), F32)] + shapes
    call = pl.pallas_call(
        body, grid_spec=pltpu.PrefetchScalarGridSpec(**spec), out_shape=shapes, **others
    )

    def run(*args):
        mark, *result = call(*args, *waits)
        done[:] = [mark]
        return result[0] if single else result

    return run


def head_ones(dtype=BF):
    row = lax.broadcasted_iota(jnp.int32, (PAIR, PAIR), 0) // HEAD
    column = lax.broadcasted_iota(jnp.int32, (PAIR, PAIR), 1) // HEAD
    return (row == column).astype(F32).astype(dtype)


def head_sums(x):
    ones = head_ones()
    parts = []
    for at in range(0, x.shape[1], PAIR):
        high, low = halves(x[:, at : at + PAIR])
        parts.append(nn(high, ones) + nn(low, ones))
    return parts[0] if len(parts) == 1 else jnp.concatenate(parts, axis=1)


def centre(x):
    mean = jnp.mean(x, axis=-1, keepdims=True)
    centred = x - mean
    rstd = lax.rsqrt(jnp.mean(centred * centred, axis=-1, keepdims=True) + NORM_EPS)
    return centred * rstd, rstd


def modulation_kernel(device, *refs, order, slots, rows, own, width):
    *tables, ada, class_vec, lifted, labels, modulation = refs
    me = device[0]
    held = tables[0].shape[0]
    count = rows * (held // own)
    total = count * len(tables)
    iota = lambda shape, axis: lax.broadcasted_iota(jnp.int32, shape, axis)

    def place_of(owner):
        return relative_place(owner, me, order) if len(tables) == 2 else owner

    for index, table in enumerate(tables):
        at = (iota((count, held), 0) // rows) * own
        row = iota((count, held), 1)
        edge = table[:, width:]
        pick = lambda x: nn(jnp.where(row == x, 1.0, 0.0).astype(BF), edge)
        both = 256.0 * pick(at) + pick(at + 1)
        slot = iota(both.shape, 0) % rows
        mine = (iota(both.shape, 1) == slot) & (slot < slots)
        label = jnp.sum(jnp.where(mine, both, 0.0), axis=1, keepdims=True).astype(jnp.int32)
        place = place_of(label // own) * own + label % own
        place = jnp.where((iota(place.shape, 0) % rows) < slots, place, -1)
        vec = jnp.zeros((count, width), F32)
        for other, source in enumerate(tables):
            vec += nn(jnp.where(place - other * held == row, 1.0, 0.0).astype(BF), source[:, :width])
        here = slice(index * count, (index + 1) * count)
        class_vec[here, :] = vec.astype(BF)
        label = jnp.where((iota(label.shape, 0) % rows) < slots, label, -1)
        labels[here, :] = jnp.broadcast_to(label, (count, PAIR))
        lifted[here, :] = (vec / (1.0 + jnp.exp(-vec))).astype(BF)
    slot = iota((total, total), 0)
    wanted = place_of(slot // rows) * rows + slot % rows
    swap = jnp.where(wanted == iota((total, total), 1), 1.0, 0.0).astype(BF)
    modulation[...] = nn(nn(swap, lifted[...]).astype(BF), ada[...])


def modulation_call(device, tables, ada, order, slots, rows, own):
    width = ada.shape[0]
    total = rows * (tables[0].shape[0] // own) * len(tables)
    whole = lambda shape: pl.BlockSpec(shape, lambda s, d: (0, 0))
    shapes = [(total, width), (total, width), (total, PAIR), (total, ada.shape[1])]
    return launch(
        functools.partial(
            modulation_kernel, order=order, slots=slots, rows=rows, own=own, width=width
        ),
        grid_spec=dict(
            num_scalar_prefetch=1,
            grid=(1,),
            in_specs=[whole(t.shape) for t in tables] + [whole(ada.shape)],
            out_specs=[whole(s) for s in shapes],
        ),
        out_shape=[jax.ShapeDtypeStruct(s, d) for s, d in zip(shapes, (BF, BF, jnp.int32, F32))],
        compiler_params=params(),
        cost_estimate=cost(6 * total * width * width, 8 * width * width),
        name="modulation",
    )(device, *tables, ada)


def ada_kernel(flags, *refs, devices, order):
    early, *lates, lifted, class_vec, labels, ada, scale, ada_grad, outgoing = refs
    own, width = outgoing.shape[1] - scale.shape[0], lifted.shape[1]
    share = width // devices
    size = max(share, PAIR)
    row = lax.broadcasted_iota(jnp.int32, (width, size), 0)
    lane = lax.broadcasted_iota(jnp.int32, (width, size), 1)
    pick = jnp.where((row == flags[0] * share + lane) & (lane < share), 1.0, 0.0).astype(BF)
    own_lifted = nn(lifted[...], pick).astype(BF)
    own_vec = nn(class_vec[...], pick)[:, :share]
    slots = early.shape[0]
    slot = lax.broadcasted_iota(jnp.int32, (slots, slots), 1)
    rows = slots // devices
    place = relative_place(slot // rows, flags[0], order) * rows + slot % rows
    place_of = lax.broadcasted_iota(jnp.int32, (slots, slots), 0)
    early_grad = nn(jnp.where(place == place_of, 1.0, 0.0).astype(BF), early[...]).astype(BF)
    late_grad = jnp.concatenate([late[...] for late in lates], axis=0)
    cut = lambda x, i: x[:, i * width : (i + 1) * width]
    grad = jnp.concatenate(
        [cut(early_grad, 0), cut(early_grad, 1), cut(late_grad, 0)]
        + [cut(early_grad, 2), cut(late_grad, 1), cut(early_grad, 3)],
        axis=1,
    )
    total = tn(own_lifted, grad)
    ada_grad[...] = total[:share]
    gate = 1.0 / (1.0 + jnp.exp(-own_vec))
    grad = nt(grad, ada[...]) * (gate * (1.0 + own_vec * (1.0 - gate)))
    classes = devices * own
    column = lax.broadcasted_iota(jnp.int32, (slots, classes), 1)
    hot = jnp.where(labels[:, 0:1] == column, 1.0, 0.0).astype(BF)
    high, low = halves(grad)
    least = (grad - high.astype(F32) - low.astype(F32)).astype(BF)
    table = tn(hot, high) + tn(hot, low) + tn(hot, least)
    for device in range(devices):
        outgoing[device, :own, :] = table[device * own : (device + 1) * own]
        outgoing[device, own:, :] = scale[...]


def ada_call(flags, early, lates, lifted, class_vec, labels, ada, scale, devices, order):
    own, width = ada.shape[0], lifted.shape[1]
    whole = lambda x: pl.BlockSpec(x.shape, lambda s, f: (0,) * len(x.shape))
    shapes = [
        jax.ShapeDtypeStruct(ada.shape, F32),
        jax.ShapeDtypeStruct((devices, own + scale.shape[0], width // devices), F32),
    ]
    args = (early, *lates, lifted, class_vec, labels, ada, scale)
    return launch(
        functools.partial(ada_kernel, devices=devices, order=order),
        grid_spec=dict(
            num_scalar_prefetch=1,
            grid=(1,),
            in_specs=[whole(x) for x in args],
            out_specs=[whole(x) for x in shapes],
        ),
        out_shape=shapes,
        compiler_params=params(),
        cost_estimate=cost(10**9, 10**7),
        name="adaptive_norm_backward",
    )(flags, *args)


def qkv_kernel(places, tokens, member, modulation, *refs, pieces, parts):
    weights, (scale, hidden, q, k, v, rq, rk, ordered) = refs[: pieces * parts], refs[pieces * parts :]
    step = pl.program_id(0)
    width = tokens.shape[1]
    block = ordered.shape[1]
    per = width // block
    share = 3 * per // parts
    rows = 256

    @pl.when(step == 0)
    def _():
        for at in range(0, tokens.shape[0], rows):
            here = pl.ds(at, rows)
            unit, _ = centre(tokens[here, :].astype(F32))
            sc = nn(member[here, :], modulation[:, 2 * width : 3 * width])
            sh = nn(member[here, :], modulation[:, 4 * width : 5 * width])
            hidden[here, :] = (unit * (1.0 + sc) + sh).astype(BF)

    for part in range(parts):

        @pl.when((step >= part * share) & (step < (part + 1) * share))
        def _():
            if pieces == 1:
                ordered[...] = weights[part][...]
                return
            own, other = weights[2 * part : 2 * part + 2]
            owners = places.shape[1]
            size = width // owners
            for owner in range(owners):
                place = places[part, owner]
                second = place >= owners // 2
                at = pl.multiple_of((place - jnp.where(second, owners // 2, 0)) * size, size)
                put = slice(owner * size, (owner + 1) * size)

                @pl.when(jnp.logical_not(second))
                def _():
                    ordered[put, :] = own[pl.ds(at, size), :]

                @pl.when(second)
                def _():
                    ordered[put, :] = other[pl.ds(at, size), :]

    for which in range(3):

        @pl.when((step >= which * per) & (step < (which + 1) * per))
        def _():
            for at in range(0, tokens.shape[0], rows):
                here = pl.ds(at, rows)
                out = nn(hidden[here, :], ordered[...])
                if which < 2:
                    r = lax.rsqrt(head_sums(out * out) + NORM_EPS)
                    (rq, rk)[which][here, :] = r.astype(BF)
                    out = out * r
                if which == 0:
                    out = out * scale[0:1, :]
                (q, k, v)[which][here, :] = out.astype(BF)


def qkv_call(places, tokens, member, modulation, weights, scale_lanes, block=512):
    count, width = tokens.shape
    per = width // block
    pieces, parts = len(weights[0]), len(weights)
    share = 3 * per // parts
    column = lambda rows, first, number: pl.BlockSpec(
        (rows, block), lambda s, p: (0, jnp.clip(s - first, 0, number - 1))
    )
    whole = lambda x: pl.BlockSpec(x.shape, lambda s, p: (0, 0))
    columns = [column(count, i * per, per) for i in range(3)]
    return launch(
        functools.partial(qkv_kernel, pieces=pieces, parts=parts),
        grid_spec=dict(
            num_scalar_prefetch=1,
            grid=(3 * per,),
            in_specs=[whole(tokens), whole(member), whole(modulation)]
            + [column(w.shape[0], i * share, share) for i in range(parts) for w in weights[i]]
            + [column(8, 0, per)],
            out_specs=[pl.BlockSpec((count, width), lambda s, p: (0, 0))]
            + columns
            + columns[:2]
            + [pl.BlockSpec((width, block), lambda s, p: (0, s))],
        ),
        out_shape=[jax.ShapeDtypeStruct((count, width), BF)] * 6
        + [jax.ShapeDtypeStruct((width, 3 * width), BF)],
        compiler_params=params(),
        cost_estimate=cost(6 * count * width * width, 2 * (13 * count * width)),
        name="qkv_forward",
    )(places, tokens, member, modulation, *[w for ws in weights for w in ws], scale_lanes)


def lane_masked(x, which):
    lane = lax.broadcasted_iota(jnp.int32, x.shape, 1) // HEAD
    return jnp.where(lane == which, x, jnp.zeros_like(x))


def attn_fwd_kernel(span, q, k, v, start, end, mixed, rest, inverse, v_ext, qm, *, qb, kb):
    count = q.shape[0]
    pairs = q.shape[1] // PAIR
    for pair in range(pairs):
        lanes = slice(pair * PAIR, (pair + 1) * PAIR)
        for h in range(2):
            vv = v[:, lanes]
            lane = lax.broadcasted_iota(jnp.int32, vv.shape, 1) // HEAD
            v_ext[2 * pair + h] = jnp.where(lane == h, vv, jnp.ones_like(vv))
            qm[2 * pair + h] = lane_masked(q[:, lanes], h)

    def one_block(i, _):
        first = pl.multiple_of(i * qb, qb)
        here = pl.ds(first, qb)
        low, high = start[here, :], end[here, :]

        def step(j, totals):
            at = pl.multiple_of(j * kb, kb)
            there = pl.ds(at, kb)
            place = at + lax.broadcasted_iota(jnp.int32, (qb, kb), 1)
            seen = (place >= low) & (place < high)
            out = []
            for h in range(2 * pairs):
                pair = h // 2
                s = nt(qm[h, here, :], k[there, pair * PAIR : (pair + 1) * PAIR])
                p = jnp.where(seen, jnp.exp(s), 0.0).astype(BF)
                out.append(totals[h] + nn(p, v_ext[h, there, :]))
            return tuple(out)

        totals = lax.fori_loop(
            span[0, i], span[1, i], step, tuple(jnp.zeros((qb, PAIR), F32) for _ in range(2 * pairs))
        )
        for pair in range(pairs):
            t0, t1 = totals[2 * pair], totals[2 * pair + 1]
            lane = lax.broadcasted_iota(jnp.int32, t0.shape, 1) // HEAD
            top = jnp.where(lane == 0, t0, t1)
            sums = pltpu.roll(jnp.where(lane == 0, t1, t0), HEAD, 1)
            inv = 1.0 / sums
            high_part, low_part = halves(top * inv)
            mixed[here, pair * PAIR : (pair + 1) * PAIR] = high_part
            rest[here, pair * PAIR : (pair + 1) * PAIR] = low_part
            turned = jnp.transpose(inv)
            inverse[0, 2 * pair : 2 * pair + 1, here] = turned[0:1, :]
            inverse[0, 2 * pair + 1 : 2 * pair + 2, here] = turned[HEAD : HEAD + 1, :]
        return 0

    lax.fori_loop(0, count // qb, one_block, 0)


def attn_fwd_call(span, q, k, v, start, end, qb=256, kb=256):
    count, width = q.shape
    lanes = GROUP * HEAD
    column = pl.BlockSpec((count, lanes), lambda g, s: (0, g))
    edge = pl.BlockSpec((count, 1), lambda g, s: (0, 0))
    heads = width // HEAD
    return launch(
        functools.partial(attn_fwd_kernel, qb=qb, kb=kb),
        grid_spec=dict(
            num_scalar_prefetch=1,
            grid=(heads // GROUP,),
            in_specs=[column, column, column, edge, edge],
            out_specs=[column, column, pl.BlockSpec((1, 8, count), lambda g, s: (g, 0, 0))],
            scratch_shapes=[
                pltpu.VMEM((GROUP, count, PAIR), BF),
                pltpu.VMEM((GROUP, count, PAIR), BF),
            ],
        ),
        out_shape=[
            jax.ShapeDtypeStruct((count, width), BF),
            jax.ShapeDtypeStruct((count, width), BF),
            jax.ShapeDtypeStruct((heads // GROUP, 8, count), F32),
        ],
        compiler_params=params(),
        cost_estimate=cost(16 * count * count * heads * HEAD, 8 * count * width, heads * count * count),
        name="attention_forward",
    )(span, q, k, v, start, end)


def attn_bwd_kernel(
    span, q, k, v, do, start, end, inverse, delta, rq, rk, scale,
    dq, dk, dv, scale_grad, qm, km, dom, dq_acc, dk_acc, dv_acc, *, qb, kb,
):
    count = q.shape[0]
    pairs = q.shape[1] // PAIR
    for pair in range(pairs):
        lanes = slice(pair * PAIR, (pair + 1) * PAIR)
        for h in range(2):
            qm[2 * pair + h] = lane_masked(q[:, lanes], h)
            km[2 * pair + h] = lane_masked(k[:, lanes], h)
            dom[2 * pair + h] = lane_masked(do[:, lanes], h)
    dk_acc[...] = jnp.zeros_like(dk_acc)
    dv_acc[...] = jnp.zeros_like(dv_acc)

    def one_block(i, _):
        first = pl.multiple_of(i * qb, qb)
        here = pl.ds(first, qb)
        low, high = start[0:1, here], end[0:1, here]
        dq_acc[...] = jnp.zeros_like(dq_acc)

        def step(j, _):
            at = pl.multiple_of(j * kb, kb)
            there = pl.ds(at, kb)
            place = at + lax.broadcasted_iota(jnp.int32, (kb, qb), 0)
            seen = (place >= low) & (place < high)
            for pair in range(pairs):
                lanes = slice(pair * PAIR, (pair + 1) * PAIR)
                ps, dss = [], []
                for h in (2 * pair, 2 * pair + 1):
                    s = nt(k[there, lanes], qm[h, here, :])
                    p = jnp.where(seen, jnp.exp(s) * inverse[0, h : h + 1, here], 0.0)
                    dp = nt(v[there, lanes], dom[h, here, :])
                    ps.append(p.astype(BF))
                    dss.append((p * (dp - delta[0, h : h + 1, here])).astype(BF))
                dv_acc[there, lanes] += nn(ps[0], dom[2 * pair, here, :]) + nn(ps[1], dom[2 * pair + 1, here, :])
                dk_acc[there, lanes] += nn(dss[0], qm[2 * pair, here, :]) + nn(dss[1], qm[2 * pair + 1, here, :])
                dq_acc[:, lanes] += tn(dss[0], km[2 * pair, there, :]) + tn(dss[1], km[2 * pair + 1, there, :])
            return 0

        lax.fori_loop(span[0, i], span[1, i], step, 0)
        g = dq_acc[...]
        sc = scale[0:1, :]
        unit = q[here, :].astype(F32) / sc
        inner = head_sums(unit * g)
        dq[here, :] = (sc * rq[here, :].astype(F32) * (g - unit * inner)).astype(BF)
        return jnp.sum(inner, axis=0, keepdims=True)

    def looped(i, total):
        return total + one_block(i, 0)

    total = lax.fori_loop(0, count // qb, looped, jnp.zeros((1, q.shape[1]), F32))
    scale_grad[...] = jnp.broadcast_to(total, scale_grad.shape)
    for at in range(0, count, qb):
        here = pl.ds(at, qb)
        g = dk_acc[here, :]
        unit = k[here, :].astype(F32)
        dk[here, :] = (rk[here, :].astype(F32) * (g - unit * head_sums(unit * g))).astype(BF)
    dv[...] = dv_acc[...].astype(BF)


def attn_bwd_call(
    span, q, k, v, do, start, end, inverse, delta, rq, rk, scale_lanes, first, groups, qb=256, kb=256
):
    count, width = q.shape
    lanes = GROUP * HEAD
    column = pl.BlockSpec((count, lanes), lambda g, s: (0, first + g))
    edge = pl.BlockSpec((1, count), lambda g, s: (0, 0))
    row = pl.BlockSpec((1, 8, count), lambda g, s: (first + g, 0, 0))
    out = pl.BlockSpec((count, lanes), lambda g, s: (0, g))
    heads = groups * GROUP
    return launch(
        functools.partial(attn_bwd_kernel, qb=qb, kb=kb),
        grid_spec=dict(
            num_scalar_prefetch=1,
            grid=(groups,),
            in_specs=[column] * 4
            + [edge] * 2
            + [row] * 2
            + [column] * 2
            + [pl.BlockSpec((8, lanes), lambda g, s: (0, first + g))],
            out_specs=[out] * 3 + [pl.BlockSpec((8, lanes), lambda g, s: (0, g))],
            scratch_shapes=[pltpu.VMEM((GROUP, count, PAIR), BF)] * 3
            + [pltpu.VMEM((qb, lanes), F32)]
            + [pltpu.VMEM((count, lanes), F32)] * 2,
        ),
        out_shape=[jax.ShapeDtypeStruct((count, groups * lanes), BF)] * 3
        + [jax.ShapeDtypeStruct((8, groups * lanes), F32)],
        compiler_params=params(),
        cost_estimate=cost(40 * count * count * heads * HEAD, 18 * count * heads * HEAD, heads * count * count),
        name="attention_backward",
    )(span, q, k, v, do, start, end, inverse, delta, rq, rk, scale_lanes)


def proj_kernel(tokens, mixed, cotangent, member, modulation, weight, after, branch, hidden, down):
    width = tokens.shape[1]
    part = lambda i: nn(member[...], modulation[:, i * width : (i + 1) * width])
    out = nn(mixed[...], weight[...])
    total = tokens[...].astype(F32) + part(0) * out
    after[...] = total
    branch[...] = out.astype(BF)
    unit, _ = centre(total)
    hidden[...] = (unit * (1.0 + part(3)) + part(5)).astype(BF)
    down[...] = (cotangent[...].astype(F32) * part(1)).astype(BF)


def proj_call(tokens, mixed, cotangent, member, modulation, weight, rows=256):
    count, width = tokens.shape
    some = pl.BlockSpec((rows, width), lambda s: (s, 0))
    whole = lambda x: pl.BlockSpec(x.shape, lambda s: (0, 0))
    return launch(
        proj_kernel,
        grid=(count // rows,),
        in_specs=[
            some,
            some,
            some,
            pl.BlockSpec((rows, member.shape[1]), lambda s: (s, 0)),
            whole(modulation),
            pl.BlockSpec((width, width), lambda s: (0, 0)),
        ],
        out_specs=[some] * 4,
        out_shape=[
            jax.ShapeDtypeStruct((count, width), d) for d in (F32, BF, BF, BF)
        ],
        compiler_params=params(),
        cost_estimate=cost(2 * count * width * width, 16 * count * width),
        name="projection",
    )(tokens, mixed, cotangent, member, modulation, weight)


def split_blocks(odd, result, rows, kept, sent):
    result = result.astype(BF)
    for at in range(0, result.shape[0], 2 * rows):
        even_part = result[at : at + rows]
        odd_part = result[at + rows : at + 2 * rows]
        put = slice(at // 2, at // 2 + rows)
        kept[put, :] = jnp.where(odd, odd_part, even_part)
        sent[put, :] = jnp.where(odd, even_part, odd_part)


def mlp_kernel(core, hidden, down, up_w, down_w, *refs, rows, own):
    split = len(refs) == 9
    mlp, back = refs[:2]
    grads = refs[2:-3]
    active, grad, turned = refs[-3:]
    step = pl.program_id(0)
    odd = core[1] == 1

    @pl.when(step == 0)
    def _():
        mlp[...] = jnp.zeros_like(mlp)
        back[...] = jnp.zeros_like(back)
        turned[...] = jnp.transpose(hidden[...])

    for at in range(0, hidden.shape[0], rows):
        here = pl.ds(at, rows)
        e = nn(hidden[here, :], up_w[...])
        da = nt(down[here, :], down_w[...])
        square = e * e
        t = jnp.tanh(e * (GELU_A + GELU_A * GELU_B * square))
        half = 0.5 + 0.5 * t
        act = (e * half).astype(BF)
        slope = half + e * (0.5 - 0.5 * t * t) * (GELU_A + 3.0 * GELU_A * GELU_B * square)
        de = (da * slope).astype(BF)
        active[here, :] = act
        grad[here, :] = de
        mlp[here, :] += nn(act, down_w[...])
        back[here, :] += nt(de, up_w[...])
    if split:
        split_blocks(odd, tn(active[...], down[...]), own, grads[2], grads[3])
        split_blocks(odd, nn(turned[...], grad[...]), own, grads[0], grads[1])
    else:
        grads[1][...] = tn(active[...], down[...]).astype(BF)
        grads[0][...] = nn(turned[...], grad[...]).astype(BF)


def mlp_call(core, hidden, down, packed, own, split, first, count_of, block=512, rows=256):
    count, width = hidden.shape
    units = (packed.shape[1] - width) // 2
    per = width // block
    whole = pl.BlockSpec((count, width), lambda s, c: (0, 0))
    first_up, first_down = width // block + first * per, (width + units) // width + first
    kept = 2 if split else 1
    copies = 2 if split else 1
    wide = pl.BlockSpec((width // kept, block), lambda s, c: (0, s))
    tall = pl.BlockSpec((block // kept, width), lambda s, c: (s % per, s // per))
    return launch(
        functools.partial(mlp_kernel, rows=rows, own=own),
        grid_spec=dict(
            num_scalar_prefetch=1,
            grid=(count_of * per,),
            in_specs=[
                whole,
                whole,
                pl.BlockSpec((width, block), lambda s, c: (0, first_up + s)),
                pl.BlockSpec((block, width), lambda s, c: (s % per, first_down + s // per)),
            ],
            out_specs=[whole, whole] + [wide] * copies + [tall] * copies,
            scratch_shapes=[
                pltpu.VMEM((count, block), BF),
                pltpu.VMEM((count, block), BF),
                pltpu.VMEM((width, count), BF),
            ],
        ),
        out_shape=[jax.ShapeDtypeStruct((count, width), F32)] * 2
        + [jax.ShapeDtypeStruct((width // kept, count_of * width), BF)] * (2 * copies),
        compiler_params=params(),
        cost_estimate=cost(12 * count * width * width * count_of, 20 * count * width),
        name="feed_forward",
    )(core, hidden, down, packed, packed)


def item_sums(turned, x):
    high, low = halves(x)
    return nn(turned, high) + nn(turned, low)


def norm_back(unit, rstd, w):
    inner = jnp.mean(w * unit, axis=-1, keepdims=True)
    return (w - jnp.mean(w, axis=-1, keepdims=True) - unit * inner) * rstd


def middle_kernel(
    mlp_sum, back, after, cotangent, branch, mixed, rest, member, turned, modulation, weight,
    output, grad_in, branch_grad, mixed_grad, delta, sums,
):
    width = after.shape[1]
    part = lambda i: nn(member[...], modulation[:, i * width : (i + 1) * width])
    upstream = cotangent[...].astype(F32)
    v = after[...]
    mlp = mlp_sum[...]
    output[...] = (v + part(1) * mlp).astype(BF)
    g = back[...]
    unit, rstd = centre(v)
    total = upstream + norm_back(unit, rstd, g * (1.0 + part(3)))
    grad_in[...] = total
    down = (total * part(0)).astype(BF)
    branch_grad[...] = down
    mg = nt(down, weight[...]).astype(BF)
    mixed_grad[...] = mg
    product = mg.astype(F32) * (mixed[...].astype(F32) + rest[...].astype(F32))
    head = lax.broadcasted_iota(jnp.int32, (32, width), 0)
    lane = lax.broadcasted_iota(jnp.int32, (32, width), 1) // HEAD
    wanted = GROUP * (head // 8) + head % 8
    pick = jnp.where((wanted == lane) & (head % 8 < GROUP), 1.0, 0.0).astype(BF)
    high, low = halves(product)
    delta[...] = nt(pick, high) + nt(pick, low)

    @pl.when(pl.program_id(0) == 0)
    def _():
        sums[...] = jnp.zeros_like(sums)

    for i, x in enumerate((total * branch[...].astype(F32), upstream * mlp, g * unit, g)):
        sums[:, i * width : (i + 1) * width] += item_sums(turned[...], x)


def middle_call(mlp, back, after, cotangent, branch, mixed, rest, member, turned, modulation, weight, rows=256):
    count, width = after.shape
    some = pl.BlockSpec((rows, width), lambda s: (s, 0))
    whole = lambda x: pl.BlockSpec(x.shape, lambda s: (0, 0))
    items = turned.shape[0]
    heads = 8 * (width // HEAD // GROUP)
    return launch(
        middle_kernel,
        grid=(count // rows,),
        in_specs=[some] * 7
        + [
            pl.BlockSpec((rows, member.shape[1]), lambda s: (s, 0)),
            pl.BlockSpec((items, rows), lambda s: (0, s)),
            whole(modulation),
            pl.BlockSpec((width, width), lambda s: (0, 0)),
        ],
        out_specs=[some] * 4
        + [
            pl.BlockSpec((heads, rows), lambda s: (0, s)),
            pl.BlockSpec((items, 4 * width), lambda s: (0, 0)),
        ],
        out_shape=[jax.ShapeDtypeStruct((count, width), d) for d in (BF, F32, BF, BF)]
        + [
            jax.ShapeDtypeStruct((heads, count), F32),
            jax.ShapeDtypeStruct((items, 4 * width), F32),
        ],
        compiler_params=params(),
        cost_estimate=cost(4 * count * width * width, 30 * count * width),
        name="middle",
    )(mlp, back, after, cotangent, branch, mixed, rest, member, turned, modulation, weight)


def first_kernel(*refs):
    *parts, weight, tokens, grad_in, member, turned, modulation, tokens_grad, sums = refs
    width = tokens.shape[1]
    g, at = 0.0, 0
    for part in parts:
        g = g + nt(part[...], weight[:, at : at + part.shape[1]])
        at += part.shape[1]
    unit, rstd = centre(tokens[...].astype(F32))
    sc = nn(member[...], modulation[:, 2 * width : 3 * width])
    tokens_grad[...] = (grad_in[...] + norm_back(unit, rstd, g * (1.0 + sc))).astype(BF)

    @pl.when(pl.program_id(0) == 0)
    def _():
        sums[...] = jnp.zeros_like(sums)

    for i, x in enumerate((g * unit, g)):
        sums[:, i * width : (i + 1) * width] += item_sums(turned[...], x)


def first_call(parts, weight, tokens, grad_in, member, turned, modulation, rows=256):
    count, width = tokens.shape
    some = pl.BlockSpec((rows, width), lambda s: (s, 0))
    whole = lambda x: pl.BlockSpec(x.shape, lambda s: (0, 0))
    items = turned.shape[0]
    return launch(
        first_kernel,
        grid=(count // rows,),
        in_specs=[pl.BlockSpec((rows, p.shape[1]), lambda s: (s, 0)) for p in parts]
        + [
            pl.BlockSpec((width, 3 * width), lambda s: (0, 0)),
            some,
            some,
            pl.BlockSpec((rows, member.shape[1]), lambda s: (s, 0)),
            pl.BlockSpec((items, rows), lambda s: (0, s)),
            whole(modulation),
        ],
        out_specs=[some, pl.BlockSpec((items, 2 * width), lambda s: (0, 0))],
        out_shape=[
            jax.ShapeDtypeStruct((count, width), BF),
            jax.ShapeDtypeStruct((items, 2 * width), F32),
        ],
        compiler_params=params(),
        cost_estimate=cost(6 * count * width * width, 18 * count * width),
        name="first_norm_backward",
    )(*parts, weight, tokens, grad_in, member, turned, modulation)


def weight_grad_kernel(core, *refs, rows, starts):
    jobs = len(starts) - 1
    xs, ys = refs[:jobs], refs[jobs : jobs + starts[-1][1]]
    outs, turned = refs[jobs + starts[-1][1] : -1], refs[-1]
    step = pl.program_id(0)
    for job in range(jobs):

        @pl.when(step == starts[job][0])
        def _():
            turned[...] = jnp.transpose(xs[job][...])

        (begin, first), (end, last) = starts[job], starts[job + 1]
        per = (end - begin) // (last - first)
        for which in range(first, last):
            at = begin + (which - first) * per

            @pl.when((step >= at) & (step < at + per))
            def _():
                result = nn(turned[...], ys[which][...])
                if len(outs) == 2:
                    split_blocks(core[1] == 1, result, rows, outs[0], outs[1])
                else:
                    outs[0][...] = result.astype(BF)


def weight_grad_call(core, jobs, rows, split, block=512):
    count, width = jobs[0][0].shape
    starts, specs = [(0, 0)], []
    for _, ys in jobs:
        begin, number = starts[-1]
        for y in ys:
            per = y.shape[1] // block
            specs.append(
                pl.BlockSpec(
                    (count, block), lambda s, c, at=begin, per=per: (0, jnp.clip(s - at, 0, per - 1))
                )
            )
            begin, number = begin + per, number + 1
        starts.append((begin, number))
    steps = starts[-1][0]
    columns = steps * block
    wide = lambda n: pl.BlockSpec((n, block), lambda s, c: (0, s))
    shapes = [(width // 2, columns)] * 2 if split else [(width, columns)]
    return launch(
        functools.partial(weight_grad_kernel, rows=rows, starts=tuple(starts)),
        grid_spec=dict(
            num_scalar_prefetch=1,
            grid=(steps,),
            in_specs=[pl.BlockSpec((count, width), lambda s, c: (0, 0)) for _ in jobs] + specs,
            out_specs=[wide(shape[0]) for shape in shapes],
            scratch_shapes=[pltpu.VMEM((width, count), BF)],
        ),
        out_shape=[jax.ShapeDtypeStruct(s, BF) for s in shapes],
        compiler_params=params(),
        cost_estimate=cost(2 * count * width * columns, 4 * count * columns),
        name="weight_grad",
    )(core, *[x for x, _ in jobs], *[y for _, ys in jobs for y in ys])


BOTH = ("wide", "narrow")
LENGTH_TABLE = np.array([0, 1, 5, 14, 30, 55, 91, 155, 255, 424, 680], np.int32)
SCALE_BOUNDS = np.array([1, 5, 14, 30, 55, 91, 155, 255, 424], np.int32)


def bit_count(size):
    return size.bit_length() - 1


def flip(values, axis, size, bit):
    return lax.ppermute(values, axis, [(i, i ^ (1 << bit)) for i in range(size)])


def chip_order(wide, turn):
    outer = list(range(bit_count(wide)))
    turning, last = outer[:-1], outer[-1:]
    turn = turn % max(1, len(turning))
    return turning[turn:] + turning[:turn] + last


def halving_kernel(flags, *refs):
    number = len(refs) // 6
    inputs, outs = refs[: 4 * number], refs[4 * number :]
    for i in range(number):
        kept_here, got_here, kept_there, got_there = inputs[4 * i : 4 * i + 4]
        kept, sent = outs[2 * i : 2 * i + 2]
        add = lambda x, y: (x[:, 0].astype(F32) + y[:, 0].astype(F32)).astype(BF)
        sent[...] = add(kept_there, got_there)
        kept[...] = add(kept_here, got_here)


class Chain:
    def __init__(self, kept, got, sizes, turn, columns=None, index=0):
        self.kept, self.got, self.index = kept, got, index
        self.columns, self.wide = columns or kept.shape[1], sizes["wide"]
        self.dims = list(reversed(range(bit_count(self.wide))))
        self.order = chip_order(self.wide, turn)


def finish_kernel(*refs, blocks):
    number = len(refs) // 3
    for index, (kept, got, out) in enumerate(
        zip(refs[:number], refs[number : 2 * number], refs[2 * number :])
    ):
        total = kept[...].astype(F32) + got[...].astype(F32)
        if not blocks:
            out[...] = total
            continue
        own = total.shape[0]
        width = total.shape[1] // blocks
        if index == 0:
            for owner in range(width // own):
                at = [i * width + owner * own for i in range(blocks)]
                out[:, owner * own * blocks : (owner + 1) * own * blocks] = jnp.concatenate(
                    [total[:, x : x + own] for x in at], axis=1
                )
        else:
            for i in range(blocks):
                out[i * own : (i + 1) * own, :] = total[:, i * width : (i + 1) * width]


def finish(chains, blocks=0):
    whole = lambda x: pl.BlockSpec(x.shape, lambda s: (0, 0))
    kept, got = [c.kept for c in chains], [c.got for c in chains]
    shapes = [jax.ShapeDtypeStruct(x.shape, F32) for x in kept]
    if blocks:
        rows, columns = shapes[1].shape
        shapes[1] = jax.ShapeDtypeStruct((rows * blocks, columns // blocks), F32)
    size = sum(x.size for x in kept)
    return launch(
        functools.partial(finish_kernel, blocks=blocks),
        grid=(1,),
        in_specs=[whole(x) for x in (*kept, *got)],
        out_specs=[whole(x) for x in shapes],
        out_shape=shapes,
        compiler_params=params(),
        cost_estimate=cost(size, 8 * size),
        name="last_sum",
    )(*kept, *got)


def halve(flags, chains, steps):
    specs, args, outs, shapes = [], [], [], []
    for chain in chains:
        bit = chain.order.pop(0)
        at = chain.dims.index(bit)
        chain.dims.pop(at)
        chain.bit = bit
        lead, rows = 2**at, chain.kept.shape[0] // 2 ** (at + 1)
        over = min(lead, steps)
        within = steps // over
        block = (lead // over, rows // within, chain.columns)
        which, index = bit, chain.index
        spec = lambda flip: pl.BlockSpec(
            (block[0], 1, block[1], block[2]),
            lambda s, b, within=within, which=which, index=index: (
                s // within,
                b[2 + which] ^ flip,
                s % within,
                index,
            ),
        )
        kept, got = (x.reshape(lead, 2, rows, -1) for x in (chain.kept, chain.got))
        specs += [spec(0), spec(0), spec(1), spec(1)]
        args += [kept, got, kept, got]
        outs += [pl.BlockSpec(block, lambda s, b, within=within: (s // within, s % within, 0))] * 2
        shapes += [jax.ShapeDtypeStruct((lead, rows, chain.columns), BF)] * 2
    size = sum(int(np.prod(x.shape)) for x in shapes)
    result = launch(
        halving_kernel,
        grid_spec=dict(num_scalar_prefetch=1, grid=(steps,), in_specs=specs, out_specs=outs),
        out_shape=shapes,
        compiler_params=params(),
        cost_estimate=cost(size, 6 * size),
        name="halving_sum",
    )(flags, *args)
    for i, chain in enumerate(chains):
        flat = lambda x: x.reshape(-1, chain.columns)
        chain.kept, chain.index = flat(result[2 * i]), 0
        chain.got = flip(flat(result[2 * i + 1]), "wide", chain.wide, chain.bit)
    return result[0]


def land_kernel(*refs):
    number = len(refs) // 3
    for block, got, out in zip(refs[:number], refs[number : 2 * number], refs[2 * number :]):
        half = block.shape[0]
        out[:half] = block[...]
        out[half:] = got[...]


def land(moves):
    blocks, gots = [m.block for m in moves], [m.got for m in moves]
    shapes = [(2 * x.shape[0],) + x.shape[1:] for x in blocks]
    whole = lambda shape: pl.BlockSpec(shape, lambda s: (0, 0, 0))
    joined = launch(
        land_kernel,
        grid=(1,),
        in_specs=[whole(x.shape) for x in (*blocks, *gots)],
        out_specs=[whole(x) for x in shapes],
        out_shape=[jax.ShapeDtypeStruct(x, BF) for x in shapes],
        compiler_params=params(),
        cost_estimate=cost(0, 4 * sum(int(np.prod(x)) for x in shapes)),
        name="land",
    )(*blocks, *gots)
    for move, block in zip(moves, joined):
        move.block = block


class Gather:
    def __init__(self, block, sizes, order):
        self.block, self.sizes, self.order = block, sizes, list(order) + [None]

    def send(self):
        bit = self.order.pop(0)
        axis = "narrow" if bit is None else "wide"
        self.got = flip(self.block, axis, self.sizes[axis], 0 if bit is None else bit)


    def halves(self):
        return [self.block, self.got]


def owner_sum(x, axis):
    return lax.psum_scatter(x, axis, scatter_dimension=0, tiled=True)


def relative_place(owner, me, order):
    apart = owner ^ me
    place = (apart & 1) << len(order)
    for at, bit in enumerate(order):
        place = place | (((apart >> (bit + 1)) & 1) << at)
    return place


def layout(level_row, count):
    lengths = jnp.sum(
        jnp.where(
            level_row[:, None] == jnp.arange(11, dtype=jnp.int32)[None, :],
            jnp.asarray(LENGTH_TABLE)[None, :],
            0,
        ),
        axis=1,
    ).astype(jnp.int32)
    starts = jnp.cumsum(lengths) - lengths
    position = jnp.arange(count, dtype=jnp.int32)[None, :]
    inside = (position >= starts[:, None]) & (position < (starts + lengths)[:, None])
    inside_int = inside.astype(jnp.int32)
    covered = jnp.sum(inside_int, axis=0, keepdims=True) > 0
    first = jnp.where(covered, jnp.sum(inside_int * starts[:, None], axis=0, keepdims=True), position)
    offset = position - first
    length = jnp.full_like(position, int(LENGTH_TABLE[1]))
    for low, high in zip(LENGTH_TABLE[1:-1], LENGTH_TABLE[2:]):
        length = jnp.where(offset >= int(low), int(high), length)
    return inside, first, first + jnp.where(covered, length, 1)


def per_device(
    tokens,
    class_table,
    ada_weight,
    qkv_weight,
    proj_weight,
    head_scale,
    fc1_weight,
    fc2_weight,
    levels,
    labels,
    cotangent,
):
    count, width = tokens.shape
    head_count = head_scale.shape[0]
    sizes = {"wide": lax.axis_size("wide"), "narrow": lax.axis_size("narrow")}
    devices = sizes["wide"] * sizes["narrow"]
    me = lax.axis_index("wide") * sizes["narrow"] + lax.axis_index("narrow")
    chip = lax.axis_index("wide")
    flags = [me, lax.axis_index("narrow") & 1]
    flags += [(chip >> i) & 1 for i in range(bit_count(sizes["wide"]))]
    flags = jnp.stack(flags).astype(jnp.int32)
    slots = labels.shape[1]
    rows = 8
    own = proj_weight.shape[0]
    blocks = fc2_weight.shape[0] // own
    paired = own % 32 == 0 and sizes["narrow"] == 2

    label_block = jnp.zeros((own, PAIR), BF)
    label_block = label_block.at[0, :slots].set((labels[0] // 256).astype(BF))
    label_block = label_block.at[1, :slots].set((labels[0] % 256).astype(BF))
    table_shard = jnp.concatenate([class_table, label_block], axis=1)
    up_shard = fc1_weight.reshape(own, devices, blocks, own).transpose(0, 2, 1, 3)
    feed_shard = jnp.concatenate(
        [proj_weight, up_shard.reshape(own, -1)]
        + [fc2_weight[i * own : (i + 1) * own] for i in range(blocks)],
        axis=1,
    )
    ada_columns = lax.all_to_all(ada_weight, BOTH, 1, 0, tiled=True)
    if paired:
        orders = [chip_order(sizes["wide"], turn)[::-1] for turn in (0, 1)]
        orders.append([orders[0][0]] + orders[0][1:])
        stages = len(orders[0])
        both = Gather(jnp.concatenate([table_shard, qkv_weight], axis=1)[None], sizes, orders[0][:1])
        both.send()
        land([both])
        cuts = (0, width + PAIR, width + PAIR + 3 * width // 2, 4 * width + PAIR)
        table_move, *moves = (
            Gather(both.block[:, :, low:high], sizes, order[1:])
            for low, high, order in zip(cuts, cuts[1:], orders)
        )
        for move in (table_move, *moves):
            move.send()
        for step in range(1, stages):
            land([table_move])
            table_move.send()
            if step < stages - 1:
                await_all(done[0])
                if step == 1:
                    await_all(ada_columns)
                land(moves)
                for move in moves:
                    move.send()
                await_all(done[0])
            if step == stages - 2:
                feed_shard, table_move.got = lax.optimization_barrier((feed_shard, table_move.got))
        tables = [h.reshape(-1, width + PAIR) for h in table_move.halves()]
    else:
        orders = [()]
        tables = [lax.all_gather(table_shard, BOTH, axis=0, tiled=True)]
    class_vec, lifted, slot_labels, modulation_columns = modulation_call(
        flags, tables, ada_columns, orders[0], slots, rows, own
    )
    if paired:
        await_all(done[0])
        land(moves)
        for move in moves:
            move.send()
        weights = [[h.reshape(width // 2, -1) for h in move.halves()] for move in moves]
        owners = jnp.arange(devices, dtype=jnp.int32)
        places = jnp.stack([relative_place(owners, me, o) for o in orders[1:]]).astype(jnp.int32)
    else:
        weights = [(lax.all_gather(qkv_weight, BOTH, axis=0, tiled=True),)]
        places = jnp.zeros((1, devices), jnp.int32)
    feed_weight = lax.all_gather(feed_shard, BOTH, axis=0, tiled=True)

    modulation = lax.all_to_all(modulation_columns, BOTH, 0, 1, tiled=True)
    high = lax.reduce_precision(modulation, 8, 7)
    middle = lax.reduce_precision(modulation - high, 8, 7)
    low = modulation - high - middle
    terms = jnp.pad(jnp.concatenate([high, middle, low]), ((0, 8), (0, 0))).astype(BF)

    inside, first, last = layout(levels[0], count)
    turned = jnp.pad(inside.astype(BF), ((0, 16 - slots), (0, 0)))
    inside = jnp.pad(inside.astype(BF), ((0, rows - slots), (0, 0)))
    member = jnp.concatenate([inside] * 3 + [jnp.zeros_like(inside)]).T
    tile = 256
    span = jnp.concatenate(
        [first[:, ::tile] // tile, (last[:, tile - 1 :: tile] + tile - 1) // tile]
    ).astype(jnp.int32)
    scale_lanes = jnp.broadcast_to(jnp.repeat(head_scale, width // head_count)[None], (8, width))

    hidden_one, q, k, v, rq, rk, qkv_full = qkv_call(
        places, tokens, member, terms, weights, scale_lanes
    )
    mixed, rest, inverse = attn_fwd_call(
        span, q, k, v, first.reshape(count, 1), last.reshape(count, 1), tile, tile
    )
    after, branch, hidden_two, down = proj_call(
        tokens, mixed, cotangent, member, terms, feed_weight
    )
    mlp, back, *grads = mlp_call(flags, hidden_two, down, feed_weight, own, paired, 0, blocks)
    swap = lambda x: flip(x, "narrow", sizes["narrow"], 0)
    if paired:
        up, down = (
            Chain(kept, swap(sent), sizes, turn)
            for turn, kept, sent in ((0, *grads[:2]), (1, *grads[2:]))
        )
    output, grad_in, branch_grad, mixed_grad, delta, sums = middle_call(
        mlp, back, after, cotangent, branch, mixed, rest, member, turned, terms, feed_weight
    )
    early = jnp.pad(sums[:slots], ((0, rows - slots), (0, 0))).astype(BF)
    early = lax.all_gather(early, BOTH, axis=0, tiled=True)
    if paired:
        await_all(done[0])
        halve(flags, [up, down], 8)
        await_all(done[0])
    else:
        feed = owner_sum(jnp.concatenate(grads, axis=1), BOTH).astype(F32)
        units = blocks * width
        fc1_grad = feed[:, :units].reshape(own, blocks, devices, own).transpose(0, 2, 1, 3)
        fc1_grad = fc1_grad.reshape(own, -1)
        fc2_grad = jnp.concatenate(
            [feed[:, units + i * width : units + (i + 1) * width] for i in range(blocks)]
        )
    *heads, scale_part = attn_bwd_call(
        span, q, k, v, mixed_grad, first, last, inverse, delta.reshape(-1, 8, count), rq, rk,
        scale_lanes, 0, head_count // GROUP, tile, tile,
    )
    if paired:
        await_all(done[0])
        halve(flags, [up, down], 4)
        await_all(done[0])
    qkv_parts = weight_grad_call(flags, [(hidden_one, heads)], own, paired)
    if paired:
        qkv_got = swap(qkv_parts[1])
        await_all(done[0])
    proj_parts = weight_grad_call(flags, [(mixed, [branch_grad])], own, paired)
    if paired:
        qkv = [Chain(qkv_parts[0], qkv_got, sizes, i, 3 * width // 2, i) for i in range(2)]
        proj = Chain(proj_parts[0], swap(proj_parts[1]), sizes, 2)
        await_all(done[0])
        halve(flags, [*qkv, proj], 4)
        await_all(done[0])
    else:
        qkv_grad = owner_sum(qkv_parts[0], BOTH).astype(F32)
        proj_grad = owner_sum(proj_parts[0], BOTH).astype(F32)
    tokens_grad, first_sums = first_call(
        heads, qkv_full, tokens, grad_in, member, turned, terms
    )
    late = jnp.pad(first_sums[:slots], ((0, rows - slots), (0, 0))).astype(BF)
    own_width = width // devices
    scale_sums = scale_part[0].reshape(head_count, HEAD)[:, 0]
    head_rows = -(-head_count // own_width)
    head_rows += -head_rows % 8
    scale_rows = jnp.pad(scale_sums, (0, head_rows * own_width - head_count)).reshape(
        head_rows, own_width
    )
    if paired:
        move = Gather(late[None], sizes, orders[0])
        move.send()
        await_all(done[0])
        halve(flags, [*qkv, proj, up, down], 2)
        for step in range(stages):
            await_all(done[0])
            land([move])
            move.send()
            if step == 2:
                await_all(done[0])
                halve(flags, [*qkv, proj, up, down], 2)
        lates = [h.reshape(-1, h.shape[-1]) for h in move.halves()]
        await_all(done[0])
        ada_grad, outgoing = ada_call(
            flags, early, lates, lifted, class_vec, slot_labels, ada_weight, scale_rows, devices,
            orders[0],
        )
        await_all(done[0])
        halve(flags, [*qkv, proj], 2)
        await_all(done[0])
        fc1_grad, fc2_grad = finish([up, down], blocks)
        await_all(done[0])
        *parts, proj_grad = finish([*qkv, proj])
        qkv_grad = jnp.concatenate(parts, axis=1)
    else:
        late = lax.all_gather(late, BOTH, axis=0, tiled=True)
        cut = lambda x, i: x[:, i * width : (i + 1) * width]
        item_grad = jnp.concatenate(
            [cut(early, 0), cut(early, 1), cut(late, 0), cut(early, 2), cut(late, 1), cut(early, 3)],
            axis=1,
        )
        ada_grad = tn(lax.dynamic_slice_in_dim(lifted, me * own_width, own_width, 1), item_grad)
        own_vec = lax.dynamic_slice_in_dim(class_vec, me * own_width, own_width, 1).astype(F32)
        _, silu_pull = jax.vjp(jax.nn.silu, own_vec)
        class_grad = silu_pull(nt(item_grad, ada_weight))[0]
        hot = (slot_labels[:, :1] == jnp.arange(devices * own, dtype=jnp.int32)[None, :]).astype(F32)
        table_columns = jnp.einsum("ic,id->cd", hot, class_grad, precision=lax.Precision.HIGHEST)
        outgoing = jnp.concatenate(
            [
                table_columns.reshape(devices, own, own_width),
                jnp.broadcast_to(scale_rows[None], (devices,) + scale_rows.shape),
            ],
            axis=1,
        )
    outgoing = outgoing.reshape(-1, own_width)
    incoming = lax.all_to_all(outgoing, BOTH, 0, 1, tiled=True)
    table_grad = incoming[:own]
    scale_grad = jnp.sum(incoming[own:].reshape(head_rows, devices, own_width), axis=1).reshape(-1)[
        :head_count
    ]
    units = blocks * width
    return (
        output,
        tokens_grad,
        table_grad,
        ada_grad,
        qkv_grad,
        proj_grad,
        scale_grad,
        fc1_grad,
        fc2_grad,
    )


def solution(mesh):
    rows = P(BOTH, None)
    in_specs = (rows,) * 5 + (P(),) + (rows,) * 5
    out_specs = (rows,) * 6 + (P(),) + (rows,) * 2
    return jax.shard_map(
        per_device, mesh=mesh, in_specs=in_specs, out_specs=out_specs, check_vma=False
    )
```

```python
import functools
import jax
import jax.numpy as jnp
import numpy as np
from jax import lax
from jax.experimental import pallas as pl
from jax.experimental.pallas import tpu as pltpu
from jax.sharding import PartitionSpec as P

NORM_EPS = 1e-06
BF, F32 = jnp.bfloat16, jnp.float32
VMEM_BYTES = 56 * 2**20
HEAD = 64
PAIR = 2 * HEAD
GROUP = 4
GELU_A, GELU_B = 0.7978845608028654, 0.044715


def nn(a, b):
    return lax.dot_general(a, b, (((1,), (0,)), ((), ())), preferred_element_type=F32)


def nt(a, b):
    return lax.dot_general(a, b, (((1,), (1,)), ((), ())), preferred_element_type=F32)


def tn(a, b):
    return lax.dot_general(a, b, (((0,), (0,)), ((), ())), preferred_element_type=F32)


def halves(x):
    high = x.astype(BF)
    return high, (x - high.astype(F32)).astype(BF)


def params(steps=1):
    return pltpu.CompilerParams(
        vmem_limit_bytes=VMEM_BYTES, dimension_semantics=("arbitrary",) * steps
    )


def cost(flops, size, exps=0):
    return pl.CostEstimate(flops=int(flops), bytes_accessed=int(size), transcendentals=int(exps))


awaited, done = [], []


def await_all(*values):
    awaited.extend(values)


def launch(kernel, grid_spec=None, grid=None, in_specs=None, out_specs=None, out_shape=None, **others):
    spec = grid_spec or dict(num_scalar_prefetch=0, grid=grid, in_specs=in_specs, out_specs=out_specs)
    waits = tuple(awaited)
    awaited.clear()
    given = spec["num_scalar_prefetch"] + len(spec["in_specs"])
    single = not isinstance(out_shape, (list, tuple))
    outs = [spec["out_specs"]] if single else list(spec["out_specs"])
    shapes = [out_shape] if single else list(out_shape)

    def body(*refs):
        mark = refs[given + len(waits)]
        mark[...] = jnp.zeros_like(mark)
        kernel(*refs[:given], *refs[given + len(waits) + 1 :])

    zeros = lambda *_: (0, 0)
    spec = dict(
        spec,
        in_specs=list(spec["in_specs"]) + [pl.BlockSpec(memory_space=pl.ANY)] * len(waits),
        out_specs=[pl.BlockSpec((8, PAIR), zeros)] + outs,
    )
    shapes = [jax.ShapeDtypeStruct((8, PAIR), F32)] + shapes
    call = pl.pallas_call(
        body, grid_spec=pltpu.PrefetchScalarGridSpec(**spec), out_shape=shapes, **others
    )

    def run(*args):
        mark, *result = call(*args, *waits)
        done[:] = [mark]
        return result[0] if single else result

    return run


def head_ones(dtype=BF):
    row = lax.broadcasted_iota(jnp.int32, (PAIR, PAIR), 0) // HEAD
    column = lax.broadcasted_iota(jnp.int32, (PAIR, PAIR), 1) // HEAD
    return (row == column).astype(F32).astype(dtype)


def head_sums(x):
    ones = head_ones()
    parts = []
    for at in range(0, x.shape[1], PAIR):
        high, low = halves(x[:, at : at + PAIR])
        parts.append(nn(high, ones) + nn(low, ones))
    return parts[0] if len(parts) == 1 else jnp.concatenate(parts, axis=1)


def centre(x):
    mean = jnp.mean(x, axis=-1, keepdims=True)
    centred = x - mean
    rstd = lax.rsqrt(jnp.mean(centred * centred, axis=-1, keepdims=True) + NORM_EPS)
    return centred * rstd, rstd


def modulation_kernel(device, *refs, order, slots, rows, own, width):
    *tables, ada, class_vec, lifted, labels, modulation = refs
    me = device[0]
    held = tables[0].shape[0]
    count = rows * (held // own)
    total = count * len(tables)
    iota = lambda shape, axis: lax.broadcasted_iota(jnp.int32, shape, axis)

    def place_of(owner):
        return relative_place(owner, me, order) if len(tables) == 2 else owner

    for index, table in enumerate(tables):
        at = (iota((count, held), 0) // rows) * own
        row = iota((count, held), 1)
        edge = table[:, width:]
        pick = lambda x: nn(jnp.where(row == x, 1.0, 0.0).astype(BF), edge)
        both = 256.0 * pick(at) + pick(at + 1)
        slot = iota(both.shape, 0) % rows
        mine = (iota(both.shape, 1) == slot) & (slot < slots)
        label = jnp.sum(jnp.where(mine, both, 0.0), axis=1, keepdims=True).astype(jnp.int32)
        place = place_of(label // own) * own + label % own
        place = jnp.where((iota(place.shape, 0) % rows) < slots, place, -1)
        vec = jnp.zeros((count, width), F32)
        for other, source in enumerate(tables):
            vec += nn(jnp.where(place - other * held == row, 1.0, 0.0).astype(BF), source[:, :width])
        here = slice(index * count, (index + 1) * count)
        class_vec[here, :] = vec.astype(BF)
        label = jnp.where((iota(label.shape, 0) % rows) < slots, label, -1)
        labels[here, :] = jnp.broadcast_to(label, (count, PAIR))
        lifted[here, :] = (vec / (1.0 + jnp.exp(-vec))).astype(BF)
    slot = iota((total, total), 0)
    wanted = place_of(slot // rows) * rows + slot % rows
    swap = jnp.where(wanted == iota((total, total), 1), 1.0, 0.0).astype(BF)
    modulation[...] = nn(nn(swap, lifted[...]).astype(BF), ada[...])


def modulation_call(device, tables, ada, order, slots, rows, own):
    width = ada.shape[0]
    total = rows * (tables[0].shape[0] // own) * len(tables)
    whole = lambda shape: pl.BlockSpec(shape, lambda s, d: (0, 0))
    shapes = [(total, width), (total, width), (total, PAIR), (total, ada.shape[1])]
    return launch(
        functools.partial(
            modulation_kernel, order=order, slots=slots, rows=rows, own=own, width=width
        ),
        grid_spec=dict(
            num_scalar_prefetch=1,
            grid=(1,),
            in_specs=[whole(t.shape) for t in tables] + [whole(ada.shape)],
            out_specs=[whole(s) for s in shapes],
        ),
        out_shape=[jax.ShapeDtypeStruct(s, d) for s, d in zip(shapes, (BF, BF, jnp.int32, F32))],
        compiler_params=params(),
        cost_estimate=cost(6 * total * width * width, 8 * width * width),
        name="modulation",
    )(device, *tables, ada)


def ada_kernel(flags, *refs, devices, order):
    early, *lates, lifted, class_vec, labels, ada, scale, ada_grad, outgoing = refs
    own, width = outgoing.shape[1] - scale.shape[0], lifted.shape[1]
    share = width // devices
    size = max(share, PAIR)
    row = lax.broadcasted_iota(jnp.int32, (width, size), 0)
    lane = lax.broadcasted_iota(jnp.int32, (width, size), 1)
    pick = jnp.where((row == flags[0] * share + lane) & (lane < share), 1.0, 0.0).astype(BF)
    own_lifted = nn(lifted[...], pick).astype(BF)
    own_vec = nn(class_vec[...], pick)[:, :share]
    slots = early.shape[0]
    slot = lax.broadcasted_iota(jnp.int32, (slots, slots), 1)
    rows = slots // devices
    place = relative_place(slot // rows, flags[0], order) * rows + slot % rows
    place_of = lax.broadcasted_iota(jnp.int32, (slots, slots), 0)
    early_grad = nn(jnp.where(place == place_of, 1.0, 0.0).astype(BF), early[...]).astype(BF)
    late_grad = jnp.concatenate([late[...] for late in lates], axis=0)
    cut = lambda x, i: x[:, i * width : (i + 1) * width]
    grad = jnp.concatenate(
        [cut(early_grad, 0), cut(early_grad, 1), cut(late_grad, 0)]
        + [cut(early_grad, 2), cut(late_grad, 1), cut(early_grad, 3)],
        axis=1,
    )
    total = tn(own_lifted, grad)
    ada_grad[...] = total[:share]
    gate = 1.0 / (1.0 + jnp.exp(-own_vec))
    grad = nt(grad, ada[...]) * (gate * (1.0 + own_vec * (1.0 - gate)))
    classes = devices * own
    column = lax.broadcasted_iota(jnp.int32, (slots, classes), 1)
    hot = jnp.where(labels[:, 0:1] == column, 1.0, 0.0).astype(BF)
    high, low = halves(grad)
    least = (grad - high.astype(F32) - low.astype(F32)).astype(BF)
    table = tn(hot, high) + tn(hot, low) + tn(hot, least)
    for device in range(devices):
        outgoing[device, :own, :] = table[device * own : (device + 1) * own]
        outgoing[device, own:, :] = scale[...]


def ada_call(flags, early, lates, lifted, class_vec, labels, ada, scale, devices, order):
    own, width = ada.shape[0], lifted.shape[1]
    whole = lambda x: pl.BlockSpec(x.shape, lambda s, f: (0,) * len(x.shape))
    shapes = [
        jax.ShapeDtypeStruct(ada.shape, F32),
        jax.ShapeDtypeStruct((devices, own + scale.shape[0], width // devices), F32),
    ]
    args = (early, *lates, lifted, class_vec, labels, ada, scale)
    return launch(
        functools.partial(ada_kernel, devices=devices, order=order),
        grid_spec=dict(
            num_scalar_prefetch=1,
            grid=(1,),
            in_specs=[whole(x) for x in args],
            out_specs=[whole(x) for x in shapes],
        ),
        out_shape=shapes,
        compiler_params=params(),
        cost_estimate=cost(10**9, 10**7),
        name="adaptive_norm_backward",
    )(flags, *args)


def qkv_kernel(places, tokens, member, modulation, *refs, pieces, parts):
    weights, (scale, hidden, q, k, v, rq, rk, ordered) = refs[: pieces * parts], refs[pieces * parts :]
    step = pl.program_id(0)
    width = tokens.shape[1]
    block = ordered.shape[1]
    per = width // block
    share = 4 * per // parts
    rows = 256

    @pl.when(step == 0)
    def _():
        for at in range(0, tokens.shape[0], rows):
            here = pl.ds(at, rows)
            unit, _ = centre(tokens[here, :].astype(F32))
            sc = nn(member[here, :], modulation[:, 2 * width : 3 * width])
            sh = nn(member[here, :], modulation[:, 4 * width : 5 * width])
            hidden[here, :] = (unit * (1.0 + sc) + sh).astype(BF)

    for part in range(parts):

        @pl.when((step >= part * share) & (step < (part + 1) * share))
        def _():
            if pieces == 1:
                ordered[...] = weights[part][...]
                return
            own, other = weights[2 * part : 2 * part + 2]
            owners = places.shape[1]
            size = width // owners
            for owner in range(owners):
                place = places[part, owner]
                second = place >= owners // 2
                at = pl.multiple_of((place - jnp.where(second, owners // 2, 0)) * size, size)
                put = slice(owner * size, (owner + 1) * size)

                @pl.when(jnp.logical_not(second))
                def _():
                    ordered[put, :] = own[pl.ds(at, size), :]

                @pl.when(second)
                def _():
                    ordered[put, :] = other[pl.ds(at, size), :]

    for which in range(3):

        @pl.when((step >= which * per) & (step < (which + 1) * per))
        def _():
            for at in range(0, tokens.shape[0], rows):
                here = pl.ds(at, rows)
                out = nn(hidden[here, :], ordered[...])
                if which < 2:
                    r = lax.rsqrt(head_sums(out * out) + NORM_EPS)
                    (rq, rk)[which][here, :] = r.astype(BF)
                    out = out * r
                if which == 0:
                    out = out * scale[0:1, :]
                (q, k, v)[which][here, :] = out.astype(BF)


def qkv_call(places, tokens, member, modulation, weights, scale_lanes, block=512):
    count, width = tokens.shape
    per = width // block
    pieces, parts = len(weights[0]), len(weights)
    share = 4 * per // parts
    column = lambda rows, first, number: pl.BlockSpec(
        (rows, block), lambda s, p: (0, jnp.clip(s - first, 0, number - 1))
    )
    whole = lambda x: pl.BlockSpec(x.shape, lambda s, p: (0, 0))
    columns = [column(count, i * per, per) for i in range(3)]
    return launch(
        functools.partial(qkv_kernel, pieces=pieces, parts=parts),
        grid_spec=dict(
            num_scalar_prefetch=1,
            grid=(4 * per,),
            in_specs=[whole(tokens), whole(member), whole(modulation)]
            + [column(w.shape[0], i * share, share) for i in range(parts) for w in weights[i]]
            + [column(8, 0, per)],
            out_specs=[pl.BlockSpec((count, width), lambda s, p: (0, 0))]
            + columns
            + columns[:2]
            + [pl.BlockSpec((width, block), lambda s, p: (0, s))],
        ),
        out_shape=[jax.ShapeDtypeStruct((count, width), BF)] * 6
        + [jax.ShapeDtypeStruct((width, 4 * width), BF)],
        compiler_params=params(),
        cost_estimate=cost(6 * count * width * width, 2 * (13 * count * width)),
        name="qkv_forward",
    )(places, tokens, member, modulation, *[w for ws in weights for w in ws], scale_lanes)


def lane_masked(x, which):
    lane = lax.broadcasted_iota(jnp.int32, x.shape, 1) // HEAD
    return jnp.where(lane == which, x, jnp.zeros_like(x))


def attn_fwd_kernel(span, q, k, v, start, end, mixed, rest, inverse, v_ext, qm, *, qb, kb):
    count = q.shape[0]
    pairs = q.shape[1] // PAIR
    for pair in range(pairs):
        lanes = slice(pair * PAIR, (pair + 1) * PAIR)
        for h in range(2):
            vv = v[:, lanes]
            lane = lax.broadcasted_iota(jnp.int32, vv.shape, 1) // HEAD
            v_ext[2 * pair + h] = jnp.where(lane == h, vv, jnp.ones_like(vv))
            qm[2 * pair + h] = lane_masked(q[:, lanes], h)

    def one_block(i, _):
        first = pl.multiple_of(i * qb, qb)
        here = pl.ds(first, qb)
        low, high = start[here, :], end[here, :]

        def step(j, totals):
            at = pl.multiple_of(j * kb, kb)
            there = pl.ds(at, kb)
            place = at + lax.broadcasted_iota(jnp.int32, (qb, kb), 1)
            seen = jnp.where((place >= low) & (place < high), 1.0, 0.0).astype(BF)
            lanes = [slice(h // 2 * PAIR, (h // 2 + 1) * PAIR) for h in range(2 * pairs)]
            scores = [nt(qm[h, here, :], k[there, lanes[h]]) for h in range(2 * pairs)]
            probs = [jnp.exp(s).astype(BF) * seen for s in scores]
            return tuple(
                total + nn(p, v_ext[h, there, :]) for h, (total, p) in enumerate(zip(totals, probs))
            )

        totals = lax.fori_loop(
            span[0, i], span[1, i], step, tuple(jnp.zeros((qb, PAIR), F32) for _ in range(2 * pairs))
        )
        for pair in range(pairs):
            t0, t1 = totals[2 * pair], totals[2 * pair + 1]
            lane = lax.broadcasted_iota(jnp.int32, t0.shape, 1) // HEAD
            top = jnp.where(lane == 0, t0, t1)
            sums = pltpu.roll(jnp.where(lane == 0, t1, t0), HEAD, 1)
            inv = 1.0 / sums
            high_part, low_part = halves(top * inv)
            mixed[here, pair * PAIR : (pair + 1) * PAIR] = high_part
            rest[here, pair * PAIR : (pair + 1) * PAIR] = low_part
            turned = jnp.transpose(inv)
            inverse[0, 2 * pair : 2 * pair + 1, here] = turned[0:1, :]
            inverse[0, 2 * pair + 1 : 2 * pair + 2, here] = turned[HEAD : HEAD + 1, :]
        return 0

    lax.fori_loop(0, count // qb, one_block, 0)


def attn_fwd_call(span, q, k, v, start, end, qb=256, kb=256):
    count, width = q.shape
    lanes = GROUP * HEAD
    column = pl.BlockSpec((count, lanes), lambda g, s: (0, g))
    edge = pl.BlockSpec((count, 1), lambda g, s: (0, 0))
    heads = width // HEAD
    return launch(
        functools.partial(attn_fwd_kernel, qb=qb, kb=kb),
        grid_spec=dict(
            num_scalar_prefetch=1,
            grid=(heads // GROUP,),
            in_specs=[column, column, column, edge, edge],
            out_specs=[column, column, pl.BlockSpec((1, 8, count), lambda g, s: (g, 0, 0))],
            scratch_shapes=[
                pltpu.VMEM((GROUP, count, PAIR), BF),
                pltpu.VMEM((GROUP, count, PAIR), BF),
            ],
        ),
        out_shape=[
            jax.ShapeDtypeStruct((count, width), BF),
            jax.ShapeDtypeStruct((count, width), BF),
            jax.ShapeDtypeStruct((heads // GROUP, 8, count), F32),
        ],
        compiler_params=params(),
        cost_estimate=cost(16 * count * count * heads * HEAD, 8 * count * width, heads * count * count),
        name="attention_forward",
    )(span, q, k, v, start, end)


def attn_bwd_kernel(
    span, q, k, v, do, start, end, inverse, delta, rq, rk, scale,
    dq, dk, dv, scale_grad, qm, dom, kt, dq_acc, dk_acc, dv_acc, *, qb, kb,
):
    count = q.shape[0]
    pairs = q.shape[1] // PAIR
    for pair in range(pairs):
        lanes = slice(pair * PAIR, (pair + 1) * PAIR)
        for at in range(0, count, qb):
            for h in range(2):
                put = slice(2 * at + h * qb, 2 * at + (h + 1) * qb)
                qm[pair, put, :] = lane_masked(q[at : at + qb, lanes], h)
                dom[pair, put, :] = lane_masked(do[at : at + qb, lanes], h)
    kt[...] = jnp.transpose(k[...])
    dk_acc[...] = jnp.zeros_like(dk_acc)
    dv_acc[...] = jnp.zeros_like(dv_acc)

    def one_block(i, total):
        here = pl.ds(pl.multiple_of(i * qb, qb), qb)
        twice = pl.ds(pl.multiple_of(i * (2 * qb), 2 * qb), 2 * qb)
        one = [pl.ds(pl.multiple_of(i * (2 * qb) + h * qb, qb), qb) for h in range(2)]
        low, high = start[0:1, here], end[0:1, here]
        dq_acc[...] = jnp.zeros_like(dq_acc)

        def step(j, _):
            at = pl.multiple_of(j * kb, kb)
            there = pl.ds(at, kb)
            place = at + lax.broadcasted_iota(jnp.int32, (kb, qb), 0)
            seen = jnp.where((place >= low) & (place < high), 1.0, 0.0).astype(BF)
            for pair in range(pairs):
                lanes = slice(pair * PAIR, (pair + 1) * PAIR)
                heads = (2 * pair, 2 * pair + 1)
                s = [nt(k[there, lanes], qm[pair, x, :]) for x in one]
                dp = [nt(v[there, lanes], dom[pair, x, :]) for x in one]
                p = [jnp.exp(x) * inverse[0, h : h + 1, here] for x, h in zip(s, heads)]
                ds = [x * (y - delta[0, h : h + 1, here]) for x, y, h in zip(p, dp, heads)]
                p = [x.astype(BF) * seen for x in p]
                ds = [x.astype(BF) * seen for x in ds]
                dv_acc[there, lanes] += nn(jnp.concatenate(p, axis=1), dom[pair, twice, :])
                dk_acc[there, lanes] += nn(jnp.concatenate(ds, axis=1), qm[pair, twice, :])
                for x, h in zip(ds, heads):
                    rows = slice(h * HEAD, (h + 1) * HEAD)
                    dq_acc[rows, :] += nn(kt[rows, there], x)
            return 0

        lax.fori_loop(span[0, i], span[1, i], step, 0)
        g = jnp.transpose(dq_acc[...])
        sc = scale[0:1, :]
        unit = q[here, :].astype(F32) / sc
        inner = head_sums(unit * g)
        dq[here, :] = (sc * rq[here, :].astype(F32) * (g - unit * inner)).astype(BF)
        return total + jnp.sum(inner, axis=0, keepdims=True)

    total = lax.fori_loop(0, count // qb, one_block, jnp.zeros((1, q.shape[1]), F32))
    scale_grad[...] = jnp.broadcast_to(total, scale_grad.shape)
    for at in range(0, count, qb):
        here = pl.ds(at, qb)
        g = dk_acc[here, :]
        unit = k[here, :].astype(F32)
        dk[here, :] = (rk[here, :].astype(F32) * (g - unit * head_sums(unit * g))).astype(BF)
    dv[...] = dv_acc[...].astype(BF)


def attn_bwd_call(
    span, q, k, v, do, start, end, inverse, delta, rq, rk, scale_lanes, first, groups, qb=256, kb=256
):
    count, width = q.shape
    lanes = GROUP * HEAD
    column = pl.BlockSpec((count, lanes), lambda g, s: (0, first + g))
    edge = pl.BlockSpec((1, count), lambda g, s: (0, 0))
    row = pl.BlockSpec((1, 8, count), lambda g, s: (first + g, 0, 0))
    out = pl.BlockSpec((count, lanes), lambda g, s: (0, g))
    heads = groups * GROUP
    return launch(
        functools.partial(attn_bwd_kernel, qb=qb, kb=kb),
        grid_spec=dict(
            num_scalar_prefetch=1,
            grid=(groups,),
            in_specs=[column] * 4
            + [edge] * 2
            + [row] * 2
            + [column] * 2
            + [pl.BlockSpec((8, lanes), lambda g, s: (0, first + g))],
            out_specs=[out] * 3 + [pl.BlockSpec((8, lanes), lambda g, s: (0, g))],
            scratch_shapes=[pltpu.VMEM((GROUP // 2, 2 * count, PAIR), BF)] * 2
            + [pltpu.VMEM((lanes, count), BF), pltpu.VMEM((lanes, qb), F32)]
            + [pltpu.VMEM((count, lanes), F32)] * 2,
        ),
        out_shape=[jax.ShapeDtypeStruct((count, groups * lanes), BF)] * 3
        + [jax.ShapeDtypeStruct((8, groups * lanes), F32)],
        compiler_params=params(),
        cost_estimate=cost(40 * count * count * heads * HEAD, 18 * count * heads * HEAD, heads * count * count),
        name="attention_backward",
    )(span, q, k, v, do, start, end, inverse, delta, rq, rk, scale_lanes)


def proj_kernel(tokens, mixed, cotangent, member, modulation, weight, after, branch, hidden, down):
    width = tokens.shape[1]
    part = lambda i: nn(member[...], modulation[:, i * width : (i + 1) * width])
    out = nn(mixed[...], weight[...])
    total = tokens[...].astype(F32) + part(0) * out
    after[...] = total
    branch[...] = out.astype(BF)
    unit, _ = centre(total)
    hidden[...] = (unit * (1.0 + part(3)) + part(5)).astype(BF)
    down[...] = (cotangent[...].astype(F32) * part(1)).astype(BF)


def proj_call(tokens, mixed, cotangent, member, modulation, weight, rows=256):
    count, width = tokens.shape
    some = pl.BlockSpec((rows, width), lambda s: (s, 0))
    whole = lambda x: pl.BlockSpec(x.shape, lambda s: (0, 0))
    return launch(
        proj_kernel,
        grid=(count // rows,),
        in_specs=[
            some,
            some,
            some,
            pl.BlockSpec((rows, member.shape[1]), lambda s: (s, 0)),
            whole(modulation),
            pl.BlockSpec((width, width), lambda s: (0, 3)),
        ],
        out_specs=[some] * 4,
        out_shape=[
            jax.ShapeDtypeStruct((count, width), d) for d in (F32, BF, BF, BF)
        ],
        compiler_params=params(),
        cost_estimate=cost(2 * count * width * width, 16 * count * width),
        name="projection",
    )(tokens, mixed, cotangent, member, modulation, weight)


def split_blocks(odd, result, rows, kept, sent):
    result = result.astype(BF)
    for at in range(0, result.shape[0], 2 * rows):
        even_part = result[at : at + rows]
        odd_part = result[at + rows : at + 2 * rows]
        put = slice(at // 2, at // 2 + rows)
        kept[put, :] = jnp.where(odd, odd_part, even_part)
        sent[put, :] = jnp.where(odd, even_part, odd_part)


def mlp_kernel(core, hidden, down, up_w, down_w, *refs, rows, own):
    split = len(refs) == 9
    mlp, back = refs[:2]
    grads = refs[2:-3]
    active, grad, turned = refs[-3:]
    step = pl.program_id(0)
    odd = core[1] == 1

    @pl.when(step == 0)
    def _():
        mlp[...] = jnp.zeros_like(mlp)
        back[...] = jnp.zeros_like(back)
        turned[...] = jnp.transpose(hidden[...])

    for at in range(0, hidden.shape[0], rows):
        here = pl.ds(at, rows)
        e = nn(hidden[here, :], up_w[...])
        da = nt(down[here, :], down_w[...])
        square = e * e
        t = jnp.tanh(e * (GELU_A + GELU_A * GELU_B * square))
        half = 0.5 + 0.5 * t
        act = (e * half).astype(BF)
        slope = half + e * (0.5 - 0.5 * t * t) * (GELU_A + 3.0 * GELU_A * GELU_B * square)
        de = (da * slope).astype(BF)
        active[here, :] = act
        grad[here, :] = de
        mlp[here, :] += nn(act, down_w[...])
        back[here, :] += nt(de, up_w[...])
    if split:
        split_blocks(odd, tn(active[...], down[...]), own, grads[2], grads[3])
        split_blocks(odd, nn(turned[...], grad[...]), own, grads[0], grads[1])
    else:
        grads[1][...] = tn(active[...], down[...]).astype(BF)
        grads[0][...] = nn(turned[...], grad[...]).astype(BF)


def mlp_call(core, hidden, down, packed, own, split, first, count_of, block=512, rows=256):
    count, width = hidden.shape
    units = packed.shape[1] // 2
    per = width // block
    whole = pl.BlockSpec((count, width), lambda s, c: (0, 0))
    first_up, first_down = first * per, units // width + first
    kept = 2 if split else 1
    copies = 2 if split else 1
    wide = pl.BlockSpec((width // kept, block), lambda s, c: (0, s))
    tall = pl.BlockSpec((block // kept, width), lambda s, c: (s % per, s // per))
    return launch(
        functools.partial(mlp_kernel, rows=rows, own=own),
        grid_spec=dict(
            num_scalar_prefetch=1,
            grid=(count_of * per,),
            in_specs=[
                whole,
                whole,
                pl.BlockSpec((width, block), lambda s, c: (0, first_up + s)),
                pl.BlockSpec((block, width), lambda s, c: (s % per, first_down + s // per)),
            ],
            out_specs=[whole, whole] + [wide] * copies + [tall] * copies,
            scratch_shapes=[
                pltpu.VMEM((count, block), BF),
                pltpu.VMEM((count, block), BF),
                pltpu.VMEM((width, count), BF),
            ],
        ),
        out_shape=[jax.ShapeDtypeStruct((count, width), F32)] * 2
        + [jax.ShapeDtypeStruct((width // kept, count_of * width), BF)] * (2 * copies),
        compiler_params=params(),
        cost_estimate=cost(12 * count * width * width * count_of, 20 * count * width),
        name="feed_forward",
    )(core, hidden, down, packed, packed)


def item_sums(turned, x):
    high, low = halves(x)
    return nn(turned, high) + nn(turned, low)


def norm_back(unit, rstd, w):
    inner = jnp.mean(w * unit, axis=-1, keepdims=True)
    return (w - jnp.mean(w, axis=-1, keepdims=True) - unit * inner) * rstd


def middle_kernel(
    mlp_sum, back, after, cotangent, branch, mixed, rest, member, turned, modulation, weight,
    output, grad_in, branch_grad, mixed_grad, delta, sums,
):
    width = after.shape[1]
    part = lambda i: nn(member[...], modulation[:, i * width : (i + 1) * width])
    upstream = cotangent[...].astype(F32)
    v = after[...]
    mlp = mlp_sum[...]
    output[...] = (v + part(1) * mlp).astype(BF)
    g = back[...]
    unit, rstd = centre(v)
    total = upstream + norm_back(unit, rstd, g * (1.0 + part(3)))
    grad_in[...] = total
    down = (total * part(0)).astype(BF)
    branch_grad[...] = down
    mg = nt(down, weight[...]).astype(BF)
    mixed_grad[...] = mg
    product = mg.astype(F32) * (mixed[...].astype(F32) + rest[...].astype(F32))
    head = lax.broadcasted_iota(jnp.int32, (32, width), 0)
    lane = lax.broadcasted_iota(jnp.int32, (32, width), 1) // HEAD
    wanted = GROUP * (head // 8) + head % 8
    pick = jnp.where((wanted == lane) & (head % 8 < GROUP), 1.0, 0.0).astype(BF)
    high, low = halves(product)
    delta[...] = nt(pick, high) + nt(pick, low)

    @pl.when(pl.program_id(0) == 0)
    def _():
        sums[...] = jnp.zeros_like(sums)

    for i, x in enumerate((total * branch[...].astype(F32), upstream * mlp, g * unit, g)):
        sums[:, i * width : (i + 1) * width] += item_sums(turned[...], x)


def middle_call(mlp, back, after, cotangent, branch, mixed, rest, member, turned, modulation, weight, rows=256):
    count, width = after.shape
    some = pl.BlockSpec((rows, width), lambda s: (s, 0))
    whole = lambda x: pl.BlockSpec(x.shape, lambda s: (0, 0))
    items = turned.shape[0]
    heads = 8 * (width // HEAD // GROUP)
    return launch(
        middle_kernel,
        grid=(count // rows,),
        in_specs=[some] * 7
        + [
            pl.BlockSpec((rows, member.shape[1]), lambda s: (s, 0)),
            pl.BlockSpec((items, rows), lambda s: (0, s)),
            whole(modulation),
            pl.BlockSpec((width, width), lambda s: (0, 3)),
        ],
        out_specs=[some] * 4
        + [
            pl.BlockSpec((heads, rows), lambda s: (0, s)),
            pl.BlockSpec((items, 4 * width), lambda s: (0, 0)),
        ],
        out_shape=[jax.ShapeDtypeStruct((count, width), d) for d in (BF, F32, BF, BF)]
        + [
            jax.ShapeDtypeStruct((heads, count), F32),
            jax.ShapeDtypeStruct((items, 4 * width), F32),
        ],
        compiler_params=params(),
        cost_estimate=cost(4 * count * width * width, 30 * count * width),
        name="middle",
    )(mlp, back, after, cotangent, branch, mixed, rest, member, turned, modulation, weight)


def first_kernel(*refs):
    *parts, weight, tokens, grad_in, member, turned, modulation, tokens_grad, sums = refs
    width = tokens.shape[1]
    g, at = 0.0, 0
    for part in parts:
        g = g + nt(part[...], weight[:, at : at + part.shape[1]])
        at += part.shape[1]
    unit, rstd = centre(tokens[...].astype(F32))
    sc = nn(member[...], modulation[:, 2 * width : 3 * width])
    tokens_grad[...] = (grad_in[...] + norm_back(unit, rstd, g * (1.0 + sc))).astype(BF)

    @pl.when(pl.program_id(0) == 0)
    def _():
        sums[...] = jnp.zeros_like(sums)

    for i, x in enumerate((g * unit, g)):
        sums[:, i * width : (i + 1) * width] += item_sums(turned[...], x)


def first_call(parts, weight, tokens, grad_in, member, turned, modulation, rows=256):
    count, width = tokens.shape
    some = pl.BlockSpec((rows, width), lambda s: (s, 0))
    whole = lambda x: pl.BlockSpec(x.shape, lambda s: (0, 0))
    items = turned.shape[0]
    return launch(
        first_kernel,
        grid=(count // rows,),
        in_specs=[pl.BlockSpec((rows, p.shape[1]), lambda s: (s, 0)) for p in parts]
        + [
            pl.BlockSpec((width, 3 * width), lambda s: (0, 0)),
            some,
            some,
            pl.BlockSpec((rows, member.shape[1]), lambda s: (s, 0)),
            pl.BlockSpec((items, rows), lambda s: (0, s)),
            whole(modulation),
        ],
        out_specs=[some, pl.BlockSpec((items, 2 * width), lambda s: (0, 0))],
        out_shape=[
            jax.ShapeDtypeStruct((count, width), BF),
            jax.ShapeDtypeStruct((items, 2 * width), F32),
        ],
        compiler_params=params(),
        cost_estimate=cost(6 * count * width * width, 18 * count * width),
        name="first_norm_backward",
    )(*parts, weight, tokens, grad_in, member, turned, modulation)


def weight_grad_kernel(core, *refs, rows, starts):
    jobs = len(starts) - 1
    xs, ys = refs[:jobs], refs[jobs : jobs + starts[-1][1]]
    outs, turned = refs[jobs + starts[-1][1] : -1], refs[-1]
    step = pl.program_id(0)
    for job in range(jobs):

        @pl.when(step == starts[job][0])
        def _():
            turned[...] = jnp.transpose(xs[job][...])

        (begin, first), (end, last) = starts[job], starts[job + 1]
        per = (end - begin) // (last - first)
        for which in range(first, last):
            at = begin + (which - first) * per

            @pl.when((step >= at) & (step < at + per))
            def _():
                result = nn(turned[...], ys[which][...])
                if len(outs) == 2:
                    split_blocks(core[1] == 1, result, rows, outs[0], outs[1])
                else:
                    outs[0][...] = result.astype(BF)


def weight_grad_call(core, jobs, rows, split, block=512):
    count, width = jobs[0][0].shape
    starts, specs = [(0, 0)], []
    for _, ys in jobs:
        begin, number = starts[-1]
        for y in ys:
            per = y.shape[1] // block
            specs.append(
                pl.BlockSpec(
                    (count, block), lambda s, c, at=begin, per=per: (0, jnp.clip(s - at, 0, per - 1))
                )
            )
            begin, number = begin + per, number + 1
        starts.append((begin, number))
    steps = starts[-1][0]
    columns = steps * block
    wide = lambda n: pl.BlockSpec((n, block), lambda s, c: (0, s))
    shapes = [(width // 2, columns)] * 2 if split else [(width, columns)]
    return launch(
        functools.partial(weight_grad_kernel, rows=rows, starts=tuple(starts)),
        grid_spec=dict(
            num_scalar_prefetch=1,
            grid=(steps,),
            in_specs=[pl.BlockSpec((count, width), lambda s, c: (0, 0)) for _ in jobs] + specs,
            out_specs=[wide(shape[0]) for shape in shapes],
            scratch_shapes=[pltpu.VMEM((width, count), BF)],
        ),
        out_shape=[jax.ShapeDtypeStruct(s, BF) for s in shapes],
        compiler_params=params(),
        cost_estimate=cost(2 * count * width * columns, 4 * count * columns),
        name="weight_grad",
    )(core, *[x for x, _ in jobs], *[y for _, ys in jobs for y in ys])


BOTH = ("wide", "narrow")
LENGTH_TABLE = np.array([0, 1, 5, 14, 30, 55, 91, 155, 255, 424, 680], np.int32)
SCALE_BOUNDS = np.array([1, 5, 14, 30, 55, 91, 155, 255, 424], np.int32)


def bit_count(size):
    return size.bit_length() - 1


def flip(values, axis, size, bit):
    return lax.ppermute(values, axis, [(i, i ^ (1 << bit)) for i in range(size)])


def chip_order(wide, turn):
    outer = list(range(bit_count(wide)))
    turning, last = outer[:-1], outer[-1:]
    turn = turn % max(1, len(turning))
    return turning[turn:] + turning[:turn] + last


def halving_kernel(flags, *refs):
    number = len(refs) // 6
    inputs, outs = refs[: 4 * number], refs[4 * number :]
    for i in range(number):
        kept_here, got_here, kept_there, got_there = inputs[4 * i : 4 * i + 4]
        kept, sent = outs[2 * i : 2 * i + 2]
        add = lambda x, y: (x[:, 0].astype(F32) + y[:, 0].astype(F32)).astype(BF)
        sent[...] = add(kept_there, got_there)
        kept[...] = add(kept_here, got_here)


class Chain:
    def __init__(self, kept, got, sizes, turn, columns=None, index=0):
        self.kept, self.got, self.index = kept, got, index
        self.columns, self.wide = columns or kept.shape[1], sizes["wide"]
        self.dims = list(reversed(range(bit_count(self.wide))))
        self.order = chip_order(self.wide, turn)


def finish_kernel(*refs, blocks):
    number = len(refs) // 3
    for index, (kept, got, out) in enumerate(
        zip(refs[:number], refs[number : 2 * number], refs[2 * number :])
    ):
        total = kept[...].astype(F32) + got[...].astype(F32)
        if not blocks:
            out[...] = total
            continue
        own = total.shape[0]
        width = total.shape[1] // blocks
        if index == 0:
            for owner in range(width // own):
                at = [i * width + owner * own for i in range(blocks)]
                out[:, owner * own * blocks : (owner + 1) * own * blocks] = jnp.concatenate(
                    [total[:, x : x + own] for x in at], axis=1
                )
        else:
            for i in range(blocks):
                out[i * own : (i + 1) * own, :] = total[:, i * width : (i + 1) * width]


def finish(chains, blocks=0):
    whole = lambda x: pl.BlockSpec(x.shape, lambda s: (0, 0))
    kept, got = [c.kept for c in chains], [c.got for c in chains]
    shapes = [jax.ShapeDtypeStruct(x.shape, F32) for x in kept]
    if blocks:
        rows, columns = shapes[1].shape
        shapes[1] = jax.ShapeDtypeStruct((rows * blocks, columns // blocks), F32)
    size = sum(x.size for x in kept)
    return launch(
        functools.partial(finish_kernel, blocks=blocks),
        grid=(1,),
        in_specs=[whole(x) for x in (*kept, *got)],
        out_specs=[whole(x) for x in shapes],
        out_shape=shapes,
        compiler_params=params(),
        cost_estimate=cost(size, 8 * size),
        name="last_sum",
    )(*kept, *got)


def halve(flags, chains, steps):
    specs, args, outs, shapes = [], [], [], []
    for chain in chains:
        bit = chain.order.pop(0)
        at = chain.dims.index(bit)
        chain.dims.pop(at)
        chain.bit = bit
        lead, rows = 2**at, chain.kept.shape[0] // 2 ** (at + 1)
        over = min(lead, steps)
        within = steps // over
        block = (lead // over, rows // within, chain.columns)
        which, index = bit, chain.index
        spec = lambda flip: pl.BlockSpec(
            (block[0], 1, block[1], block[2]),
            lambda s, b, within=within, which=which, index=index: (
                s // within,
                b[2 + which] ^ flip,
                s % within,
                index,
            ),
        )
        kept, got = (x.reshape(lead, 2, rows, -1) for x in (chain.kept, chain.got))
        specs += [spec(0), spec(0), spec(1), spec(1)]
        args += [kept, got, kept, got]
        outs += [pl.BlockSpec(block, lambda s, b, within=within: (s // within, s % within, 0))] * 2
        shapes += [jax.ShapeDtypeStruct((lead, rows, chain.columns), BF)] * 2
    size = sum(int(np.prod(x.shape)) for x in shapes)
    result = launch(
        halving_kernel,
        grid_spec=dict(num_scalar_prefetch=1, grid=(steps,), in_specs=specs, out_specs=outs),
        out_shape=shapes,
        compiler_params=params(),
        cost_estimate=cost(size, 6 * size),
        name="halving_sum",
    )(flags, *args)
    for i, chain in enumerate(chains):
        flat = lambda x: x.reshape(-1, chain.columns)
        chain.kept, chain.index = flat(result[2 * i]), 0
        chain.got = flip(flat(result[2 * i + 1]), "wide", chain.wide, chain.bit)
    return result[0]


def land_kernel(*refs):
    number = len(refs) // 3
    for block, got, out in zip(refs[:number], refs[number : 2 * number], refs[2 * number :]):
        half = block.shape[0]
        out[:half] = block[...]
        out[half:] = got[...]


def land(moves):
    blocks, gots = [m.block for m in moves], [m.got for m in moves]
    shapes = [(2 * x.shape[0],) + x.shape[1:] for x in blocks]
    whole = lambda shape: pl.BlockSpec(shape, lambda s: (0, 0, 0))
    joined = launch(
        land_kernel,
        grid=(1,),
        in_specs=[whole(x.shape) for x in (*blocks, *gots)],
        out_specs=[whole(x) for x in shapes],
        out_shape=[jax.ShapeDtypeStruct(x, BF) for x in shapes],
        compiler_params=params(),
        cost_estimate=cost(0, 4 * sum(int(np.prod(x)) for x in shapes)),
        name="land",
    )(*blocks, *gots)
    for move, block in zip(moves, joined):
        move.block = block


class Gather:
    def __init__(self, block, sizes, order):
        self.block, self.sizes, self.order = block, sizes, list(order) + [None]

    def send(self):
        bit = self.order.pop(0)
        axis = "narrow" if bit is None else "wide"
        self.got = flip(self.block, axis, self.sizes[axis], 0 if bit is None else bit)


    def halves(self):
        return [self.block, self.got]


def owner_sum(x, axis):
    return lax.psum_scatter(x, axis, scatter_dimension=0, tiled=True)


def relative_place(owner, me, order):
    apart = owner ^ me
    place = (apart & 1) << len(order)
    for at, bit in enumerate(order):
        place = place | (((apart >> (bit + 1)) & 1) << at)
    return place


def layout(level_row, count):
    lengths = jnp.sum(
        jnp.where(
            level_row[:, None] == jnp.arange(11, dtype=jnp.int32)[None, :],
            jnp.asarray(LENGTH_TABLE)[None, :],
            0,
        ),
        axis=1,
    ).astype(jnp.int32)
    starts = jnp.cumsum(lengths) - lengths
    position = jnp.arange(count, dtype=jnp.int32)[None, :]
    inside = (position >= starts[:, None]) & (position < (starts + lengths)[:, None])
    inside_int = inside.astype(jnp.int32)
    covered = jnp.sum(inside_int, axis=0, keepdims=True) > 0
    first = jnp.where(covered, jnp.sum(inside_int * starts[:, None], axis=0, keepdims=True), position)
    offset = position - first
    length = jnp.full_like(position, int(LENGTH_TABLE[1]))
    for low, high in zip(LENGTH_TABLE[1:-1], LENGTH_TABLE[2:]):
        length = jnp.where(offset >= int(low), int(high), length)
    return inside, first, first + jnp.where(covered, length, 1)


def per_device(
    tokens,
    class_table,
    ada_weight,
    qkv_weight,
    proj_weight,
    head_scale,
    fc1_weight,
    fc2_weight,
    levels,
    labels,
    cotangent,
):
    count, width = tokens.shape
    head_count = head_scale.shape[0]
    sizes = {"wide": lax.axis_size("wide"), "narrow": lax.axis_size("narrow")}
    devices = sizes["wide"] * sizes["narrow"]
    me = lax.axis_index("wide") * sizes["narrow"] + lax.axis_index("narrow")
    chip = lax.axis_index("wide")
    flags = [me, lax.axis_index("narrow") & 1]
    flags += [(chip >> i) & 1 for i in range(bit_count(sizes["wide"]))]
    flags = jnp.stack(flags).astype(jnp.int32)
    slots = labels.shape[1]
    rows = 8
    own = proj_weight.shape[0]
    blocks = fc2_weight.shape[0] // own
    paired = own % 32 == 0 and sizes["narrow"] == 2

    label_block = jnp.zeros((own, PAIR), BF)
    label_block = label_block.at[0, :slots].set((labels[0] // 256).astype(BF))
    label_block = label_block.at[1, :slots].set((labels[0] % 256).astype(BF))
    table_shard = jnp.concatenate([class_table, label_block], axis=1)
    up_shard = fc1_weight.reshape(own, devices, blocks, own).transpose(0, 2, 1, 3)
    feed_shard = jnp.concatenate(
        [up_shard.reshape(own, -1)]
        + [fc2_weight[i * own : (i + 1) * own] for i in range(blocks)],
        axis=1,
    )
    ada_columns = lax.all_to_all(ada_weight, BOTH, 1, 0, tiled=True)
    if paired:
        orders = [chip_order(sizes["wide"], turn)[::-1] for turn in (0, 1)]
        orders.append([orders[0][0]] + orders[0][1:])
        stages = len(orders[0])
        both = Gather(jnp.concatenate([table_shard, qkv_weight, proj_weight], axis=1)[None], sizes, orders[0][:1])
        both.send()
        land([both])
        cuts = (0, width + PAIR, 3 * width + PAIR, 5 * width + PAIR)
        table_move, *moves = (
            Gather(both.block[:, :, low:high], sizes, order[1:])
            for low, high, order in zip(cuts, cuts[1:], orders)
        )
        table_move.send()
        land([table_move])
        for step in range(1, stages):
            for move in (table_move, *moves):
                move.send()
            if step == 1:
                await_all(ada_columns)
            if step < stages - 1:
                land([table_move, *moves])
            if step == stages - 2:
                feed_shard, table_move.block = lax.optimization_barrier((feed_shard, table_move.block))
        tables = [h.reshape(-1, width + PAIR) for h in table_move.halves()]
    else:
        orders = [()]
        tables = [lax.all_gather(table_shard, BOTH, axis=0, tiled=True)]
    class_vec, lifted, slot_labels, modulation_columns = modulation_call(
        flags, tables, ada_columns, orders[0], slots, rows, own
    )
    if paired:
        await_all(done[0])
        land(moves)
        for move in moves:
            move.send()
        weights = [[h.reshape(width // 2, -1) for h in move.halves()] for move in moves]
        owners = jnp.arange(devices, dtype=jnp.int32)
        places = jnp.stack([relative_place(owners, me, o) for o in orders[1:]]).astype(jnp.int32)
    else:
        weights = [
            (lax.all_gather(jnp.concatenate([qkv_weight, proj_weight], axis=1), BOTH, axis=0, tiled=True),)
        ]
        places = jnp.zeros((1, devices), jnp.int32)
    feed_weight = lax.all_gather(feed_shard, BOTH, axis=0, tiled=True)

    modulation = lax.all_to_all(modulation_columns, BOTH, 0, 1, tiled=True)
    high = lax.reduce_precision(modulation, 8, 7)
    middle = lax.reduce_precision(modulation - high, 8, 7)
    low = modulation - high - middle
    terms = jnp.pad(jnp.concatenate([high, middle, low]), ((0, 8), (0, 0))).astype(BF)

    inside, first, last = layout(levels[0], count)
    turned = jnp.pad(inside.astype(BF), ((0, 16 - slots), (0, 0)))
    inside = jnp.pad(inside.astype(BF), ((0, rows - slots), (0, 0)))
    member = jnp.concatenate([inside] * 3 + [jnp.zeros_like(inside)]).T
    tile = 256
    span = jnp.concatenate(
        [first[:, ::tile] // tile, (last[:, tile - 1 :: tile] + tile - 1) // tile]
    ).astype(jnp.int32)
    scale_lanes = jnp.broadcast_to(jnp.repeat(head_scale, width // head_count)[None], (8, width))

    hidden_one, q, k, v, rq, rk, ordered = qkv_call(
        places, tokens, member, terms, weights, scale_lanes
    )
    mixed, rest, inverse = attn_fwd_call(
        span, q, k, v, first.reshape(count, 1), last.reshape(count, 1), tile, tile
    )
    after, branch, hidden_two, down = proj_call(
        tokens, mixed, cotangent, member, terms, ordered
    )
    mlp, back, *grads = mlp_call(flags, hidden_two, down, feed_weight, own, paired, 0, blocks)
    swap = lambda x: flip(x, "narrow", sizes["narrow"], 0)
    if paired:
        up, down = (
            Chain(kept, swap(sent), sizes, turn)
            for turn, kept, sent in ((0, *grads[:2]), (1, *grads[2:]))
        )
    output, grad_in, branch_grad, mixed_grad, delta, sums = middle_call(
        mlp, back, after, cotangent, branch, mixed, rest, member, turned, terms, ordered
    )
    early = jnp.pad(sums[:slots], ((0, rows - slots), (0, 0))).astype(BF)
    early = lax.all_gather(early, BOTH, axis=0, tiled=True)
    if paired:
        await_all(done[0])
        halve(flags, [up, down], 8)
        await_all(done[0])
    else:
        feed = owner_sum(jnp.concatenate(grads, axis=1), BOTH).astype(F32)
        units = blocks * width
        fc1_grad = feed[:, :units].reshape(own, blocks, devices, own).transpose(0, 2, 1, 3)
        fc1_grad = fc1_grad.reshape(own, -1)
        fc2_grad = jnp.concatenate(
            [feed[:, units + i * width : units + (i + 1) * width] for i in range(blocks)]
        )
    *heads, scale_part = attn_bwd_call(
        span, q, k, v, mixed_grad, first, last, inverse, delta.reshape(-1, 8, count), rq, rk,
        scale_lanes, 0, head_count // GROUP, tile, tile,
    )
    if paired:
        await_all(done[0])
        halve(flags, [up, down], 4)
        await_all(done[0])
    qkv_parts = weight_grad_call(flags, [(hidden_one, heads)], own, paired)
    if paired:
        qkv_got = swap(qkv_parts[1])
        await_all(done[0])
    proj_parts = weight_grad_call(flags, [(mixed, [branch_grad])], own, paired)
    if paired:
        qkv = [Chain(qkv_parts[0], qkv_got, sizes, i, 3 * width // 2, i) for i in range(2)]
        proj = Chain(proj_parts[0], swap(proj_parts[1]), sizes, 2)
        await_all(done[0])
        halve(flags, [*qkv, proj], 4)
        await_all(done[0])
    else:
        qkv_grad = owner_sum(qkv_parts[0], BOTH).astype(F32)
        proj_grad = owner_sum(proj_parts[0], BOTH).astype(F32)
    tokens_grad, first_sums = first_call(
        heads, ordered, tokens, grad_in, member, turned, terms
    )
    late = jnp.pad(first_sums[:slots], ((0, rows - slots), (0, 0))).astype(BF)
    own_width = width // devices
    scale_sums = scale_part[0].reshape(head_count, HEAD)[:, 0]
    head_rows = -(-head_count // own_width)
    head_rows += -head_rows % 8
    scale_rows = jnp.pad(scale_sums, (0, head_rows * own_width - head_count)).reshape(
        head_rows, own_width
    )
    if paired:
        move = Gather(late[None], sizes, orders[0])
        move.send()
        await_all(done[0])
        halve(flags, [*qkv, proj, up, down], 2)
        for step in range(stages):
            await_all(done[0])
            land([move])
            move.send()
            if step == 2:
                await_all(done[0])
                halve(flags, [*qkv, proj, up, down], 2)
        lates = [h.reshape(-1, h.shape[-1]) for h in move.halves()]
        await_all(done[0])
        ada_grad, outgoing = ada_call(
            flags, early, lates, lifted, class_vec, slot_labels, ada_weight, scale_rows, devices,
            orders[0],
        )
        await_all(done[0])
        halve(flags, [*qkv, proj], 2)
        await_all(done[0])
        fc1_grad, fc2_grad = finish([up, down], blocks)
        await_all(done[0])
        *parts, proj_grad = finish([*qkv, proj])
        qkv_grad = jnp.concatenate(parts, axis=1)
    else:
        late = lax.all_gather(late, BOTH, axis=0, tiled=True)
        cut = lambda x, i: x[:, i * width : (i + 1) * width]
        item_grad = jnp.concatenate(
            [cut(early, 0), cut(early, 1), cut(late, 0), cut(early, 2), cut(late, 1), cut(early, 3)],
            axis=1,
        )
        ada_grad = tn(lax.dynamic_slice_in_dim(lifted, me * own_width, own_width, 1), item_grad)
        own_vec = lax.dynamic_slice_in_dim(class_vec, me * own_width, own_width, 1).astype(F32)
        _, silu_pull = jax.vjp(jax.nn.silu, own_vec)
        class_grad = silu_pull(nt(item_grad, ada_weight))[0]
        hot = (slot_labels[:, :1] == jnp.arange(devices * own, dtype=jnp.int32)[None, :]).astype(F32)
        table_columns = jnp.einsum("ic,id->cd", hot, class_grad, precision=lax.Precision.HIGHEST)
        outgoing = jnp.concatenate(
            [
                table_columns.reshape(devices, own, own_width),
                jnp.broadcast_to(scale_rows[None], (devices,) + scale_rows.shape),
            ],
            axis=1,
        )
    outgoing = outgoing.reshape(-1, own_width)
    incoming = lax.all_to_all(outgoing, BOTH, 0, 1, tiled=True)
    table_grad = incoming[:own]
    scale_grad = jnp.sum(incoming[own:].reshape(head_rows, devices, own_width), axis=1).reshape(-1)[
        :head_count
    ]
    units = blocks * width
    return (
        output,
        tokens_grad,
        table_grad,
        ada_grad,
        qkv_grad,
        proj_grad,
        scale_grad,
        fc1_grad,
        fc2_grad,
    )


def solution(mesh):
    rows = P(BOTH, None)
    in_specs = (rows,) * 5 + (P(),) + (rows,) * 5
    out_specs = (rows,) * 6 + (P(),) + (rows,) * 2
    return jax.shard_map(
        per_device, mesh=mesh, in_specs=in_specs, out_specs=out_specs, check_vma=False
    )
```

```python
import functools
import jax
import jax.numpy as jnp
import numpy as np
from jax import lax
from jax.experimental import pallas as pl
from jax.experimental.pallas import tpu as pltpu
from jax.sharding import PartitionSpec as P

NORM_EPS = 1e-06
BF, F32 = jnp.bfloat16, jnp.float32
VMEM_BYTES = 60 * 2**20
HEAD = 64
PAIR = 2 * HEAD
GROUP = 4
GELU_A, GELU_B = 0.7978845608028654, 0.044715


def nn(a, b):
    return lax.dot_general(a, b, (((1,), (0,)), ((), ())), preferred_element_type=F32)


def nt(a, b):
    return lax.dot_general(a, b, (((1,), (1,)), ((), ())), preferred_element_type=F32)


def tn(a, b):
    return lax.dot_general(a, b, (((0,), (0,)), ((), ())), preferred_element_type=F32)


def halves(x):
    high = x.astype(BF)
    return high, (x - high.astype(F32)).astype(BF)


def params(steps=1):
    return pltpu.CompilerParams(
        vmem_limit_bytes=VMEM_BYTES, dimension_semantics=("arbitrary",) * steps
    )


def cost(flops, size, exps=0):
    return pl.CostEstimate(flops=int(flops), bytes_accessed=int(size), transcendentals=int(exps))


awaited, done = [], []


def await_all(*values):
    awaited.extend(values)


def launch(kernel, grid_spec=None, grid=None, in_specs=None, out_specs=None, out_shape=None, **others):
    spec = grid_spec or dict(num_scalar_prefetch=0, grid=grid, in_specs=in_specs, out_specs=out_specs)
    waits = tuple(awaited)
    awaited.clear()
    given = spec["num_scalar_prefetch"] + len(spec["in_specs"])
    single = not isinstance(out_shape, (list, tuple))
    outs = [spec["out_specs"]] if single else list(spec["out_specs"])
    shapes = [out_shape] if single else list(out_shape)

    def body(*refs):
        mark = refs[given + len(waits)]
        mark[...] = jnp.zeros_like(mark)
        kernel(*refs[:given], *refs[given + len(waits) + 1 :])

    zeros = lambda *_: (0, 0)
    spec = dict(
        spec,
        in_specs=list(spec["in_specs"]) + [pl.BlockSpec(memory_space=pl.ANY)] * len(waits),
        out_specs=[pl.BlockSpec((8, PAIR), zeros)] + outs,
    )
    shapes = [jax.ShapeDtypeStruct((8, PAIR), F32)] + shapes
    call = pl.pallas_call(
        body, grid_spec=pltpu.PrefetchScalarGridSpec(**spec), out_shape=shapes, **others
    )

    def run(*args):
        mark, *result = call(*args, *waits)
        done[:] = [mark]
        return result[0] if single else result

    return run


def head_ones(dtype=BF):
    row = lax.broadcasted_iota(jnp.int32, (PAIR, PAIR), 0) // HEAD
    column = lax.broadcasted_iota(jnp.int32, (PAIR, PAIR), 1) // HEAD
    return (row == column).astype(F32).astype(dtype)


def head_sums(x):
    ones = head_ones()
    parts = []
    for at in range(0, x.shape[1], PAIR):
        high, low = halves(x[:, at : at + PAIR])
        parts.append(nn(high, ones) + nn(low, ones))
    return parts[0] if len(parts) == 1 else jnp.concatenate(parts, axis=1)


def centre(x):
    mean = jnp.mean(x, axis=-1, keepdims=True)
    centred = x - mean
    rstd = lax.rsqrt(jnp.mean(centred * centred, axis=-1, keepdims=True) + NORM_EPS)
    return centred * rstd, rstd


def modulation_kernel(device, *refs, order, slots, rows, own, width):
    *tables, ada, class_vec, lifted, labels, modulation = refs
    me = device[0]
    held = tables[0].shape[0]
    count = rows * (held // own)
    total = count * len(tables)
    iota = lambda shape, axis: lax.broadcasted_iota(jnp.int32, shape, axis)

    def place_of(owner):
        return relative_place(owner, me, order) if len(tables) == 2 else owner

    for index, table in enumerate(tables):
        at = (iota((count, held), 0) // rows) * own
        row = iota((count, held), 1)
        edge = table[:, width:]
        pick = lambda x: nn(jnp.where(row == x, 1.0, 0.0).astype(BF), edge)
        both = 256.0 * pick(at) + pick(at + 1)
        slot = iota(both.shape, 0) % rows
        mine = (iota(both.shape, 1) == slot) & (slot < slots)
        label = jnp.sum(jnp.where(mine, both, 0.0), axis=1, keepdims=True).astype(jnp.int32)
        place = place_of(label // own) * own + label % own
        place = jnp.where((iota(place.shape, 0) % rows) < slots, place, -1)
        vec = jnp.zeros((count, width), F32)
        for other, source in enumerate(tables):
            vec += nn(jnp.where(place - other * held == row, 1.0, 0.0).astype(BF), source[:, :width])
        here = slice(index * count, (index + 1) * count)
        class_vec[here, :] = vec.astype(BF)
        label = jnp.where((iota(label.shape, 0) % rows) < slots, label, -1)
        labels[here, :] = jnp.broadcast_to(label, (count, PAIR))
        lifted[here, :] = (vec / (1.0 + jnp.exp(-vec))).astype(BF)
    slot = iota((total, total), 0)
    wanted = place_of(slot // rows) * rows + slot % rows
    swap = jnp.where(wanted == iota((total, total), 1), 1.0, 0.0).astype(BF)
    modulation[...] = nn(nn(swap, lifted[...]).astype(BF), ada[...])


def modulation_call(device, tables, ada, order, slots, rows, own):
    width = ada.shape[0]
    total = rows * (tables[0].shape[0] // own) * len(tables)
    whole = lambda shape: pl.BlockSpec(shape, lambda s, d: (0, 0))
    shapes = [(total, width), (total, width), (total, PAIR), (total, ada.shape[1])]
    return launch(
        functools.partial(
            modulation_kernel, order=order, slots=slots, rows=rows, own=own, width=width
        ),
        grid_spec=dict(
            num_scalar_prefetch=1,
            grid=(1,),
            in_specs=[whole(t.shape) for t in tables] + [whole(ada.shape)],
            out_specs=[whole(s) for s in shapes],
        ),
        out_shape=[jax.ShapeDtypeStruct(s, d) for s, d in zip(shapes, (BF, BF, jnp.int32, F32))],
        compiler_params=params(),
        cost_estimate=cost(6 * total * width * width, 8 * width * width),
        name="modulation",
    )(device, *tables, ada)


def ada_kernel(flags, *refs, devices, order):
    early, *lates, lifted, class_vec, labels, ada, scale, ada_grad, outgoing = refs
    own, width = outgoing.shape[1] - scale.shape[0], lifted.shape[1]
    share = width // devices
    size = max(share, PAIR)
    row = lax.broadcasted_iota(jnp.int32, (width, size), 0)
    lane = lax.broadcasted_iota(jnp.int32, (width, size), 1)
    pick = jnp.where((row == flags[0] * share + lane) & (lane < share), 1.0, 0.0).astype(BF)
    own_lifted = nn(lifted[...], pick).astype(BF)
    own_vec = nn(class_vec[...], pick)[:, :share]
    slots = early.shape[0]
    slot = lax.broadcasted_iota(jnp.int32, (slots, slots), 1)
    rows = slots // devices
    place = relative_place(slot // rows, flags[0], order) * rows + slot % rows
    place_of = lax.broadcasted_iota(jnp.int32, (slots, slots), 0)
    early_grad = nn(jnp.where(place == place_of, 1.0, 0.0).astype(BF), early[...]).astype(BF)
    late_grad = jnp.concatenate([late[...] for late in lates], axis=0)
    cut = lambda x, i: x[:, i * width : (i + 1) * width]
    grad = jnp.concatenate(
        [cut(early_grad, 0), cut(early_grad, 1), cut(late_grad, 0)]
        + [cut(early_grad, 2), cut(late_grad, 1), cut(early_grad, 3)],
        axis=1,
    )
    total = tn(own_lifted, grad)
    ada_grad[...] = total[:share]
    gate = 1.0 / (1.0 + jnp.exp(-own_vec))
    grad = nt(grad, ada[...]) * (gate * (1.0 + own_vec * (1.0 - gate)))
    classes = devices * own
    column = lax.broadcasted_iota(jnp.int32, (slots, classes), 1)
    hot = jnp.where(labels[:, 0:1] == column, 1.0, 0.0).astype(BF)
    high, low = halves(grad)
    least = (grad - high.astype(F32) - low.astype(F32)).astype(BF)
    table = tn(hot, high) + tn(hot, low) + tn(hot, least)
    for device in range(devices):
        outgoing[device, :own, :] = table[device * own : (device + 1) * own]
        outgoing[device, own:, :] = scale[...]


def ada_call(flags, early, lates, lifted, class_vec, labels, ada, scale, devices, order):
    own, width = ada.shape[0], lifted.shape[1]
    whole = lambda x: pl.BlockSpec(x.shape, lambda s, f: (0,) * len(x.shape))
    shapes = [
        jax.ShapeDtypeStruct(ada.shape, F32),
        jax.ShapeDtypeStruct((devices, own + scale.shape[0], width // devices), F32),
    ]
    args = (early, *lates, lifted, class_vec, labels, ada, scale)
    return launch(
        functools.partial(ada_kernel, devices=devices, order=order),
        grid_spec=dict(
            num_scalar_prefetch=1,
            grid=(1,),
            in_specs=[whole(x) for x in args],
            out_specs=[whole(x) for x in shapes],
        ),
        out_shape=shapes,
        compiler_params=params(),
        cost_estimate=cost(10**9, 10**7),
        name="adaptive_norm_backward",
    )(flags, *args)


def qkv_kernel(places, tokens, member, modulation, *refs, pieces, parts):
    weights, (scale, hidden, q, k, v, rq, rk, ordered) = refs[: pieces * parts], refs[pieces * parts :]
    step = pl.program_id(0)
    width = tokens.shape[1]
    block = ordered.shape[1]
    per = width // block
    share = 4 * per // parts
    rows = 256

    @pl.when(step == 0)
    def _():
        for at in range(0, tokens.shape[0], rows):
            here = pl.ds(at, rows)
            unit, _ = centre(tokens[here, :].astype(F32))
            sc = nn(member[here, :], modulation[:, 2 * width : 3 * width])
            sh = nn(member[here, :], modulation[:, 4 * width : 5 * width])
            hidden[here, :] = (unit * (1.0 + sc) + sh).astype(BF)

    for part in range(parts):

        @pl.when((step >= part * share) & (step < (part + 1) * share))
        def _():
            if pieces == 1:
                ordered[...] = weights[part][...]
                return
            own, other = weights[2 * part : 2 * part + 2]
            owners = places.shape[1]
            size = width // owners
            for owner in range(owners):
                place = places[part, owner]
                second = place >= owners // 2
                at = pl.multiple_of((place - jnp.where(second, owners // 2, 0)) * size, size)
                put = slice(owner * size, (owner + 1) * size)

                @pl.when(jnp.logical_not(second))
                def _():
                    ordered[put, :] = own[pl.ds(at, size), :]

                @pl.when(second)
                def _():
                    ordered[put, :] = other[pl.ds(at, size), :]

    for which in range(3):

        @pl.when((step >= which * per) & (step < (which + 1) * per))
        def _():
            for at in range(0, tokens.shape[0], rows):
                here = pl.ds(at, rows)
                out = nn(hidden[here, :], ordered[...])
                if which < 2:
                    r = lax.rsqrt(head_sums(out * out) + NORM_EPS)
                    (rq, rk)[which][here, :] = r.astype(BF)
                    out = out * r
                if which == 0:
                    out = out * scale[0:1, :]
                (q, k, v)[which][here, :] = out.astype(BF)


def qkv_call(places, tokens, member, modulation, weights, scale_lanes, block=512):
    count, width = tokens.shape
    per = width // block
    pieces, parts = len(weights[0]), len(weights)
    share = 4 * per // parts
    column = lambda rows, first, number: pl.BlockSpec(
        (rows, block), lambda s, p: (0, jnp.clip(s - first, 0, number - 1))
    )
    whole = lambda x: pl.BlockSpec(x.shape, lambda s, p: (0, 0))
    columns = [column(count, i * per, per) for i in range(3)]
    return launch(
        functools.partial(qkv_kernel, pieces=pieces, parts=parts),
        grid_spec=dict(
            num_scalar_prefetch=1,
            grid=(4 * per,),
            in_specs=[whole(tokens), whole(member), whole(modulation)]
            + [column(w.shape[0], i * share, share) for i in range(parts) for w in weights[i]]
            + [column(8, 0, per)],
            out_specs=[pl.BlockSpec((count, width), lambda s, p: (0, 0))]
            + columns
            + columns[:2]
            + [pl.BlockSpec((width, block), lambda s, p: (0, s))],
        ),
        out_shape=[jax.ShapeDtypeStruct((count, width), BF)] * 6
        + [jax.ShapeDtypeStruct((width, 4 * width), BF)],
        compiler_params=params(),
        cost_estimate=cost(6 * count * width * width, 2 * (13 * count * width)),
        name="qkv_forward",
    )(places, tokens, member, modulation, *[w for ws in weights for w in ws], scale_lanes)


def lane_masked(x, which):
    lane = lax.broadcasted_iota(jnp.int32, x.shape, 1) // HEAD
    return jnp.where(lane == which, x, jnp.zeros_like(x))


def attn_fwd_kernel(span, q, k, v, start, end, mixed, rest, inverse, v_ext, qm, *, qb, kb):
    count = q.shape[0]
    pairs = q.shape[1] // PAIR
    for pair in range(pairs):
        lanes = slice(pair * PAIR, (pair + 1) * PAIR)
        for h in range(2):
            vv = v[:, lanes]
            lane = lax.broadcasted_iota(jnp.int32, vv.shape, 1) // HEAD
            v_ext[2 * pair + h] = jnp.where(lane == h, vv, jnp.ones_like(vv))
            qm[2 * pair + h] = lane_masked(q[:, lanes], h)

    def one_block(i, _):
        first = pl.multiple_of(i * qb, qb)
        here = pl.ds(first, qb)
        low, high = start[here, :], end[here, :]

        def step(j, totals):
            at = pl.multiple_of(j * kb, kb)
            there = pl.ds(at, kb)
            place = at + lax.broadcasted_iota(jnp.int32, (qb, kb), 1)
            seen = jnp.where((place >= low) & (place < high), 1.0, 0.0).astype(BF)
            lanes = [slice(h // 2 * PAIR, (h // 2 + 1) * PAIR) for h in range(2 * pairs)]
            scores = [nt(qm[h, here, :], k[there, lanes[h]]) for h in range(2 * pairs)]
            probs = [jnp.exp(s).astype(BF) * seen for s in scores]
            return tuple(
                total + nn(p, v_ext[h, there, :]) for h, (total, p) in enumerate(zip(totals, probs))
            )

        totals = lax.fori_loop(
            span[0, i], span[1, i], step, tuple(jnp.zeros((qb, PAIR), F32) for _ in range(2 * pairs))
        )
        for pair in range(pairs):
            t0, t1 = totals[2 * pair], totals[2 * pair + 1]
            lane = lax.broadcasted_iota(jnp.int32, t0.shape, 1) // HEAD
            top = jnp.where(lane == 0, t0, t1)
            sums = pltpu.roll(jnp.where(lane == 0, t1, t0), HEAD, 1)
            inv = 1.0 / sums
            high_part, low_part = halves(top * inv)
            mixed[here, pair * PAIR : (pair + 1) * PAIR] = high_part
            rest[here, pair * PAIR : (pair + 1) * PAIR] = low_part
            turned = jnp.transpose(inv)
            inverse[0, 2 * pair : 2 * pair + 1, here] = turned[0:1, :]
            inverse[0, 2 * pair + 1 : 2 * pair + 2, here] = turned[HEAD : HEAD + 1, :]
        return 0

    lax.fori_loop(0, count // qb, one_block, 0)


def attn_fwd_call(span, q, k, v, start, end, qb=256, kb=256):
    count, width = q.shape
    lanes = GROUP * HEAD
    column = pl.BlockSpec((count, lanes), lambda g, s: (0, g))
    edge = pl.BlockSpec((count, 1), lambda g, s: (0, 0))
    heads = width // HEAD
    return launch(
        functools.partial(attn_fwd_kernel, qb=qb, kb=kb),
        grid_spec=dict(
            num_scalar_prefetch=1,
            grid=(heads // GROUP,),
            in_specs=[column, column, column, edge, edge],
            out_specs=[column, column, pl.BlockSpec((1, 8, count), lambda g, s: (g, 0, 0))],
            scratch_shapes=[
                pltpu.VMEM((GROUP, count, PAIR), BF),
                pltpu.VMEM((GROUP, count, PAIR), BF),
            ],
        ),
        out_shape=[
            jax.ShapeDtypeStruct((count, width), BF),
            jax.ShapeDtypeStruct((count, width), BF),
            jax.ShapeDtypeStruct((heads // GROUP, 8, count), F32),
        ],
        compiler_params=params(),
        cost_estimate=cost(16 * count * count * heads * HEAD, 8 * count * width, heads * count * count),
        name="attention_forward",
    )(span, q, k, v, start, end)


def attn_bwd_kernel(
    span, q, k, v, do, start, end, inverse, delta, rq, rk, scale,
    dq, dk, dv, scale_grad, qm, dom, kt, dq_acc, dk_acc, dv_acc, *, qb, kb,
):
    count = q.shape[0]
    pairs = q.shape[1] // PAIR
    for pair in range(pairs):
        lanes = slice(pair * PAIR, (pair + 1) * PAIR)
        for at in range(0, count, qb):
            for h in range(2):
                put = slice(2 * at + h * qb, 2 * at + (h + 1) * qb)
                qm[pair, put, :] = lane_masked(q[at : at + qb, lanes], h)
                dom[pair, put, :] = lane_masked(do[at : at + qb, lanes], h)
    kt[...] = jnp.transpose(k[...])
    dk_acc[...] = jnp.zeros_like(dk_acc)
    dv_acc[...] = jnp.zeros_like(dv_acc)

    def one_block(i, total):
        here = pl.ds(pl.multiple_of(i * qb, qb), qb)
        twice = pl.ds(pl.multiple_of(i * (2 * qb), 2 * qb), 2 * qb)
        one = [pl.ds(pl.multiple_of(i * (2 * qb) + h * qb, qb), qb) for h in range(2)]
        low, high = start[0:1, here], end[0:1, here]
        dq_acc[...] = jnp.zeros_like(dq_acc)

        def step(j, _):
            at = pl.multiple_of(j * kb, kb)
            there = pl.ds(at, kb)
            place = at + lax.broadcasted_iota(jnp.int32, (kb, qb), 0)
            seen = jnp.where((place >= low) & (place < high), 1.0, 0.0).astype(BF)
            for pair in range(pairs):
                lanes = slice(pair * PAIR, (pair + 1) * PAIR)
                heads = (2 * pair, 2 * pair + 1)
                s = [nt(k[there, lanes], qm[pair, x, :]) for x in one]
                dp = [nt(v[there, lanes], dom[pair, x, :]) for x in one]
                p = [jnp.exp(x) * inverse[0, h : h + 1, here] for x, h in zip(s, heads)]
                ds = [x * (y - delta[0, h : h + 1, here]) for x, y, h in zip(p, dp, heads)]
                p = [x.astype(BF) * seen for x in p]
                ds = [x.astype(BF) * seen for x in ds]
                dv_acc[there, lanes] += nn(jnp.concatenate(p, axis=1), dom[pair, twice, :])
                dk_acc[there, lanes] += nn(jnp.concatenate(ds, axis=1), qm[pair, twice, :])
                for x, h in zip(ds, heads):
                    rows = slice(h * HEAD, (h + 1) * HEAD)
                    dq_acc[rows, :] += nn(kt[rows, there], x)
            return 0

        lax.fori_loop(span[0, i], span[1, i], step, 0)
        g = jnp.transpose(dq_acc[...])
        sc = scale[0:1, :]
        unit = q[here, :].astype(F32) / sc
        inner = head_sums(unit * g)
        dq[here, :] = (sc * rq[here, :].astype(F32) * (g - unit * inner)).astype(BF)
        return total + jnp.sum(inner, axis=0, keepdims=True)

    total = lax.fori_loop(0, count // qb, one_block, jnp.zeros((1, q.shape[1]), F32))
    scale_grad[...] = jnp.broadcast_to(total, scale_grad.shape)
    for at in range(0, count, qb):
        here = pl.ds(at, qb)
        g = dk_acc[here, :]
        unit = k[here, :].astype(F32)
        dk[here, :] = (rk[here, :].astype(F32) * (g - unit * head_sums(unit * g))).astype(BF)
    dv[...] = dv_acc[...].astype(BF)


def attn_bwd_call(
    span, q, k, v, do, start, end, inverse, delta, rq, rk, scale_lanes, first, groups, qb=256, kb=256
):
    count, width = q.shape
    lanes = GROUP * HEAD
    column = pl.BlockSpec((count, lanes), lambda g, s: (0, first + g))
    edge = pl.BlockSpec((1, count), lambda g, s: (0, 0))
    row = pl.BlockSpec((1, 8, count), lambda g, s: (first + g, 0, 0))
    out = pl.BlockSpec((count, lanes), lambda g, s: (0, g))
    heads = groups * GROUP
    return launch(
        functools.partial(attn_bwd_kernel, qb=qb, kb=kb),
        grid_spec=dict(
            num_scalar_prefetch=1,
            grid=(groups,),
            in_specs=[column] * 4
            + [edge] * 2
            + [row] * 2
            + [column] * 2
            + [pl.BlockSpec((8, lanes), lambda g, s: (0, first + g))],
            out_specs=[out] * 3 + [pl.BlockSpec((8, lanes), lambda g, s: (0, g))],
            scratch_shapes=[pltpu.VMEM((GROUP // 2, 2 * count, PAIR), BF)] * 2
            + [pltpu.VMEM((lanes, count), BF), pltpu.VMEM((lanes, qb), F32)]
            + [pltpu.VMEM((count, lanes), F32)] * 2,
        ),
        out_shape=[jax.ShapeDtypeStruct((count, groups * lanes), BF)] * 3
        + [jax.ShapeDtypeStruct((8, groups * lanes), F32)],
        compiler_params=params(),
        cost_estimate=cost(40 * count * count * heads * HEAD, 18 * count * heads * HEAD, heads * count * count),
        name="attention_backward",
    )(span, q, k, v, do, start, end, inverse, delta, rq, rk, scale_lanes)


def proj_kernel(tokens, mixed, cotangent, member, modulation, weight, after, branch, hidden, down):
    width = tokens.shape[1]
    part = lambda i: nn(member[...], modulation[:, i * width : (i + 1) * width])
    out = nn(mixed[...], weight[...])
    total = tokens[...].astype(F32) + part(0) * out
    after[...] = total
    branch[...] = out.astype(BF)
    unit, _ = centre(total)
    hidden[...] = (unit * (1.0 + part(3)) + part(5)).astype(BF)
    down[...] = (cotangent[...].astype(F32) * part(1)).astype(BF)


def proj_call(tokens, mixed, cotangent, member, modulation, weight, rows=256):
    count, width = tokens.shape
    some = pl.BlockSpec((rows, width), lambda s: (s, 0))
    whole = lambda x: pl.BlockSpec(x.shape, lambda s: (0, 0))
    return launch(
        proj_kernel,
        grid=(count // rows,),
        in_specs=[
            some,
            some,
            some,
            pl.BlockSpec((rows, member.shape[1]), lambda s: (s, 0)),
            whole(modulation),
            pl.BlockSpec((width, width), lambda s: (0, 3)),
        ],
        out_specs=[some] * 4,
        out_shape=[
            jax.ShapeDtypeStruct((count, width), d) for d in (F32, BF, BF, BF)
        ],
        compiler_params=params(),
        cost_estimate=cost(2 * count * width * width, 16 * count * width),
        name="projection",
    )(tokens, mixed, cotangent, member, modulation, weight)


def split_blocks(odd, result, rows, kept, sent):
    result = result.astype(BF)
    for at in range(0, result.shape[0], 2 * rows):
        even_part = result[at : at + rows]
        odd_part = result[at + rows : at + 2 * rows]
        put = slice(at // 2, at // 2 + rows)
        kept[put, :] = jnp.where(odd, odd_part, even_part)
        sent[put, :] = jnp.where(odd, even_part, odd_part)


def mlp_kernel(core, hidden, down, up_w, down_w, *refs, rows, own):
    split = len(refs) == 9
    mlp, back = refs[:2]
    grads = refs[2:-3]
    active, grad, turned = refs[-3:]
    step = pl.program_id(0)
    odd = core[1] == 1

    @pl.when(step == 0)
    def _():
        mlp[...] = jnp.zeros_like(mlp)
        back[...] = jnp.zeros_like(back)
        turned[...] = jnp.transpose(hidden[...])

    for at in range(0, hidden.shape[0], rows):
        here = pl.ds(at, rows)
        e = nn(hidden[here, :], up_w[...])
        da = nt(down[here, :], down_w[...])
        square = e * e
        t = jnp.tanh(e * (GELU_A + GELU_A * GELU_B * square))
        half = 0.5 + 0.5 * t
        act = (e * half).astype(BF)
        slope = half + e * (0.5 - 0.5 * t * t) * (GELU_A + 3.0 * GELU_A * GELU_B * square)
        de = (da * slope).astype(BF)
        active[here, :] = act
        grad[here, :] = de
        mlp[here, :] += nn(act, down_w[...])
        back[here, :] += nt(de, up_w[...])
    if split:
        split_blocks(odd, tn(active[...], down[...]), own, grads[2], grads[3])
        split_blocks(odd, nn(turned[...], grad[...]), own, grads[0], grads[1])
    else:
        grads[1][...] = tn(active[...], down[...]).astype(BF)
        grads[0][...] = nn(turned[...], grad[...]).astype(BF)


def mlp_call(core, hidden, down, packed, own, split, first, count_of, block=512, rows=256):
    count, width = hidden.shape
    units = packed.shape[1] // 2
    per = width // block
    whole = pl.BlockSpec((count, width), lambda s, c: (0, 0))
    first_up, first_down = first * per, units // width + first
    kept = 2 if split else 1
    copies = 2 if split else 1
    wide = pl.BlockSpec((width // kept, block), lambda s, c: (0, s))
    tall = pl.BlockSpec((block // kept, width), lambda s, c: (s % per, s // per))
    return launch(
        functools.partial(mlp_kernel, rows=rows, own=own),
        grid_spec=dict(
            num_scalar_prefetch=1,
            grid=(count_of * per,),
            in_specs=[
                whole,
                whole,
                pl.BlockSpec((width, block), lambda s, c: (0, first_up + s)),
                pl.BlockSpec((block, width), lambda s, c: (s % per, first_down + s // per)),
            ],
            out_specs=[whole, whole] + [wide] * copies + [tall] * copies,
            scratch_shapes=[
                pltpu.VMEM((count, block), BF),
                pltpu.VMEM((count, block), BF),
                pltpu.VMEM((width, count), BF),
            ],
        ),
        out_shape=[jax.ShapeDtypeStruct((count, width), F32)] * 2
        + [jax.ShapeDtypeStruct((width // kept, count_of * width), BF)] * (2 * copies),
        compiler_params=params(),
        cost_estimate=cost(12 * count * width * width * count_of, 20 * count * width),
        name="feed_forward",
    )(core, hidden, down, packed, packed)


def item_sums(turned, x):
    high, low = halves(x)
    return nn(turned, high) + nn(turned, low)


def norm_back(unit, rstd, w):
    inner = jnp.mean(w * unit, axis=-1, keepdims=True)
    return (w - jnp.mean(w, axis=-1, keepdims=True) - unit * inner) * rstd


def middle_kernel(
    mlp_sum, back, after, cotangent, branch, mixed, rest, member, turned, modulation, weight,
    output, grad_in, branch_grad, mixed_grad, delta, sums,
):
    width = after.shape[1]
    part = lambda i: nn(member[...], modulation[:, i * width : (i + 1) * width])
    upstream = cotangent[...].astype(F32)
    v = after[...]
    mlp = mlp_sum[...]
    output[...] = (v + part(1) * mlp).astype(BF)
    g = back[...]
    unit, rstd = centre(v)
    total = upstream + norm_back(unit, rstd, g * (1.0 + part(3)))
    grad_in[...] = total
    down = (total * part(0)).astype(BF)
    branch_grad[...] = down
    mg = nt(down, weight[...]).astype(BF)
    mixed_grad[...] = mg
    product = mg.astype(F32) * (mixed[...].astype(F32) + rest[...].astype(F32))
    head = lax.broadcasted_iota(jnp.int32, (32, width), 0)
    lane = lax.broadcasted_iota(jnp.int32, (32, width), 1) // HEAD
    wanted = GROUP * (head // 8) + head % 8
    pick = jnp.where((wanted == lane) & (head % 8 < GROUP), 1.0, 0.0).astype(BF)
    high, low = halves(product)
    delta[...] = nt(pick, high) + nt(pick, low)

    @pl.when(pl.program_id(0) == 0)
    def _():
        sums[...] = jnp.zeros_like(sums)

    for i, x in enumerate((total * branch[...].astype(F32), upstream * mlp, g * unit, g)):
        sums[:, i * width : (i + 1) * width] += item_sums(turned[...], x)


def middle_call(mlp, back, after, cotangent, branch, mixed, rest, member, turned, modulation, weight, rows=256):
    count, width = after.shape
    some = pl.BlockSpec((rows, width), lambda s: (s, 0))
    whole = lambda x: pl.BlockSpec(x.shape, lambda s: (0, 0))
    items = turned.shape[0]
    heads = 8 * (width // HEAD // GROUP)
    return launch(
        middle_kernel,
        grid=(count // rows,),
        in_specs=[some] * 7
        + [
            pl.BlockSpec((rows, member.shape[1]), lambda s: (s, 0)),
            pl.BlockSpec((items, rows), lambda s: (0, s)),
            whole(modulation),
            pl.BlockSpec((width, width), lambda s: (0, 3)),
        ],
        out_specs=[some] * 4
        + [
            pl.BlockSpec((heads, rows), lambda s: (0, s)),
            pl.BlockSpec((items, 4 * width), lambda s: (0, 0)),
        ],
        out_shape=[jax.ShapeDtypeStruct((count, width), d) for d in (BF, F32, BF, BF)]
        + [
            jax.ShapeDtypeStruct((heads, count), F32),
            jax.ShapeDtypeStruct((items, 4 * width), F32),
        ],
        compiler_params=params(),
        cost_estimate=cost(4 * count * width * width, 30 * count * width),
        name="middle",
    )(mlp, back, after, cotangent, branch, mixed, rest, member, turned, modulation, weight)


def first_kernel(*refs):
    *parts, weight, tokens, grad_in, member, turned, modulation, tokens_grad, sums = refs
    width = tokens.shape[1]
    g, at = 0.0, 0
    for part in parts:
        g = g + nt(part[...], weight[:, at : at + part.shape[1]])
        at += part.shape[1]
    unit, rstd = centre(tokens[...].astype(F32))
    sc = nn(member[...], modulation[:, 2 * width : 3 * width])
    tokens_grad[...] = (grad_in[...] + norm_back(unit, rstd, g * (1.0 + sc))).astype(BF)

    @pl.when(pl.program_id(0) == 0)
    def _():
        sums[...] = jnp.zeros_like(sums)

    for i, x in enumerate((g * unit, g)):
        sums[:, i * width : (i + 1) * width] += item_sums(turned[...], x)


def first_call(parts, weight, tokens, grad_in, member, turned, modulation, rows=256):
    count, width = tokens.shape
    some = pl.BlockSpec((rows, width), lambda s: (s, 0))
    whole = lambda x: pl.BlockSpec(x.shape, lambda s: (0, 0))
    items = turned.shape[0]
    return launch(
        first_kernel,
        grid=(count // rows,),
        in_specs=[pl.BlockSpec((rows, p.shape[1]), lambda s: (s, 0)) for p in parts]
        + [
            pl.BlockSpec((width, 3 * width), lambda s: (0, 0)),
            some,
            some,
            pl.BlockSpec((rows, member.shape[1]), lambda s: (s, 0)),
            pl.BlockSpec((items, rows), lambda s: (0, s)),
            whole(modulation),
        ],
        out_specs=[some, pl.BlockSpec((items, 2 * width), lambda s: (0, 0))],
        out_shape=[
            jax.ShapeDtypeStruct((count, width), BF),
            jax.ShapeDtypeStruct((items, 2 * width), F32),
        ],
        compiler_params=params(),
        cost_estimate=cost(6 * count * width * width, 18 * count * width),
        name="first_norm_backward",
    )(*parts, weight, tokens, grad_in, member, turned, modulation)


def weight_grad_kernel(core, *refs, rows, starts):
    jobs = len(starts) - 1
    xs, ys = refs[:jobs], refs[jobs : jobs + starts[-1][1]]
    outs, turned = refs[jobs + starts[-1][1] : -1], refs[-1]
    step = pl.program_id(0)
    for job in range(jobs):

        @pl.when(step == starts[job][0])
        def _():
            turned[...] = jnp.transpose(xs[job][...])

        (begin, first), (end, last) = starts[job], starts[job + 1]
        per = (end - begin) // (last - first)
        for which in range(first, last):
            at = begin + (which - first) * per

            @pl.when((step >= at) & (step < at + per))
            def _():
                result = nn(turned[...], ys[which][...])
                if len(outs) == 2:
                    split_blocks(core[1] == 1, result, rows, outs[0], outs[1])
                else:
                    outs[0][...] = result.astype(BF)


def weight_grad_call(core, jobs, rows, split, block=512):
    count, width = jobs[0][0].shape
    starts, specs = [(0, 0)], []
    for _, ys in jobs:
        begin, number = starts[-1]
        for y in ys:
            per = y.shape[1] // block
            specs.append(
                pl.BlockSpec(
                    (count, block), lambda s, c, at=begin, per=per: (0, jnp.clip(s - at, 0, per - 1))
                )
            )
            begin, number = begin + per, number + 1
        starts.append((begin, number))
    steps = starts[-1][0]
    columns = steps * block
    wide = lambda n: pl.BlockSpec((n, block), lambda s, c: (0, s))
    shapes = [(width // 2, columns)] * 2 if split else [(width, columns)]
    return launch(
        functools.partial(weight_grad_kernel, rows=rows, starts=tuple(starts)),
        grid_spec=dict(
            num_scalar_prefetch=1,
            grid=(steps,),
            in_specs=[pl.BlockSpec((count, width), lambda s, c: (0, 0)) for _ in jobs] + specs,
            out_specs=[wide(shape[0]) for shape in shapes],
            scratch_shapes=[pltpu.VMEM((width, count), BF)],
        ),
        out_shape=[jax.ShapeDtypeStruct(s, BF) for s in shapes],
        compiler_params=params(),
        cost_estimate=cost(2 * count * width * columns, 4 * count * columns),
        name="weight_grad",
    )(core, *[x for x, _ in jobs], *[y for _, ys in jobs for y in ys])


BOTH = ("wide", "narrow")
LENGTH_TABLE = np.array([0, 1, 5, 14, 30, 55, 91, 155, 255, 424, 680], np.int32)
SCALE_BOUNDS = np.array([1, 5, 14, 30, 55, 91, 155, 255, 424], np.int32)


def bit_count(size):
    return size.bit_length() - 1


def flip(values, axis, size, bit):
    return lax.ppermute(values, axis, [(i, i ^ (1 << bit)) for i in range(size)])


def chip_order(wide, turn):
    outer = list(range(bit_count(wide)))
    turning, last = outer[:-1], outer[-1:]
    turn = turn % max(1, len(turning))
    return turning[turn:] + turning[:turn] + last


def halving_kernel(flags, *refs):
    number = len(refs) // 6
    inputs, outs = refs[: 4 * number], refs[4 * number :]
    for i in range(number):
        kept_here, got_here, kept_there, got_there = inputs[4 * i : 4 * i + 4]
        kept, sent = outs[2 * i : 2 * i + 2]
        add = lambda x, y: (x[:, 0].astype(F32) + y[:, 0].astype(F32)).astype(BF)
        sent[...] = add(kept_there, got_there)
        kept[...] = add(kept_here, got_here)


class Chain:
    def __init__(self, kept, got, sizes, turn, columns=None, index=0):
        self.kept, self.got, self.index = kept, got, index
        self.columns, self.wide = columns or kept.shape[1], sizes["wide"]
        self.dims = list(reversed(range(bit_count(self.wide))))
        self.order = chip_order(self.wide, turn)


def finish_kernel(*refs, blocks):
    number = len(refs) // 3
    for index, (kept, got, out) in enumerate(
        zip(refs[:number], refs[number : 2 * number], refs[2 * number :])
    ):
        total = kept[...].astype(F32) + got[...].astype(F32)
        if not blocks:
            out[...] = total
            continue
        own = total.shape[0]
        width = total.shape[1] // blocks
        if index == 0:
            for owner in range(width // own):
                at = [i * width + owner * own for i in range(blocks)]
                out[:, owner * own * blocks : (owner + 1) * own * blocks] = jnp.concatenate(
                    [total[:, x : x + own] for x in at], axis=1
                )
        else:
            for i in range(blocks):
                out[i * own : (i + 1) * own, :] = total[:, i * width : (i + 1) * width]


def finish(chains, blocks=0):
    whole = lambda x: pl.BlockSpec(x.shape, lambda s: (0, 0))
    kept, got = [c.kept for c in chains], [c.got for c in chains]
    shapes = [jax.ShapeDtypeStruct(x.shape, F32) for x in kept]
    if blocks:
        rows, columns = shapes[1].shape
        shapes[1] = jax.ShapeDtypeStruct((rows * blocks, columns // blocks), F32)
    size = sum(x.size for x in kept)
    return launch(
        functools.partial(finish_kernel, blocks=blocks),
        grid=(1,),
        in_specs=[whole(x) for x in (*kept, *got)],
        out_specs=[whole(x) for x in shapes],
        out_shape=shapes,
        compiler_params=params(),
        cost_estimate=cost(size, 8 * size),
        name="last_sum",
    )(*kept, *got)


def halve(flags, chains, steps):
    specs, args, outs, shapes = [], [], [], []
    for chain in chains:
        bit = chain.order.pop(0)
        at = chain.dims.index(bit)
        chain.dims.pop(at)
        chain.bit = bit
        lead, rows = 2**at, chain.kept.shape[0] // 2 ** (at + 1)
        over = min(lead, steps)
        within = steps // over
        block = (lead // over, rows // within, chain.columns)
        which, index = bit, chain.index
        spec = lambda flip: pl.BlockSpec(
            (block[0], 1, block[1], block[2]),
            lambda s, b, within=within, which=which, index=index: (
                s // within,
                b[2 + which] ^ flip,
                s % within,
                index,
            ),
        )
        kept, got = (x.reshape(lead, 2, rows, -1) for x in (chain.kept, chain.got))
        specs += [spec(0), spec(0), spec(1), spec(1)]
        args += [kept, got, kept, got]
        outs += [pl.BlockSpec(block, lambda s, b, within=within: (s // within, s % within, 0))] * 2
        shapes += [jax.ShapeDtypeStruct((lead, rows, chain.columns), BF)] * 2
    size = sum(int(np.prod(x.shape)) for x in shapes)
    result = launch(
        halving_kernel,
        grid_spec=dict(num_scalar_prefetch=1, grid=(steps,), in_specs=specs, out_specs=outs),
        out_shape=shapes,
        compiler_params=params(),
        cost_estimate=cost(size, 6 * size),
        name="halving_sum",
    )(flags, *args)
    for i, chain in enumerate(chains):
        flat = lambda x: x.reshape(-1, chain.columns)
        chain.kept, chain.index = flat(result[2 * i]), 0
        chain.got = flip(flat(result[2 * i + 1]), "wide", chain.wide, chain.bit)
    return result[0]


def land_kernel(*refs):
    number = len(refs) // 3
    for block, got, out in zip(refs[:number], refs[number : 2 * number], refs[2 * number :]):
        half = block.shape[0]
        out[:half] = block[...]
        out[half:] = got[...]


def land(moves):
    blocks, gots = [m.block for m in moves], [m.got for m in moves]
    shapes = [(2 * x.shape[0],) + x.shape[1:] for x in blocks]
    whole = lambda shape: pl.BlockSpec(shape, lambda s: (0, 0, 0))
    joined = launch(
        land_kernel,
        grid=(1,),
        in_specs=[whole(x.shape) for x in (*blocks, *gots)],
        out_specs=[whole(x) for x in shapes],
        out_shape=[jax.ShapeDtypeStruct(x, BF) for x in shapes],
        compiler_params=params(),
        cost_estimate=cost(0, 4 * sum(int(np.prod(x)) for x in shapes)),
        name="land",
    )(*blocks, *gots)
    for move, block in zip(moves, joined):
        move.block = block


class Gather:
    def __init__(self, block, sizes, order):
        self.block, self.sizes, self.order = block, sizes, list(order) + [None]

    def send(self):
        bit = self.order.pop(0)
        axis = "narrow" if bit is None else "wide"
        self.got = flip(self.block, axis, self.sizes[axis], 0 if bit is None else bit)


    def halves(self):
        return [self.block, self.got]


def owner_sum(x, axis):
    return lax.psum_scatter(x, axis, scatter_dimension=0, tiled=True)


def relative_place(owner, me, order):
    apart = owner ^ me
    place = (apart & 1) << len(order)
    for at, bit in enumerate(order):
        place = place | (((apart >> (bit + 1)) & 1) << at)
    return place


def layout(level_row, count):
    lengths = jnp.sum(
        jnp.where(
            level_row[:, None] == jnp.arange(11, dtype=jnp.int32)[None, :],
            jnp.asarray(LENGTH_TABLE)[None, :],
            0,
        ),
        axis=1,
    ).astype(jnp.int32)
    starts = jnp.cumsum(lengths) - lengths
    position = jnp.arange(count, dtype=jnp.int32)[None, :]
    inside = (position >= starts[:, None]) & (position < (starts + lengths)[:, None])
    inside_int = inside.astype(jnp.int32)
    covered = jnp.sum(inside_int, axis=0, keepdims=True) > 0
    first = jnp.where(covered, jnp.sum(inside_int * starts[:, None], axis=0, keepdims=True), position)
    offset = position - first
    length = jnp.full_like(position, int(LENGTH_TABLE[1]))
    for low, high in zip(LENGTH_TABLE[1:-1], LENGTH_TABLE[2:]):
        length = jnp.where(offset >= int(low), int(high), length)
    return inside, first, first + jnp.where(covered, length, 1)


def per_device(
    tokens,
    class_table,
    ada_weight,
    qkv_weight,
    proj_weight,
    head_scale,
    fc1_weight,
    fc2_weight,
    levels,
    labels,
    cotangent,
):
    count, width = tokens.shape
    head_count = head_scale.shape[0]
    sizes = {"wide": lax.axis_size("wide"), "narrow": lax.axis_size("narrow")}
    devices = sizes["wide"] * sizes["narrow"]
    me = lax.axis_index("wide") * sizes["narrow"] + lax.axis_index("narrow")
    chip = lax.axis_index("wide")
    flags = [me, lax.axis_index("narrow") & 1]
    flags += [(chip >> i) & 1 for i in range(bit_count(sizes["wide"]))]
    flags = jnp.stack(flags).astype(jnp.int32)
    slots = labels.shape[1]
    rows = 8
    own = proj_weight.shape[0]
    blocks = fc2_weight.shape[0] // own
    paired = own % 32 == 0 and sizes["narrow"] == 2

    label_block = jnp.zeros((own, PAIR), BF)
    label_block = label_block.at[0, :slots].set((labels[0] // 256).astype(BF))
    label_block = label_block.at[1, :slots].set((labels[0] % 256).astype(BF))
    table_shard = jnp.concatenate([class_table, label_block], axis=1)
    up_shard = fc1_weight.reshape(own, devices, blocks, own).transpose(0, 2, 1, 3)
    feed_shard = jnp.concatenate(
        [up_shard.reshape(own, -1)]
        + [fc2_weight[i * own : (i + 1) * own] for i in range(blocks)],
        axis=1,
    )
    ada_columns = lax.all_to_all(ada_weight, BOTH, 1, 0, tiled=True)
    if paired:
        orders = [chip_order(sizes["wide"], turn)[::-1] for turn in (0, 1)]
        orders.append([orders[0][0]] + orders[0][1:])
        stages = len(orders[0])
        both = Gather(jnp.concatenate([table_shard, qkv_weight, proj_weight], axis=1)[None], sizes, orders[0][:1])
        both.send()
        land([both])
        cuts = (0, width + PAIR, 3 * width + PAIR, 5 * width + PAIR)
        table_move, *moves = (
            Gather(both.block[:, :, low:high], sizes, order[1:])
            for low, high, order in zip(cuts, cuts[1:], orders)
        )
        table_move.send()
        land([table_move])
        for step in range(1, stages):
            for move in (table_move, *moves):
                move.send()
            if step == 1:
                await_all(ada_columns)
            if step < stages - 1:
                land([table_move, *moves])
            if step == stages - 2:
                feed_shard, table_move.block = lax.optimization_barrier((feed_shard, table_move.block))
        tables = [h.reshape(-1, width + PAIR) for h in table_move.halves()]
    else:
        orders = [()]
        tables = [lax.all_gather(table_shard, BOTH, axis=0, tiled=True)]
    class_vec, lifted, slot_labels, modulation_columns = modulation_call(
        flags, tables, ada_columns, orders[0], slots, rows, own
    )
    if paired:
        await_all(done[0])
        land(moves)
        for move in moves:
            move.send()
        weights = [[h.reshape(width // 2, -1) for h in move.halves()] for move in moves]
        owners = jnp.arange(devices, dtype=jnp.int32)
        places = jnp.stack([relative_place(owners, me, o) for o in orders[1:]]).astype(jnp.int32)
    else:
        weights = [
            (lax.all_gather(jnp.concatenate([qkv_weight, proj_weight], axis=1), BOTH, axis=0, tiled=True),)
        ]
        places = jnp.zeros((1, devices), jnp.int32)
    feed_weight = lax.all_gather(feed_shard, BOTH, axis=0, tiled=True)

    modulation = lax.all_to_all(modulation_columns, BOTH, 0, 1, tiled=True)
    high = lax.reduce_precision(modulation, 8, 7)
    middle = lax.reduce_precision(modulation - high, 8, 7)
    low = modulation - high - middle
    terms = jnp.pad(jnp.concatenate([high, middle, low]), ((0, 8), (0, 0))).astype(BF)

    inside, first, last = layout(levels[0], count)
    turned = jnp.pad(inside.astype(BF), ((0, 16 - slots), (0, 0)))
    inside = jnp.pad(inside.astype(BF), ((0, rows - slots), (0, 0)))
    member = jnp.concatenate([inside] * 3 + [jnp.zeros_like(inside)]).T
    tile = 256
    span = jnp.concatenate(
        [first[:, ::tile] // tile, (last[:, tile - 1 :: tile] + tile - 1) // tile]
    ).astype(jnp.int32)
    scale_lanes = jnp.broadcast_to(jnp.repeat(head_scale, width // head_count)[None], (8, width))

    hidden_one, q, k, v, rq, rk, ordered = qkv_call(
        places, tokens, member, terms, weights, scale_lanes
    )
    mixed, rest, inverse = attn_fwd_call(
        span, q, k, v, first.reshape(count, 1), last.reshape(count, 1), tile, tile
    )
    after, branch, hidden_two, down = proj_call(
        tokens, mixed, cotangent, member, terms, ordered
    )
    mlp, back, *grads = mlp_call(flags, hidden_two, down, feed_weight, own, paired, 0, blocks)
    swap = lambda x: flip(x, "narrow", sizes["narrow"], 0)
    if paired:
        up, down = (
            Chain(kept, swap(sent), sizes, turn)
            for turn, kept, sent in ((0, *grads[:2]), (1, *grads[2:]))
        )
    output, grad_in, branch_grad, mixed_grad, delta, sums = middle_call(
        mlp, back, after, cotangent, branch, mixed, rest, member, turned, terms, ordered
    )
    early = jnp.pad(sums[:slots], ((0, rows - slots), (0, 0))).astype(BF)
    early = lax.all_gather(early, BOTH, axis=0, tiled=True)
    if paired:
        await_all(done[0])
        halve(flags, [up, down], 8)
        await_all(done[0])
    else:
        feed = owner_sum(jnp.concatenate(grads, axis=1), BOTH).astype(F32)
        units = blocks * width
        fc1_grad = feed[:, :units].reshape(own, blocks, devices, own).transpose(0, 2, 1, 3)
        fc1_grad = fc1_grad.reshape(own, -1)
        fc2_grad = jnp.concatenate(
            [feed[:, units + i * width : units + (i + 1) * width] for i in range(blocks)]
        )
    *heads, scale_part = attn_bwd_call(
        span, q, k, v, mixed_grad, first, last, inverse, delta.reshape(-1, 8, count), rq, rk,
        scale_lanes, 0, head_count // GROUP, tile, tile,
    )
    if paired:
        await_all(done[0])
        halve(flags, [up, down], 4)
        await_all(done[0])
    qkv_parts = weight_grad_call(flags, [(hidden_one, heads)], own, paired)
    if paired:
        qkv_got = swap(qkv_parts[1])
        await_all(done[0])
    proj_parts = weight_grad_call(flags, [(mixed, [branch_grad])], own, paired)
    if paired:
        qkv = [Chain(qkv_parts[0], qkv_got, sizes, i, 3 * width // 2, i) for i in range(2)]
        proj = Chain(proj_parts[0], swap(proj_parts[1]), sizes, 2)
        await_all(done[0])
        halve(flags, [*qkv, proj], 4)
        await_all(done[0])
    else:
        qkv_grad = owner_sum(qkv_parts[0], BOTH).astype(F32)
        proj_grad = owner_sum(proj_parts[0], BOTH).astype(F32)
    tokens_grad, first_sums = first_call(
        heads, ordered, tokens, grad_in, member, turned, terms
    )
    late = jnp.pad(first_sums[:slots], ((0, rows - slots), (0, 0))).astype(BF)
    own_width = width // devices
    scale_sums = scale_part[0].reshape(head_count, HEAD)[:, 0]
    head_rows = -(-head_count // own_width)
    head_rows += -head_rows % 8
    scale_rows = jnp.pad(scale_sums, (0, head_rows * own_width - head_count)).reshape(
        head_rows, own_width
    )
    if paired:
        move = Gather(late[None], sizes, orders[0])
        move.send()
        await_all(done[0])
        halve(flags, [*qkv, proj, up, down], 2)
        for step in range(stages):
            await_all(done[0])
            land([move])
            move.send()
            if step == 2:
                await_all(done[0])
                halve(flags, [*qkv, proj, up, down], 2)
        lates = [h.reshape(-1, h.shape[-1]) for h in move.halves()]
        await_all(done[0])
        ada_grad, outgoing = ada_call(
            flags, early, lates, lifted, class_vec, slot_labels, ada_weight, scale_rows, devices,
            orders[0],
        )
        await_all(done[0])
        halve(flags, [*qkv, proj], 2)
        await_all(done[0])
        fc1_grad, fc2_grad = finish([up, down], blocks)
        await_all(done[0])
        *parts, proj_grad = finish([*qkv, proj])
        qkv_grad = jnp.concatenate(parts, axis=1)
    else:
        late = lax.all_gather(late, BOTH, axis=0, tiled=True)
        cut = lambda x, i: x[:, i * width : (i + 1) * width]
        item_grad = jnp.concatenate(
            [cut(early, 0), cut(early, 1), cut(late, 0), cut(early, 2), cut(late, 1), cut(early, 3)],
            axis=1,
        )
        ada_grad = tn(lax.dynamic_slice_in_dim(lifted, me * own_width, own_width, 1), item_grad)
        own_vec = lax.dynamic_slice_in_dim(class_vec, me * own_width, own_width, 1).astype(F32)
        _, silu_pull = jax.vjp(jax.nn.silu, own_vec)
        class_grad = silu_pull(nt(item_grad, ada_weight))[0]
        hot = (slot_labels[:, :1] == jnp.arange(devices * own, dtype=jnp.int32)[None, :]).astype(F32)
        table_columns = jnp.einsum("ic,id->cd", hot, class_grad, precision=lax.Precision.HIGHEST)
        outgoing = jnp.concatenate(
            [
                table_columns.reshape(devices, own, own_width),
                jnp.broadcast_to(scale_rows[None], (devices,) + scale_rows.shape),
            ],
            axis=1,
        )
    outgoing = outgoing.reshape(-1, own_width)
    incoming = lax.all_to_all(outgoing, BOTH, 0, 1, tiled=True)
    table_grad = incoming[:own]
    scale_grad = jnp.sum(incoming[own:].reshape(head_rows, devices, own_width), axis=1).reshape(-1)[
        :head_count
    ]
    units = blocks * width
    return (
        output,
        tokens_grad,
        table_grad,
        ada_grad,
        qkv_grad,
        proj_grad,
        scale_grad,
        fc1_grad,
        fc2_grad,
    )


def solution(mesh):
    rows = P(BOTH, None)
    in_specs = (rows,) * 5 + (P(),) + (rows,) * 5
    out_specs = (rows,) * 6 + (P(),) + (rows,) * 2
    return jax.shard_map(
        per_device, mesh=mesh, in_specs=in_specs, out_specs=out_specs, check_vma=False
    )
```
